32 devices in a mesh: rows: 16 (over z, y, x), tm: 2 (over core).
Axes of the slice: x: 2, y: 2, z: 4, core: 2. Of those that a mesh axis runs over, the one named last changes fastest.
Arguments:
- inputs: bfloat16 [16, 2048, 512], P('rows', 'tm'), may hold values from -6 to 6
- cotangent: bfloat16 [16, 2048, 512], P('rows', 'tm'), may hold values from -6 to 6
- segment_ids: int32 [16, 2048], P('rows', 'tm'), may hold values from 0 to 2047, as said below
- qkv_weight: float32 [512, 1536], P('rows', 'tm'), may hold values from -0.25 to 0.25
- out_weight: float32 [512, 512], P('rows', 'tm'), may hold values from -1 to 1
- up_weight: float32 [512, 2048], P('rows', 'tm'), may hold values from -0.25 to 0.25
- down_weight: float32 [2048, 512], P('rows', 'tm'), may hold values from -0.125 to 0.125
- norm_gain_one: float32 [512], P('tm'), may hold values from 0.5 to 1.5
- norm_bias_one: float32 [512], P('tm'), may hold values from -3 to 3
- attn_scale: float32 [512], P('tm'), may hold values from 0.5 to 1.5
- norm_gain_two: float32 [512], P('tm'), may hold values from 0.5 to 1.5
- norm_bias_two: float32 [512], P('tm'), may hold values from -3 to 3
- mlp_scale: float32 [512], P('tm'), may hold values from 0.5 to 1.5
Outputs:
- outputs: bfloat16 [16, 2048, 512], P('rows', 'tm')
- input_grad: bfloat16 [16, 2048, 512], P('rows', 'tm')
- qkv_grad: float32 [512, 1536], P('rows', 'tm')
- out_grad: float32 [512, 512], P('rows', 'tm')
- up_grad: float32 [512, 2048], P('rows', 'tm')
- down_grad: float32 [2048, 512], P('rows', 'tm')
- gain_one_grad: float32 [512], P('tm')
- bias_one_grad: float32 [512], P('tm')
- attn_scale_grad: float32 [512], P('tm')
- gain_two_grad: float32 [512], P('tm')
- bias_two_grad: float32 [512], P('tm')
- mlp_scale_grad: float32 [512], P('tm')
The draws below stay inside these ranges and needn't reach their ends.
Inputs may be any that keep to these rules, and one draw needn't show every extreme that they name: `segment_ids`: in every row each frame holds the index of the last frame of its utterance, so values never fall from one frame to the next, frame 0 is an utterance of its own, and the last utterance ends at the row's last frame; one utterance of each row begins within the row's first 1024 frames and ends within its last 1024.
All inputs are finite; a program needn't handle non-finite values.
Results may differ from the reference program's by a relative error of at most 0.012.
The reference program's roundings to bfloat16 on the way count: a program that leaves them out, or rounds other values in their place, can miss the bound.
Values may be sent and summed in bfloat16 or wider, within the bound.
A program may use at most 192 MiB of HBM per device.

```python
import math
import jax
import jax.numpy as jnp
from jax import lax

D = 512
H = 8
HD = 64
FF = 2048
WINDOW = 250
REACH = 256
QBLOCK = 512
FR_DEV = 1024
ROWS = 16
LENGTH = 2048


def draw_segment_ids(key, part):
    key = jax.random.fold_in(key, 7)

    def one_row(row_key):
        key_begin, key_finish, key_cuts = jax.random.split(row_key, 3)
        begin = jax.random.randint(key_begin, (), 2, FR_DEV // 2 + 1)
        finish = jax.random.randint(key_finish, (), LENGTH - FR_DEV // 2, LENGTH)
        index = jnp.arange(LENGTH, dtype=jnp.int32)
        cuts = jax.random.randint(key_cuts, (LENGTH,), 0, 16) == 0
        outside = (index < begin) | (index > finish)
        marks = outside & (index > 0) & cuts | (index == 1) | (index == begin) | (index == finish)
        ending = jnp.concatenate([marks[1:], jnp.ones((1,), jnp.bool_)])
        candidates = jnp.where(ending, index, jnp.full_like(index, LENGTH))
        return lax.cummin(candidates, axis=0, reverse=True).astype(jnp.int32)
    return jax.vmap(one_row)(jax.random.split(key, ROWS))


def steps_of(own_key, dims, pieces, smallest, top_value):
    def one(axis_at, shards_of):
        steps = jax.random.uniform(jax.random.fold_in(jax.random.fold_in(own_key, 6), axis_at), (shards_of,), jnp.float32, smallest / len(pieces), top_value / len(pieces))
        return jnp.repeat(jnp.exp(steps), dims[axis_at] // shards_of).reshape((-1,) + (1,) * (len(dims) - axis_at - 1))

    factor_of = one(*pieces[0])
    for cut in pieces[1:]:
        factor_of = factor_of * one(*cut)
    return factor_of


def noise(stream_key, extent, spread, limit, pieces=(), held_as=jnp.bfloat16):
    entries = spread * jax.random.normal(stream_key, extent, jnp.float32)
    if pieces:
        entries = entries * steps_of(stream_key, extent, pieces, -0.22, 0.18)
    return jnp.clip(entries, -limit, limit).astype(held_as)


def setup_inputs(seed: int = 0) -> dict:
    splits = jax.random.split(jax.random.key(seed), 14)
    inputs = noise(splits[0], (ROWS, LENGTH, D), 1.0, 6.0, ((0, 16), (1, 2)))
    cotangent = noise(splits[1], (ROWS, LENGTH, D), 1.0, 6.0, ((0, 16), (1, 2)))
    segment_ids = draw_segment_ids(jax.random.fold_in(splits[13], 71), 0)
    qkv_weight = noise(splits[3], (D, 3 * D), D ** -0.5, 0.25, ((0, 16), (1, 2)), jnp.float32)
    out_weight = noise(splits[4], (D, D), (D // 16) ** -0.5, 1.0, ((0, 16), (1, 2)), jnp.float32)
    up_weight = noise(splits[5], (D, FF), D ** -0.5, 0.25, ((0, 16), (1, 2)), jnp.float32)
    down_weight = noise(splits[6], (FF, D), FF ** -0.5, 0.125, ((0, 16), (1, 2)), jnp.float32)
    norm_gain_one = jnp.clip(1.0 + 0.1 * jax.random.normal(splits[7], (D,), jnp.float32), 0.5, 1.5)
    norm_bias_one = noise(splits[8], (D,), 0.5, 3.0, ((0, 2),), jnp.float32)
    attn_scale = jnp.clip(0.5 + 1.0 * jax.random.uniform(splits[9], (D,), jnp.float32) ** steps_of(splits[9], (D,), ((0, 2),), -0.2, 0.2), 0.5, 1.5)
    norm_gain_two = jnp.clip(1.0 + 0.1 * jax.random.normal(splits[10], (D,), jnp.float32), 0.5, 1.5)
    norm_bias_two = noise(splits[11], (D,), 0.5, 3.0, ((0, 2),), jnp.float32)
    mlp_scale = jnp.clip(0.5 + 1.0 * jax.random.uniform(splits[12], (D,), jnp.float32) ** steps_of(splits[12], (D,), ((0, 2),), -0.2, 0.2), 0.5, 1.5)
    return dict(inputs=inputs, cotangent=cotangent, segment_ids=segment_ids, qkv_weight=qkv_weight, out_weight=out_weight, up_weight=up_weight, down_weight=down_weight, norm_gain_one=norm_gain_one, norm_bias_one=norm_bias_one, attn_scale=attn_scale, norm_gain_two=norm_gain_two, norm_bias_two=norm_bias_two, mlp_scale=mlp_scale)


@jax.custom_vjp
def low(v):
    return lax.optimization_barrier(v.astype(jnp.bfloat16)).astype(jnp.float32)

@jax.custom_vjp
def low_back(v):
    return v

def low_keep(v):
    return (low(v), None)

def low_pass(kept, grad):
    return (grad,)

def back_keep(v):
    return (v, None)

def back_low(kept, grad):
    return (low(grad),)
low.defvjp(low_keep, low_pass)
low_back.defvjp(back_keep, back_low)
EPSILON = 1e-05
HIGHEST = lax.Precision.HIGHEST

def layer_norm(values, gain_vec, bias_vec):
    average = lax.optimization_barrier(jnp.mean(values, axis=-1, keepdims=True))
    centred = values - average
    variance = lax.optimization_barrier(jnp.mean(centred * centred, axis=-1, keepdims=True))
    return centred * lax.rsqrt(variance + EPSILON) * gain_vec + bias_vec

def positions_in_utterance(segment):
    length = segment.shape[0]
    index = jnp.arange(length, dtype=jnp.int32)
    change = jnp.concatenate([jnp.ones((1,), jnp.bool_), segment[1:] != segment[:-1]])
    starts = lax.cummax(jnp.where(change, index, jnp.zeros_like(index)), axis=0)
    return index - starts

def rotation_tables(positions):
    half_size = HD // 2
    ladder = jnp.arange(half_size, dtype=jnp.float32)
    frequency = jnp.exp(ladder * (-2.0 * math.log(10000.0) / HD))
    angles = positions.astype(jnp.float32)[:, None] * frequency[None, :]
    return (jnp.cos(angles)[:, None, :], jnp.sin(angles)[:, None, :])

def rotate(field, cosine, sine):
    half_size = field.shape[-1] // 2
    former = field[..., :half_size]
    latter = field[..., half_size:]
    return jnp.concatenate([former * cosine - latter * sine, latter * cosine + former * sine], axis=-1)

def attention(queries, keys, values, segment):
    length = queries.shape[0]
    padded_keys = jnp.concatenate([jnp.zeros((REACH, H, HD), keys.dtype), keys], axis=0)
    padded_values = jnp.concatenate([jnp.zeros((REACH, H, HD), values.dtype), values], axis=0)
    padded_segments = jnp.concatenate([jnp.full((REACH,), -1, jnp.int32), segment.astype(jnp.int32)])
    offsets = jnp.arange(QBLOCK, dtype=jnp.int32)[:, None] - jnp.arange(QBLOCK + REACH, dtype=jnp.int32)[None, :] + REACH
    near = (offsets >= 0) & (offsets < WINDOW)
    factor = 1.0 / math.sqrt(HD)

    def one_block(begin):
        query_block = lax.dynamic_slice_in_dim(queries, begin, QBLOCK, 0)
        key_window = lax.dynamic_slice_in_dim(padded_keys, begin, QBLOCK + REACH, 0)
        value_window = lax.dynamic_slice_in_dim(padded_values, begin, QBLOCK + REACH, 0)
        query_segments = lax.dynamic_slice_in_dim(segment, begin, QBLOCK, 0)
        key_segments = lax.dynamic_slice_in_dim(padded_segments, begin, QBLOCK + REACH, 0)
        allowed = near & (query_segments[:, None] == key_segments[None, :])
        scores = low_back(jnp.einsum('qhd,khd->hqk', query_block, key_window, precision=HIGHEST) * factor)
        scores = jnp.where(allowed[None], scores, -1e+30)
        top = lax.optimization_barrier(jnp.max(scores, axis=-1, keepdims=True))
        weights = jnp.exp(scores - top)
        probs = low(weights / lax.optimization_barrier(jnp.sum(weights, axis=-1, keepdims=True)))
        return jnp.einsum('hqk,khd->qhd', probs, value_window, precision=HIGHEST)
    starts = jnp.arange(length // QBLOCK, dtype=jnp.int32) * QBLOCK
    blocks = lax.map(jax.checkpoint(one_block), starts)
    return blocks.reshape(length, H * HD)

def layer_forward(row_values, weights, segment, positions):
    w_qkv, w_out, w_up, w_down, gain_one, bias_one, scale_one, gain_two, bias_two, scale_two = weights
    length = row_values.shape[0]
    width = H * HD
    normed = low(layer_norm(row_values, low(gain_one), low(bias_one)))
    projected = low_back(jnp.dot(normed, low(w_qkv), precision=HIGHEST))
    cosine, sine = rotation_tables(positions)
    queries = low(rotate(projected[:, :width].reshape(length, H, HD), cosine, sine))
    keys = low(rotate(projected[:, width:2 * width].reshape(length, H, HD), cosine, sine))
    values = low(projected[:, 2 * width:].reshape(length, H, HD))
    mixed = low(low_back(attention(queries, keys, values, segment)))
    branch = low_back(jnp.dot(mixed, low(w_out), precision=HIGHEST))
    after = row_values + low(scale_one) * branch
    normed_two = low(layer_norm(after, low(gain_two), low(bias_two)))
    hidden = low_back(jnp.dot(normed_two, low(w_up), precision=HIGHEST))
    active = low(jax.nn.gelu(hidden, approximate=False))
    branch_two = low_back(jnp.dot(active, low(w_down), precision=HIGHEST))
    return after + low(scale_two) * branch_two

def reference(inputs, cotangent, segment_ids, qkv_weight, out_weight, up_weight, down_weight, norm_gain_one, norm_bias_one, attn_scale, norm_gain_two, norm_bias_two, mlp_scale):
    params = (qkv_weight, out_weight, up_weight, down_weight, norm_gain_one, norm_bias_one, attn_scale, norm_gain_two, norm_bias_two, mlp_scale)
    params = tuple((piece.astype(jnp.float32) for piece in params))

    def per_row(totals, row):
        row_inputs, row_cotangent, row_segment = row
        positions = positions_in_utterance(row_segment)

        def run_layer(row_values, *weights):
            return layer_forward(row_values, weights, row_segment, positions)
        result, pull = jax.vjp(run_layer, row_inputs.astype(jnp.float32), *params)
        grads = pull(row_cotangent.astype(jnp.float32))
        totals = tuple((total + grad for total, grad in zip(totals, grads[1:])))
        return (totals, (result.astype(jnp.bfloat16), grads[0].astype(jnp.bfloat16)))
    start_totals = tuple((jnp.zeros_like(piece) for piece in params))
    totals, (outputs, input_grad) = lax.scan(per_row, start_totals, (inputs, cotangent, segment_ids))
    return (outputs, input_grad, totals[0], totals[1], totals[2], totals[3], totals[4], totals[5], totals[6], totals[7], totals[8], totals[9])
```

```python
import math

import jax
import jax.numpy as jnp
from jax import lax
from jax.experimental import pallas as pl
from jax.experimental.pallas import tpu as pltpu
from jax.sharding import PartitionSpec as P

H = 8
HD = 64
WINDOW = 250
REACH = 256
QBLOCK = 512


EPSILON = 1e-05
NEGATIVE = -1e30


def prefix(part, axis, combine, identity):
    place = lax.axis_index(axis)
    gathered = jax.tree.map(lambda a: lax.all_gather(a, axis), part)
    state = jax.tree.map(lambda a, e: jnp.zeros_like(a) + jnp.asarray(e, a.dtype), part, identity)

    def one(turn, state):
        return combine(
            state, jax.tree.map(lambda a: lax.dynamic_index_in_dim(a, turn, 0, False), gathered)
        )

    return lax.fori_loop(0, place, one, state)


def shifted(block, axis, distance):
    devices = range(lax.axis_size(axis))
    route = [(i - distance, i) for i in devices if i - distance in devices]
    return lax.ppermute(block, axis, route)


def layer_norm(values, gain_vec, bias_vec):
    average = jnp.mean(values, axis=-1, keepdims=True)
    centred = values - average
    variance = jnp.mean(centred * centred, axis=-1, keepdims=True)
    return centred * lax.rsqrt(variance + EPSILON) * gain_vec + bias_vec


def gelu_exact(values):
    return jax.nn.gelu(values, approximate=False)


def rotation_tables(positions):
    half_size = HD // 2
    ladder = jnp.arange(half_size, dtype=jnp.float32)
    frequency = jnp.exp(ladder * (-2.0 * math.log(10000.0) / HD))
    angles = positions.astype(jnp.float32)[:, None] * frequency[None, :]
    return (jnp.cos(angles)[:, None, :], jnp.sin(angles)[:, None, :])


def rotate(field, cosine, sine):
    half_size = field.shape[-1] // 2
    former = field[..., :half_size]
    latter = field[..., half_size:]
    return jnp.concatenate(
        [former * cosine - latter * sine, latter * cosine + former * sine], axis=-1
    )


def outer_sum(left, right):
    return lax.dot_general(
        left, right, (((0,), (0,)), ((), ())), preferred_element_type=jnp.float32
    )


def block_allowed(begin, segment, extended_segments, valid_keys):
    offsets = (
        jnp.arange(QBLOCK, dtype=jnp.int32)[:, None]
        - jnp.arange(QBLOCK + REACH, dtype=jnp.int32)[None, :]
        + REACH
    )
    near = (offsets >= 0) & (offsets < WINDOW)
    query_segments = segment[begin : begin + QBLOCK]
    key_segments = extended_segments[begin : begin + QBLOCK + REACH]
    key_valid = valid_keys[begin : begin + QBLOCK + REACH]
    return near & (query_segments[:, None] == key_segments[None, :]) & key_valid[None, :]


def block_scores(query_block, key_window, allowed):
    raw = jnp.einsum(
        "qhd,khd->hqk", query_block, key_window, preferred_element_type=jnp.float32
    ) * (1.0 / math.sqrt(HD))
    return jnp.where(allowed[None], raw, NEGATIVE)


MESH_IDS = pl.DeviceIdType.MESH


def coordinates():
    row, core = lax.axis_index("rows"), lax.axis_index("tm")
    return row, core, lax.rem(row, 2), lax.rem(lax.div(row, 2), 2), lax.div(row, 4)


def peers_of(at):
    row, core, x, y, z = at
    found = {
        "x": (row + 1 - 2 * x, core),
        "y": (row + 2 - 4 * y, core),
        "s": (row, 1 - core),
    }
    for k in (1, 2, 3):
        found[k] = (lax.rem(z + k, 4) * 4 + lax.rem(row, 4), core)
    return found


def enter(peers):
    barrier = pltpu.get_barrier_semaphore()
    for peer in peers.values():
        pl.semaphore_signal(barrier, inc=1, device_id=peer, device_id_type=MESH_IDS)
    pl.semaphore_wait(barrier, len(peers))


def gather_copies(full, base, sems, at, peers):
    row, core, x, y, z = at
    half = full.shape[4] // 2
    low, high = pl.ds(0, half), pl.ds(half, half)
    every = slice(None)
    send, recv = sems
    table = [
        ("a1", (core, z, y, x), 1),
        ("a2", (core, z, y, x), 2),
        ("a3", (core, z, y, x), 3),
        ("b1", (core, every, y, x, low), "x"),
        ("b2", (core, every, y, x, high), "y"),
        ("c1", (core, every, y, every, low), "y"),
        ("c2", (core, every, every, x, high), "x"),
        ("da", (core, every, y, x), "s"),
        ("db1", (core, every, y, 1 - x, low), "s"),
        ("db2", (core, every, 1 - y, x, high), "s"),
        ("dc1", (core, every, 1 - y, every, low), "s"),
        ("dc2", (core, every, every, 1 - x, high), "s"),
    ]
    out = {}
    for offset, (name, where, peer) in enumerate(table):
        view = full.at[where]
        out[name] = pltpu.make_async_remote_copy(
            src_ref=view,
            dst_ref=view,
            send_sem=send.at[base + offset],
            recv_sem=recv.at[base + offset],
            device_id=peers[peer],
            device_id_type=MESH_IDS,
        )
    return out


GATHER_STEPS = (
    ((), ("a1", "a2", "a3")),
    (("a1", "a2", "a3"), ("b1", "b2", "da")),
    (("b1", "b2"), ("c1", "c2", "db1", "db2")),
    (("c1", "c2"), ("dc1", "dc2")),
    (("da", "db1", "db2", "dc1", "dc2"), ()),
)


def gather_step(copies, step):
    waits, starts = GATHER_STEPS[step]
    for name in waits:
        copies[name].wait_recv()
    for name in starts:
        copies[name].start()


def drain(copies):
    for copy in copies.values():
        copy.wait_send()


def gather_kernel(*refs):
    shards, fulls, sems = refs[:4], refs[4:8], refs[8:]
    at = coordinates()
    peers = peers_of(at)
    row, core, x, y, z = at
    for shard, full in zip(shards, fulls):
        full[core, z, y, x] = shard[...].astype(jnp.bfloat16)
    enter(peers)
    copies = [gather_copies(full, 12 * i, sems, at, peers) for i, full in enumerate(fulls)]
    for step in range(5):
        for each in copies:
            gather_step(each, step)
    for each in copies:
        drain(each)


def gather_weights(*shards):
    return pl.pallas_call(
        gather_kernel,
        out_shape=[
            jax.ShapeDtypeStruct((2, 4, 2, 2) + s.shape, jnp.bfloat16) for s in shards
        ],
        in_specs=[pl.BlockSpec(memory_space=pltpu.VMEM)] * 4,
        out_specs=[pl.BlockSpec(memory_space=pltpu.VMEM)] * 4,
        scratch_shapes=[pltpu.SemaphoreType.DMA((48,)), pltpu.SemaphoreType.DMA((48,))],
        compiler_params=pltpu.CompilerParams(
            collective_id=0, has_side_effects=True, vmem_limit_bytes=50 * 2**20
        ),
    )(*shards)


SCATTER_SLOTS = 8


def scatter_shapes(rows, columns):
    half = rows // 2
    low = jnp.bfloat16
    return [
        pltpu.VMEM((4, 2, 2, rows, columns), low),
        pltpu.VMEM((4, 2, 2, rows, columns), low),
        pltpu.VMEM((2, 4, 2, half, columns), low),
        pltpu.VMEM((2, 4, 2, half, columns), low),
        pltpu.VMEM((2, 4, half, columns), low),
        pltpu.VMEM((2, 4, half, columns), low),
        pltpu.VMEM((3, rows, columns), low),
        pltpu.VMEM((3, rows, columns), low),
    ]


def scatter_copies(bufs, base, sems, peers):
    s_out, s_in, c_out, c_in, b_out, b_in, a_out, a_in = bufs
    send, recv = sems
    table = [
        ("d", s_out, s_in, "s"),
        ("c1", c_out.at[0], c_in.at[0], "y"),
        ("c2", c_out.at[1], c_in.at[1], "x"),
        ("b1", b_out.at[0], b_in.at[0], "x"),
        ("b2", b_out.at[1], b_in.at[1], "y"),
        ("a1", a_out.at[0], a_in.at[0], 1),
        ("a2", a_out.at[1], a_in.at[1], 2),
        ("a3", a_out.at[2], a_in.at[2], 3),
    ]
    return {
        name: pltpu.make_async_remote_copy(
            src_ref=src,
            dst_ref=dst,
            send_sem=send.at[base + offset],
            recv_sem=recv.at[base + offset],
            device_id=peers[peer],
            device_id_type=MESH_IDS,
        )
        for offset, (name, src, dst, peer) in enumerate(table)
    }


def scatter_step(step, copies, own, bufs, result, at):
    s_out, s_in, c_out, c_in, b_out, b_in, a_out, a_in = bufs
    row, core, x, y, z = at
    half = own.shape[3] // 2
    low, high = pl.ds(0, half), pl.ds(half, half)
    f32, bf16 = jnp.float32, jnp.bfloat16
    if step == 0:
        copies["d"].start()
    if step == 1:
        copies["d"].wait_recv()
        for k in range(4):
            for i in range(2):
                c_out[0, k, i] = (
                    own[k, 1 - y, i, low] + s_in[k, 1 - y, i, low].astype(f32)
                ).astype(bf16)
        copies["c1"].start()
        for k in range(4):
            for i in range(2):
                c_out[1, k, i] = (
                    own[k, i, 1 - x, high] + s_in[k, i, 1 - x, high].astype(f32)
                ).astype(bf16)
        copies["c2"].start()
    if step == 2:
        copies["c1"].wait_recv()
        for k in range(4):
            b_out[0, k] = (
                own[k, y, 1 - x, low]
                + s_in[k, y, 1 - x, low].astype(f32)
                + c_in[0, k, 1 - x].astype(f32)
            ).astype(bf16)
        copies["b1"].start()
        copies["c2"].wait_recv()
        for k in range(4):
            b_out[1, k] = (
                own[k, 1 - y, x, high]
                + s_in[k, 1 - y, x, high].astype(f32)
                + c_in[1, k, 1 - y].astype(f32)
            ).astype(bf16)
        copies["b2"].start()
    def summed(k):
        one = (
            own[k, y, x, low]
            + s_in[k, y, x, low].astype(f32)
            + c_in[0, k, x].astype(f32)
            + b_in[0, k].astype(f32)
        )
        two = (
            own[k, y, x, high]
            + s_in[k, y, x, high].astype(f32)
            + c_in[1, k, y].astype(f32)
            + b_in[1, k].astype(f32)
        )
        return jnp.concatenate([one, two], axis=0)

    if step == 3:
        copies["b1"].wait_recv()
        copies["b2"].wait_recv()
        for k in (1, 2, 3):
            a_out[k - 1] = summed(lax.rem(z + k, 4)).astype(bf16)
            copies["a%d" % k].start()
        result[...] = summed(z)
    if step == 4:
        for k in (1, 2, 3):
            copies["a%d" % k].wait_recv()
        result[...] = result[...] + (
            a_in[0].astype(f32) + a_in[1].astype(f32) + a_in[2].astype(f32)
        )


def scatter_kernel(*refs):
    owns, others, results = refs[:4], refs[4:8], refs[8:12]
    bufs = [refs[12 + 8 * i : 20 + 8 * i] for i in range(4)]
    sems = refs[44:]
    at = coordinates()
    peers = peers_of(at)
    for other, each in zip(others, bufs):
        each[0][...] = other[...]
    enter(peers)
    copies = [scatter_copies(each, 8 * i, sems, peers) for i, each in enumerate(bufs)]
    for step in range(5):
        for i in range(4):
            scatter_step(step, copies[i], owns[i], bufs[i], results[i], at)
    for each in copies:
        drain(each)


def scatter_grads(owns, others):
    shapes = [o.shape[3:] for o in owns]
    return pl.pallas_call(
        scatter_kernel,
        out_shape=[jax.ShapeDtypeStruct(s, jnp.float32) for s in shapes],
        in_specs=[pl.BlockSpec(memory_space=pltpu.VMEM)] * 8,
        out_specs=[pl.BlockSpec(memory_space=pltpu.VMEM)] * 4,
        scratch_shapes=[b for s in shapes for b in scatter_shapes(*s)]
        + [pltpu.SemaphoreType.DMA((32,)), pltpu.SemaphoreType.DMA((32,))],
        compiler_params=pltpu.CompilerParams(
            collective_id=1, has_side_effects=True, vmem_limit_bytes=56 * 2**20
        ),
    )(*owns, *others)


def whole_weight(blocks):
    columns = blocks.shape[-1]
    flat = blocks.reshape(2, -1, columns)
    return jnp.concatenate([flat[0], flat[1]], axis=1)


def split_grad(grad):
    rows, columns = grad.shape
    core = lax.axis_index("tm")
    pieces = grad.reshape(4, 2, 2, rows // 16, 2, columns // 2)
    own = lax.dynamic_index_in_dim(pieces, core, 4, False)
    other = lax.dynamic_index_in_dim(pieces, 1 - core, 4, False).astype(jnp.bfloat16)
    return own, other


def local(
    inputs,
    cotangent,
    segment_ids,
    qkv_weight,
    out_weight,
    up_weight,
    down_weight,
    norm_gain_one,
    norm_bias_one,
    attn_scale,
    norm_gain_two,
    norm_bias_two,
    mlp_scale,
):
    frames = inputs.shape[1]
    width = inputs.shape[2]
    low_type = jnp.bfloat16
    gathered = (
        None, None, None, None,
        lax.all_gather(norm_gain_one.astype(low_type), "tm", axis=0, tiled=True),
        lax.all_gather(norm_bias_one.astype(low_type), "tm", axis=0, tiled=True),
        lax.all_gather(attn_scale.astype(low_type), "tm", axis=0, tiled=True),
        lax.all_gather(norm_gain_two.astype(low_type), "tm", axis=0, tiled=True),
        lax.all_gather(norm_bias_two.astype(low_type), "tm", axis=0, tiled=True),
        lax.all_gather(mlp_scale.astype(low_type), "tm", axis=0, tiled=True),
    )
    w_qkv, w_out, w_up, w_down = [
        whole_weight(w) for w in gather_weights(qkv_weight, out_weight, up_weight, down_weight)
    ]
    gain_one, bias_one, scale_one, gain_two, bias_two, scale_two = [
        piece.astype(jnp.float32) for piece in gathered[4:]
    ]
    segment = segment_ids[0]
    index = jnp.arange(frames, dtype=jnp.int32)
    last_run = jnp.sum((segment == segment[frames - 1]).astype(jnp.int32), keepdims=True)

    def join_runs(earlier, later):
        extends = (later[1] == frames) & (later[0] == earlier[0])
        joined = jnp.where(extends, earlier[1] + later[1], later[1])
        vacant = later[0] < 0
        return (jnp.where(vacant, earlier[0], later[0]), jnp.where(vacant, earlier[1], joined))

    before_id, before_run = prefix(
        (segment[frames - 1 :], last_run),
        "tm",
        join_runs,
        (jnp.full((1,), -1, jnp.int32), jnp.zeros((1,), jnp.int32)),
    )
    change = jnp.concatenate([jnp.ones((1,), jnp.bool_), segment[1:] != segment[:-1]])
    starts = lax.cummax(jnp.where(change, index, jnp.zeros_like(index)), axis=0)
    positions = index - starts + jnp.where(segment == before_id[0], before_run[0], 0)
    cosine, sine = rotation_tables(positions)
    source = inputs[0].astype(jnp.float32)
    normed_one, norm_one_pull = jax.vjp(layer_norm, source, gain_one, bias_one)
    normed_one_low = normed_one.astype(low_type)
    projected = jnp.dot(normed_one_low, w_qkv, preferred_element_type=jnp.float32)
    queries = rotate(projected[:, :width].reshape(frames, H, HD), cosine, sine).astype(low_type)
    keys_flat = (
        rotate(projected[:, width : 2 * width].reshape(frames, H, HD), cosine, sine)
        .reshape(frames, width)
        .astype(low_type)
    )
    values_flat = projected[:, 2 * width :].astype(low_type)
    got_keys, got_values, got_segments = shifted((keys_flat, values_flat, segment), "tm", 1)
    got_keys = got_keys[frames - REACH :]
    got_values = got_values[frames - REACH :]
    got_segments = got_segments[frames - REACH :]
    extended_keys = jnp.concatenate([got_keys, keys_flat], axis=0).reshape(REACH + frames, H, HD)
    extended_values = jnp.concatenate([got_values, values_flat], axis=0).reshape(
        REACH + frames, H, HD
    )
    extended_segments = jnp.concatenate([got_segments, segment])
    valid_keys = (lax.axis_index("tm") > 0) | (jnp.arange(REACH + frames, dtype=jnp.int32) >= REACH)
    block_count = frames // QBLOCK
    mixed_parts = []
    log_sums = []
    for block in range(block_count):
        begin = block * QBLOCK
        allowed = block_allowed(begin, segment, extended_segments, valid_keys)
        scores = block_scores(
            queries[begin : begin + QBLOCK], extended_keys[begin : begin + QBLOCK + REACH], allowed
        )
        top = jnp.max(scores, axis=-1, keepdims=True)
        weights = jnp.exp(scores - top)
        total = jnp.sum(weights, axis=-1, keepdims=True)
        probs = (weights / total).astype(low_type)
        mixed_parts.append(
            jnp.einsum(
                "hqk,khd->qhd",
                probs,
                extended_values[begin : begin + QBLOCK + REACH],
                preferred_element_type=jnp.float32,
            )
        )
        log_sums.append(top + jnp.log(total))
    mixed_low = jnp.concatenate(mixed_parts, axis=0).reshape(frames, width).astype(low_type)
    branch = jnp.dot(mixed_low, w_out, preferred_element_type=jnp.float32)
    after = source + scale_one * branch
    normed_two, norm_two_pull = jax.vjp(layer_norm, after, gain_two, bias_two)
    normed_two_low = normed_two.astype(low_type)
    hidden = jnp.dot(normed_two_low, w_up, preferred_element_type=jnp.float32)
    active, gelu_pull = jax.vjp(gelu_exact, hidden)
    active_low = active.astype(low_type)
    branch_two = jnp.dot(active_low, w_down, preferred_element_type=jnp.float32)
    result = (after + scale_two * branch_two).astype(low_type)
    back_qkv, back_out, back_up, back_down = w_qkv, w_out, w_up, w_down
    upstream = cotangent[0].astype(jnp.float32)
    grad_scale_two = jnp.sum(upstream * branch_two, axis=0)
    grad_branch_two = (upstream * scale_two).astype(low_type)
    grad_down = outer_sum(active_low, grad_branch_two)
    grad_active = lax.dot_general(
        grad_branch_two, back_down, (((1,), (1,)), ((), ())), preferred_element_type=jnp.float32
    )
    grad_hidden = gelu_pull(grad_active)[0].astype(low_type)
    grad_up = outer_sum(normed_two_low, grad_hidden)
    grad_normed_two = lax.dot_general(
        grad_hidden, back_up, (((1,), (1,)), ((), ())), preferred_element_type=jnp.float32
    )
    after_part, grad_gain_two, grad_bias_two = norm_two_pull(grad_normed_two)
    grad_after = upstream + after_part
    grad_scale_one = jnp.sum(grad_after * branch, axis=0)
    grad_branch = (grad_after * scale_one).astype(low_type)
    grad_out = outer_sum(mixed_low, grad_branch)
    grad_mixed = lax.dot_general(
        grad_branch, back_out, (((1,), (1,)), ((), ())), preferred_element_type=jnp.float32
    )
    grad_mixed = grad_mixed.astype(low_type).reshape(frames, H, HD)
    factor = 1.0 / math.sqrt(HD)
    grad_keys_ext = jnp.zeros((REACH + frames, H, HD), jnp.float32)
    grad_values_ext = jnp.zeros((REACH + frames, H, HD), jnp.float32)
    query_grads = []
    for block in range(block_count):
        begin = block * QBLOCK
        allowed = block_allowed(begin, segment, extended_segments, valid_keys)
        query_block = queries[begin : begin + QBLOCK]
        key_window = extended_keys[begin : begin + QBLOCK + REACH]
        value_window = extended_values[begin : begin + QBLOCK + REACH]
        scores = block_scores(query_block, key_window, allowed)
        probs_full = jnp.exp(scores - log_sums[block])
        probs_low = probs_full.astype(low_type)
        grad_out_block = grad_mixed[begin : begin + QBLOCK]
        grad_probs = jnp.einsum(
            "qhd,khd->hqk", grad_out_block, value_window, preferred_element_type=jnp.float32
        )
        grad_values_ext = grad_values_ext.at[begin : begin + QBLOCK + REACH].add(
            jnp.einsum(
                "hqk,qhd->khd", probs_low, grad_out_block, preferred_element_type=jnp.float32
            )
        )
        balance = jnp.sum(grad_probs * probs_full, axis=-1, keepdims=True)
        grad_scores = (probs_full * (grad_probs - balance)).astype(low_type)
        query_grads.append(
            jnp.einsum("hqk,khd->qhd", grad_scores, key_window, preferred_element_type=jnp.float32)
            * factor
        )
        grad_keys_ext = grad_keys_ext.at[begin : begin + QBLOCK + REACH].add(
            jnp.einsum("hqk,qhd->khd", grad_scores, query_block, preferred_element_type=jnp.float32)
            * factor
        )
    grad_keys_flat = grad_keys_ext.reshape(REACH + frames, width)
    grad_values_flat = grad_values_ext.reshape(REACH + frames, width)
    back_keys, back_values = (
        shifted(grad_keys_flat[:REACH].astype(jnp.bfloat16), "tm", -1).astype(jnp.float32),
        shifted(grad_values_flat[:REACH].astype(jnp.bfloat16), "tm", -1).astype(jnp.float32),
    )
    own_keys = grad_keys_flat[REACH:]
    own_values = grad_values_flat[REACH:]
    own_keys = jnp.concatenate(
        [own_keys[: frames - REACH], own_keys[frames - REACH :] + back_keys], axis=0
    )
    own_values = jnp.concatenate(
        [own_values[: frames - REACH], own_values[frames - REACH :] + back_values], axis=0
    )
    grad_queries = rotate(jnp.concatenate(query_grads, axis=0), cosine, -sine).reshape(
        frames, width
    )
    grad_keys = rotate(own_keys.reshape(frames, H, HD), cosine, -sine).reshape(frames, width)
    grad_projected = jnp.concatenate([grad_queries, grad_keys, own_values], axis=1).astype(low_type)
    grad_qkv = outer_sum(normed_one_low, grad_projected)
    grad_normed_one = lax.dot_general(
        grad_projected, back_qkv, (((1,), (1,)), ((), ())), preferred_element_type=jnp.float32
    )
    source_part, grad_gain_one, grad_bias_one = norm_one_pull(grad_normed_one)
    input_grad = (grad_after + source_part).astype(low_type)
    reduced = (
        None, None, None, None,
        lax.psum_scatter(grad_gain_one, "tm", scatter_dimension=0, tiled=True),
        lax.psum_scatter(grad_bias_one, "tm", scatter_dimension=0, tiled=True),
        lax.psum_scatter(grad_scale_one, "tm", scatter_dimension=0, tiled=True),
        lax.psum_scatter(grad_gain_two, "tm", scatter_dimension=0, tiled=True),
        lax.psum_scatter(grad_bias_two, "tm", scatter_dimension=0, tiled=True),
        lax.psum_scatter(grad_scale_two, "tm", scatter_dimension=0, tiled=True),
    )
    halves = [split_grad(g) for g in (grad_qkv, grad_out, grad_up, grad_down)]
    qkv_grad, out_grad, up_grad, down_grad = scatter_grads(
        [h[0] for h in halves], [h[1] for h in halves]
    )
    vector_sums = lax.psum(
        (reduced[4], reduced[5], reduced[6], reduced[7], reduced[8], reduced[9]), "rows"
    )
    return (
        result[None],
        input_grad[None],
        qkv_grad,
        out_grad,
        up_grad,
        down_grad,
        vector_sums[0],
        vector_sums[1],
        vector_sums[2],
        vector_sums[3],
        vector_sums[4],
        vector_sums[5],
    )


def local_plain(
    inputs,
    cotangent,
    segment_ids,
    qkv_weight,
    out_weight,
    up_weight,
    down_weight,
    norm_gain_one,
    norm_bias_one,
    attn_scale,
    norm_gain_two,
    norm_bias_two,
    mlp_scale,
):
    frames = inputs.shape[1]
    width = inputs.shape[2]
    low_type = jnp.bfloat16
    gathered = (
        lax.all_gather(qkv_weight.astype(low_type), "tm", axis=1, tiled=True),
        lax.all_gather(out_weight.astype(low_type), "tm", axis=1, tiled=True),
        lax.all_gather(up_weight.astype(low_type), "tm", axis=1, tiled=True),
        lax.all_gather(down_weight.astype(low_type), "tm", axis=1, tiled=True),
        lax.all_gather(norm_gain_one.astype(low_type), "tm", axis=0, tiled=True),
        lax.all_gather(norm_bias_one.astype(low_type), "tm", axis=0, tiled=True),
        lax.all_gather(attn_scale.astype(low_type), "tm", axis=0, tiled=True),
        lax.all_gather(norm_gain_two.astype(low_type), "tm", axis=0, tiled=True),
        lax.all_gather(norm_bias_two.astype(low_type), "tm", axis=0, tiled=True),
        lax.all_gather(mlp_scale.astype(low_type), "tm", axis=0, tiled=True),
    )
    w_qkv, w_out, w_up, w_down = (
        lax.all_gather(gathered[0], "rows", axis=0, tiled=True),
        lax.all_gather(gathered[1], "rows", axis=0, tiled=True),
        lax.all_gather(gathered[2], "rows", axis=0, tiled=True),
        lax.all_gather(gathered[3], "rows", axis=0, tiled=True),
    )
    gain_one, bias_one, scale_one, gain_two, bias_two, scale_two = [
        piece.astype(jnp.float32) for piece in gathered[4:]
    ]
    segment = segment_ids[0]
    index = jnp.arange(frames, dtype=jnp.int32)
    last_run = jnp.sum((segment == segment[frames - 1]).astype(jnp.int32), keepdims=True)

    def join_runs(earlier, later):
        extends = (later[1] == frames) & (later[0] == earlier[0])
        joined = jnp.where(extends, earlier[1] + later[1], later[1])
        vacant = later[0] < 0
        return (jnp.where(vacant, earlier[0], later[0]), jnp.where(vacant, earlier[1], joined))

    before_id, before_run = prefix(
        (segment[frames - 1 :], last_run),
        "tm",
        join_runs,
        (jnp.full((1,), -1, jnp.int32), jnp.zeros((1,), jnp.int32)),
    )
    change = jnp.concatenate([jnp.ones((1,), jnp.bool_), segment[1:] != segment[:-1]])
    starts = lax.cummax(jnp.where(change, index, jnp.zeros_like(index)), axis=0)
    positions = index - starts + jnp.where(segment == before_id[0], before_run[0], 0)
    cosine, sine = rotation_tables(positions)
    source = inputs[0].astype(jnp.float32)
    normed_one, norm_one_pull = jax.vjp(layer_norm, source, gain_one, bias_one)
    normed_one_low = normed_one.astype(low_type)
    projected = jnp.dot(normed_one_low, w_qkv, preferred_element_type=jnp.float32)
    queries = rotate(projected[:, :width].reshape(frames, H, HD), cosine, sine).astype(low_type)
    keys_flat = (
        rotate(projected[:, width : 2 * width].reshape(frames, H, HD), cosine, sine)
        .reshape(frames, width)
        .astype(low_type)
    )
    values_flat = projected[:, 2 * width :].astype(low_type)
    got_keys, got_values, got_segments = shifted((keys_flat, values_flat, segment), "tm", 1)
    got_keys = got_keys[frames - REACH :]
    got_values = got_values[frames - REACH :]
    got_segments = got_segments[frames - REACH :]
    extended_keys = jnp.concatenate([got_keys, keys_flat], axis=0).reshape(REACH + frames, H, HD)
    extended_values = jnp.concatenate([got_values, values_flat], axis=0).reshape(
        REACH + frames, H, HD
    )
    extended_segments = jnp.concatenate([got_segments, segment])
    valid_keys = (lax.axis_index("tm") > 0) | (jnp.arange(REACH + frames, dtype=jnp.int32) >= REACH)
    block_count = frames // QBLOCK
    mixed_parts = []
    log_sums = []
    for block in range(block_count):
        begin = block * QBLOCK
        allowed = block_allowed(begin, segment, extended_segments, valid_keys)
        scores = block_scores(
            queries[begin : begin + QBLOCK], extended_keys[begin : begin + QBLOCK + REACH], allowed
        )
        top = jnp.max(scores, axis=-1, keepdims=True)
        weights = jnp.exp(scores - top)
        total = jnp.sum(weights, axis=-1, keepdims=True)
        probs = (weights / total).astype(low_type)
        mixed_parts.append(
            jnp.einsum(
                "hqk,khd->qhd",
                probs,
                extended_values[begin : begin + QBLOCK + REACH],
                preferred_element_type=jnp.float32,
            )
        )
        log_sums.append(top + jnp.log(total))
    mixed_low = jnp.concatenate(mixed_parts, axis=0).reshape(frames, width).astype(low_type)
    branch = jnp.dot(mixed_low, w_out, preferred_element_type=jnp.float32)
    after = source + scale_one * branch
    normed_two, norm_two_pull = jax.vjp(layer_norm, after, gain_two, bias_two)
    normed_two_low = normed_two.astype(low_type)
    hidden = jnp.dot(normed_two_low, w_up, preferred_element_type=jnp.float32)
    active, gelu_pull = jax.vjp(gelu_exact, hidden)
    active_low = active.astype(low_type)
    branch_two = jnp.dot(active_low, w_down, preferred_element_type=jnp.float32)
    result = (after + scale_two * branch_two).astype(low_type)
    again = (
        lax.all_gather(qkv_weight.astype(low_type), "tm", axis=1, tiled=True),
        lax.all_gather(out_weight.astype(low_type), "tm", axis=1, tiled=True),
        lax.all_gather(up_weight.astype(low_type), "tm", axis=1, tiled=True),
        lax.all_gather(down_weight.astype(low_type), "tm", axis=1, tiled=True),
    )
    back_qkv, back_out, back_up, back_down = (
        lax.all_gather(again[0], "rows", axis=0, tiled=True),
        lax.all_gather(again[1], "rows", axis=0, tiled=True),
        lax.all_gather(again[2], "rows", axis=0, tiled=True),
        lax.all_gather(again[3], "rows", axis=0, tiled=True),
    )
    upstream = cotangent[0].astype(jnp.float32)
    grad_scale_two = jnp.sum(upstream * branch_two, axis=0)
    grad_branch_two = (upstream * scale_two).astype(low_type)
    grad_down = outer_sum(active_low, grad_branch_two)
    grad_active = lax.dot_general(
        grad_branch_two, back_down, (((1,), (1,)), ((), ())), preferred_element_type=jnp.float32
    )
    grad_hidden = gelu_pull(grad_active)[0].astype(low_type)
    grad_up = outer_sum(normed_two_low, grad_hidden)
    grad_normed_two = lax.dot_general(
        grad_hidden, back_up, (((1,), (1,)), ((), ())), preferred_element_type=jnp.float32
    )
    after_part, grad_gain_two, grad_bias_two = norm_two_pull(grad_normed_two)
    grad_after = upstream + after_part
    grad_scale_one = jnp.sum(grad_after * branch, axis=0)
    grad_branch = (grad_after * scale_one).astype(low_type)
    grad_out = outer_sum(mixed_low, grad_branch)
    grad_mixed = lax.dot_general(
        grad_branch, back_out, (((1,), (1,)), ((), ())), preferred_element_type=jnp.float32
    )
    grad_mixed = grad_mixed.astype(low_type).reshape(frames, H, HD)
    factor = 1.0 / math.sqrt(HD)
    grad_keys_ext = jnp.zeros((REACH + frames, H, HD), jnp.float32)
    grad_values_ext = jnp.zeros((REACH + frames, H, HD), jnp.float32)
    query_grads = []
    for block in range(block_count):
        begin = block * QBLOCK
        allowed = block_allowed(begin, segment, extended_segments, valid_keys)
        query_block = queries[begin : begin + QBLOCK]
        key_window = extended_keys[begin : begin + QBLOCK + REACH]
        value_window = extended_values[begin : begin + QBLOCK + REACH]
        scores = block_scores(query_block, key_window, allowed)
        probs_full = jnp.exp(scores - log_sums[block])
        probs_low = probs_full.astype(low_type)
        grad_out_block = grad_mixed[begin : begin + QBLOCK]
        grad_probs = jnp.einsum(
            "qhd,khd->hqk", grad_out_block, value_window, preferred_element_type=jnp.float32
        )
        grad_values_ext = grad_values_ext.at[begin : begin + QBLOCK + REACH].add(
            jnp.einsum(
                "hqk,qhd->khd", probs_low, grad_out_block, preferred_element_type=jnp.float32
            )
        )
        balance = jnp.sum(grad_probs * probs_full, axis=-1, keepdims=True)
        grad_scores = (probs_full * (grad_probs - balance)).astype(low_type)
        query_grads.append(
            jnp.einsum("hqk,khd->qhd", grad_scores, key_window, preferred_element_type=jnp.float32)
            * factor
        )
        grad_keys_ext = grad_keys_ext.at[begin : begin + QBLOCK + REACH].add(
            jnp.einsum("hqk,qhd->khd", grad_scores, query_block, preferred_element_type=jnp.float32)
            * factor
        )
    grad_keys_flat = grad_keys_ext.reshape(REACH + frames, width)
    grad_values_flat = grad_values_ext.reshape(REACH + frames, width)
    back_keys, back_values = (
        shifted(grad_keys_flat[:REACH].astype(jnp.bfloat16), "tm", -1).astype(jnp.float32),
        shifted(grad_values_flat[:REACH].astype(jnp.bfloat16), "tm", -1).astype(jnp.float32),
    )
    own_keys = grad_keys_flat[REACH:]
    own_values = grad_values_flat[REACH:]
    own_keys = jnp.concatenate(
        [own_keys[: frames - REACH], own_keys[frames - REACH :] + back_keys], axis=0
    )
    own_values = jnp.concatenate(
        [own_values[: frames - REACH], own_values[frames - REACH :] + back_values], axis=0
    )
    grad_queries = rotate(jnp.concatenate(query_grads, axis=0), cosine, -sine).reshape(
        frames, width
    )
    grad_keys = rotate(own_keys.reshape(frames, H, HD), cosine, -sine).reshape(frames, width)
    grad_projected = jnp.concatenate([grad_queries, grad_keys, own_values], axis=1).astype(low_type)
    grad_qkv = outer_sum(normed_one_low, grad_projected)
    grad_normed_one = lax.dot_general(
        grad_projected, back_qkv, (((1,), (1,)), ((), ())), preferred_element_type=jnp.float32
    )
    source_part, grad_gain_one, grad_bias_one = norm_one_pull(grad_normed_one)
    input_grad = (grad_after + source_part).astype(low_type)
    reduced = (
        lax.psum_scatter(grad_qkv, "tm", scatter_dimension=1, tiled=True),
        lax.psum_scatter(grad_out, "tm", scatter_dimension=1, tiled=True),
        lax.psum_scatter(grad_up, "tm", scatter_dimension=1, tiled=True),
        lax.psum_scatter(grad_down, "tm", scatter_dimension=1, tiled=True),
        lax.psum_scatter(grad_gain_one, "tm", scatter_dimension=0, tiled=True),
        lax.psum_scatter(grad_bias_one, "tm", scatter_dimension=0, tiled=True),
        lax.psum_scatter(grad_scale_one, "tm", scatter_dimension=0, tiled=True),
        lax.psum_scatter(grad_gain_two, "tm", scatter_dimension=0, tiled=True),
        lax.psum_scatter(grad_bias_two, "tm", scatter_dimension=0, tiled=True),
        lax.psum_scatter(grad_scale_two, "tm", scatter_dimension=0, tiled=True),
    )
    qkv_grad, out_grad, up_grad, down_grad = (
        lax.psum_scatter(reduced[0], "rows", scatter_dimension=0, tiled=True),
        lax.psum_scatter(reduced[1], "rows", scatter_dimension=0, tiled=True),
        lax.psum_scatter(reduced[2], "rows", scatter_dimension=0, tiled=True),
        lax.psum_scatter(reduced[3], "rows", scatter_dimension=0, tiled=True),
    )
    vector_sums = lax.psum(
        (reduced[4], reduced[5], reduced[6], reduced[7], reduced[8], reduced[9]), "rows"
    )
    return (
        result[None],
        input_grad[None],
        qkv_grad,
        out_grad,
        up_grad,
        down_grad,
        vector_sums[0],
        vector_sums[1],
        vector_sums[2],
        vector_sums[3],
        vector_sums[4],
        vector_sums[5],
    )


def solution(mesh):
    placed = (
        P("rows", "tm", None),
        P("rows", "tm", None),
        P("rows", "tm"),
        P("rows", "tm"),
        P("rows", "tm"),
        P("rows", "tm"),
        P("rows", "tm"),
        P("tm"),
        P("tm"),
        P("tm"),
        P("tm"),
        P("tm"),
        P("tm"),
    )
    staged = mesh.shape["rows"] == 16 and mesh.shape["tm"] == 2
    return jax.shard_map(
        local if staged else local_plain,
        mesh=mesh,
        in_specs=placed,
        out_specs=(
            P("rows", "tm", None),
            P("rows", "tm", None),
            P("rows", "tm"),
            P("rows", "tm"),
            P("rows", "tm"),
            P("rows", "tm"),
            P("tm"),
            P("tm"),
            P("tm"),
            P("tm"),
            P("tm"),
            P("tm"),
        ),
        check_vma=False,
    )
```

```python
import functools
import math

import jax
import jax.numpy as jnp
from jax import lax
from jax.experimental import pallas as pl
from jax.experimental.pallas import tpu as pltpu
from jax.sharding import PartitionSpec as P

H = 8
HD = 64
WINDOW = 250
REACH = 256
QBLOCK = 512


EPSILON = 1e-05
NEGATIVE = -1e30


def prefix(part, axis, combine, identity):
    place = lax.axis_index(axis)
    gathered = jax.tree.map(lambda a: lax.all_gather(a, axis), part)
    state = jax.tree.map(lambda a, e: jnp.zeros_like(a) + jnp.asarray(e, a.dtype), part, identity)

    def one(turn, state):
        return combine(
            state, jax.tree.map(lambda a: lax.dynamic_index_in_dim(a, turn, 0, False), gathered)
        )

    return lax.fori_loop(0, place, one, state)


def shifted(block, axis, distance):
    devices = range(lax.axis_size(axis))
    route = [(i - distance, i) for i in devices if i - distance in devices]
    return lax.ppermute(block, axis, route)


def layer_norm(values, gain_vec, bias_vec):
    average = jnp.mean(values, axis=-1, keepdims=True)
    centred = values - average
    variance = jnp.mean(centred * centred, axis=-1, keepdims=True)
    return centred * lax.rsqrt(variance + EPSILON) * gain_vec + bias_vec


def gelu_exact(values):
    return jax.nn.gelu(values, approximate=False)


def rotation_tables(positions):
    half_size = HD // 2
    ladder = jnp.arange(half_size, dtype=jnp.float32)
    frequency = jnp.exp(ladder * (-2.0 * math.log(10000.0) / HD))
    angles = positions.astype(jnp.float32)[:, None] * frequency[None, :]
    return (jnp.cos(angles)[:, None, :], jnp.sin(angles)[:, None, :])


def rotate(field, cosine, sine):
    half_size = field.shape[-1] // 2
    former = field[..., :half_size]
    latter = field[..., half_size:]
    return jnp.concatenate(
        [former * cosine - latter * sine, latter * cosine + former * sine], axis=-1
    )


def outer_sum(left, right):
    return lax.dot_general(
        left, right, (((0,), (0,)), ((), ())), preferred_element_type=jnp.float32
    )


def block_allowed(begin, segment, extended_segments, valid_keys):
    offsets = (
        jnp.arange(QBLOCK, dtype=jnp.int32)[:, None]
        - jnp.arange(QBLOCK + REACH, dtype=jnp.int32)[None, :]
        + REACH
    )
    near = (offsets >= 0) & (offsets < WINDOW)
    query_segments = segment[begin : begin + QBLOCK]
    key_segments = extended_segments[begin : begin + QBLOCK + REACH]
    key_valid = valid_keys[begin : begin + QBLOCK + REACH]
    return near & (query_segments[:, None] == key_segments[None, :]) & key_valid[None, :]


def block_scores(query_block, key_window, allowed):
    raw = jnp.einsum(
        "qhd,khd->hqk", query_block, key_window, preferred_element_type=jnp.float32
    ) * (1.0 / math.sqrt(HD))
    return jnp.where(allowed[None], raw, NEGATIVE)


def local(
    inputs,
    cotangent,
    segment_ids,
    qkv_weight,
    out_weight,
    up_weight,
    down_weight,
    norm_gain_one,
    norm_bias_one,
    attn_scale,
    norm_gain_two,
    norm_bias_two,
    mlp_scale,
):
    frames = inputs.shape[1]
    width = inputs.shape[2]
    low_type = jnp.bfloat16
    gathered = (
        lax.all_gather(qkv_weight.astype(low_type), "tm", axis=1, tiled=True),
        lax.all_gather(out_weight.astype(low_type), "tm", axis=1, tiled=True),
        lax.all_gather(up_weight.astype(low_type), "tm", axis=1, tiled=True),
        lax.all_gather(down_weight.astype(low_type), "tm", axis=1, tiled=True),
        lax.all_gather(norm_gain_one.astype(low_type), "tm", axis=0, tiled=True),
        lax.all_gather(norm_bias_one.astype(low_type), "tm", axis=0, tiled=True),
        lax.all_gather(attn_scale.astype(low_type), "tm", axis=0, tiled=True),
        lax.all_gather(norm_gain_two.astype(low_type), "tm", axis=0, tiled=True),
        lax.all_gather(norm_bias_two.astype(low_type), "tm", axis=0, tiled=True),
        lax.all_gather(mlp_scale.astype(low_type), "tm", axis=0, tiled=True),
    )
    w_qkv, w_out, w_up, w_down = (
        lax.all_gather(gathered[0], "rows", axis=0, tiled=True),
        lax.all_gather(gathered[1], "rows", axis=0, tiled=True),
        lax.all_gather(gathered[2], "rows", axis=0, tiled=True),
        lax.all_gather(gathered[3], "rows", axis=0, tiled=True),
    )
    gain_one, bias_one, scale_one, gain_two, bias_two, scale_two = [
        piece.astype(jnp.float32) for piece in gathered[4:]
    ]
    segment = segment_ids[0]
    index = jnp.arange(frames, dtype=jnp.int32)
    last_run = jnp.sum((segment == segment[frames - 1]).astype(jnp.int32), keepdims=True)

    def join_runs(earlier, later):
        extends = (later[1] == frames) & (later[0] == earlier[0])
        joined = jnp.where(extends, earlier[1] + later[1], later[1])
        vacant = later[0] < 0
        return (jnp.where(vacant, earlier[0], later[0]), jnp.where(vacant, earlier[1], joined))

    before_id, before_run = prefix(
        (segment[frames - 1 :], last_run),
        "tm",
        join_runs,
        (jnp.full((1,), -1, jnp.int32), jnp.zeros((1,), jnp.int32)),
    )
    change = jnp.concatenate([jnp.ones((1,), jnp.bool_), segment[1:] != segment[:-1]])
    starts = lax.cummax(jnp.where(change, index, jnp.zeros_like(index)), axis=0)
    positions = index - starts + jnp.where(segment == before_id[0], before_run[0], 0)
    cosine, sine = rotation_tables(positions)
    source = inputs[0].astype(jnp.float32)
    normed_one, norm_one_pull = jax.vjp(layer_norm, source, gain_one, bias_one)
    normed_one_low = normed_one.astype(low_type)
    projected = jnp.dot(normed_one_low, w_qkv, preferred_element_type=jnp.float32)
    queries = rotate(projected[:, :width].reshape(frames, H, HD), cosine, sine).astype(low_type)
    keys_flat = (
        rotate(projected[:, width : 2 * width].reshape(frames, H, HD), cosine, sine)
        .reshape(frames, width)
        .astype(low_type)
    )
    values_flat = projected[:, 2 * width :].astype(low_type)
    got_keys, got_values, got_segments = shifted((keys_flat, values_flat, segment), "tm", 1)
    got_keys = got_keys[frames - REACH :]
    got_values = got_values[frames - REACH :]
    got_segments = got_segments[frames - REACH :]
    extended_keys = jnp.concatenate([got_keys, keys_flat], axis=0).reshape(REACH + frames, H, HD)
    extended_values = jnp.concatenate([got_values, values_flat], axis=0).reshape(
        REACH + frames, H, HD
    )
    extended_segments = jnp.concatenate([got_segments, segment])
    valid_keys = (lax.axis_index("tm") > 0) | (jnp.arange(REACH + frames, dtype=jnp.int32) >= REACH)
    block_count = frames // QBLOCK
    mixed_parts = []
    log_sums = []
    for block in range(block_count):
        begin = block * QBLOCK
        allowed = block_allowed(begin, segment, extended_segments, valid_keys)
        scores = block_scores(
            queries[begin : begin + QBLOCK], extended_keys[begin : begin + QBLOCK + REACH], allowed
        )
        top = jnp.max(scores, axis=-1, keepdims=True)
        weights = jnp.exp(scores - top)
        total = jnp.sum(weights, axis=-1, keepdims=True)
        probs = (weights / total).astype(low_type)
        mixed_parts.append(
            jnp.einsum(
                "hqk,khd->qhd",
                probs,
                extended_values[begin : begin + QBLOCK + REACH],
                preferred_element_type=jnp.float32,
            )
        )
        log_sums.append(top + jnp.log(total))
    mixed_low = jnp.concatenate(mixed_parts, axis=0).reshape(frames, width).astype(low_type)
    branch = jnp.dot(mixed_low, w_out, preferred_element_type=jnp.float32)
    after = source + scale_one * branch
    normed_two, norm_two_pull = jax.vjp(layer_norm, after, gain_two, bias_two)
    normed_two_low = normed_two.astype(low_type)
    hidden = jnp.dot(normed_two_low, w_up, preferred_element_type=jnp.float32)
    active, gelu_pull = jax.vjp(gelu_exact, hidden)
    active_low = active.astype(low_type)
    branch_two = jnp.dot(active_low, w_down, preferred_element_type=jnp.float32)
    result = (after + scale_two * branch_two).astype(low_type)
    again = (
        lax.all_gather(qkv_weight.astype(low_type), "tm", axis=1, tiled=True),
        lax.all_gather(out_weight.astype(low_type), "tm", axis=1, tiled=True),
        lax.all_gather(up_weight.astype(low_type), "tm", axis=1, tiled=True),
        lax.all_gather(down_weight.astype(low_type), "tm", axis=1, tiled=True),
    )
    back_qkv, back_out, back_up, back_down = (
        lax.all_gather(again[0], "rows", axis=0, tiled=True),
        lax.all_gather(again[1], "rows", axis=0, tiled=True),
        lax.all_gather(again[2], "rows", axis=0, tiled=True),
        lax.all_gather(again[3], "rows", axis=0, tiled=True),
    )
    upstream = cotangent[0].astype(jnp.float32)
    grad_scale_two = jnp.sum(upstream * branch_two, axis=0)
    grad_branch_two = (upstream * scale_two).astype(low_type)
    grad_down = outer_sum(active_low, grad_branch_two)
    grad_active = lax.dot_general(
        grad_branch_two, back_down, (((1,), (1,)), ((), ())), preferred_element_type=jnp.float32
    )
    grad_hidden = gelu_pull(grad_active)[0].astype(low_type)
    grad_up = outer_sum(normed_two_low, grad_hidden)
    grad_normed_two = lax.dot_general(
        grad_hidden, back_up, (((1,), (1,)), ((), ())), preferred_element_type=jnp.float32
    )
    after_part, grad_gain_two, grad_bias_two = norm_two_pull(grad_normed_two)
    grad_after = upstream + after_part
    grad_scale_one = jnp.sum(grad_after * branch, axis=0)
    grad_branch = (grad_after * scale_one).astype(low_type)
    grad_out = outer_sum(mixed_low, grad_branch)
    grad_mixed = lax.dot_general(
        grad_branch, back_out, (((1,), (1,)), ((), ())), preferred_element_type=jnp.float32
    )
    grad_mixed = grad_mixed.astype(low_type).reshape(frames, H, HD)
    factor = 1.0 / math.sqrt(HD)
    grad_keys_ext = jnp.zeros((REACH + frames, H, HD), jnp.float32)
    grad_values_ext = jnp.zeros((REACH + frames, H, HD), jnp.float32)
    query_grads = []
    for block in range(block_count):
        begin = block * QBLOCK
        allowed = block_allowed(begin, segment, extended_segments, valid_keys)
        query_block = queries[begin : begin + QBLOCK]
        key_window = extended_keys[begin : begin + QBLOCK + REACH]
        value_window = extended_values[begin : begin + QBLOCK + REACH]
        scores = block_scores(query_block, key_window, allowed)
        probs_full = jnp.exp(scores - log_sums[block])
        probs_low = probs_full.astype(low_type)
        grad_out_block = grad_mixed[begin : begin + QBLOCK]
        grad_probs = jnp.einsum(
            "qhd,khd->hqk", grad_out_block, value_window, preferred_element_type=jnp.float32
        )
        grad_values_ext = grad_values_ext.at[begin : begin + QBLOCK + REACH].add(
            jnp.einsum(
                "hqk,qhd->khd", probs_low, grad_out_block, preferred_element_type=jnp.float32
            )
        )
        balance = jnp.sum(grad_probs * probs_full, axis=-1, keepdims=True)
        grad_scores = (probs_full * (grad_probs - balance)).astype(low_type)
        query_grads.append(
            jnp.einsum("hqk,khd->qhd", grad_scores, key_window, preferred_element_type=jnp.float32)
            * factor
        )
        grad_keys_ext = grad_keys_ext.at[begin : begin + QBLOCK + REACH].add(
            jnp.einsum("hqk,qhd->khd", grad_scores, query_block, preferred_element_type=jnp.float32)
            * factor
        )
    grad_keys_flat = grad_keys_ext.reshape(REACH + frames, width)
    grad_values_flat = grad_values_ext.reshape(REACH + frames, width)
    back_keys, back_values = (
        shifted(grad_keys_flat[:REACH].astype(jnp.bfloat16), "tm", -1).astype(jnp.float32),
        shifted(grad_values_flat[:REACH].astype(jnp.bfloat16), "tm", -1).astype(jnp.float32),
    )
    own_keys = grad_keys_flat[REACH:]
    own_values = grad_values_flat[REACH:]
    own_keys = jnp.concatenate(
        [own_keys[: frames - REACH], own_keys[frames - REACH :] + back_keys], axis=0
    )
    own_values = jnp.concatenate(
        [own_values[: frames - REACH], own_values[frames - REACH :] + back_values], axis=0
    )
    grad_queries = rotate(jnp.concatenate(query_grads, axis=0), cosine, -sine).reshape(
        frames, width
    )
    grad_keys = rotate(own_keys.reshape(frames, H, HD), cosine, -sine).reshape(frames, width)
    grad_projected = jnp.concatenate([grad_queries, grad_keys, own_values], axis=1).astype(low_type)
    grad_qkv = outer_sum(normed_one_low, grad_projected)
    grad_normed_one = lax.dot_general(
        grad_projected, back_qkv, (((1,), (1,)), ((), ())), preferred_element_type=jnp.float32
    )
    source_part, grad_gain_one, grad_bias_one = norm_one_pull(grad_normed_one)
    input_grad = (grad_after + source_part).astype(low_type)
    reduced = (
        lax.psum_scatter(grad_qkv, "tm", scatter_dimension=1, tiled=True),
        lax.psum_scatter(grad_out, "tm", scatter_dimension=1, tiled=True),
        lax.psum_scatter(grad_up, "tm", scatter_dimension=1, tiled=True),
        lax.psum_scatter(grad_down, "tm", scatter_dimension=1, tiled=True),
        lax.psum_scatter(grad_gain_one, "tm", scatter_dimension=0, tiled=True),
        lax.psum_scatter(grad_bias_one, "tm", scatter_dimension=0, tiled=True),
        lax.psum_scatter(grad_scale_one, "tm", scatter_dimension=0, tiled=True),
        lax.psum_scatter(grad_gain_two, "tm", scatter_dimension=0, tiled=True),
        lax.psum_scatter(grad_bias_two, "tm", scatter_dimension=0, tiled=True),
        lax.psum_scatter(grad_scale_two, "tm", scatter_dimension=0, tiled=True),
    )
    qkv_grad, out_grad, up_grad, down_grad = (
        lax.psum_scatter(reduced[0], "rows", scatter_dimension=0, tiled=True),
        lax.psum_scatter(reduced[1], "rows", scatter_dimension=0, tiled=True),
        lax.psum_scatter(reduced[2], "rows", scatter_dimension=0, tiled=True),
        lax.psum_scatter(reduced[3], "rows", scatter_dimension=0, tiled=True),
    )
    vector_sums = lax.psum(
        (reduced[4], reduced[5], reduced[6], reduced[7], reduced[8], reduced[9]), "rows"
    )
    return (
        result[None],
        input_grad[None],
        qkv_grad,
        out_grad,
        up_grad,
        down_grad,
        vector_sums[0],
        vector_sums[1],
        vector_sums[2],
        vector_sums[3],
        vector_sums[4],
        vector_sums[5],
    )


MESH_IDS = pl.DeviceIdType.MESH
F32 = jnp.float32
BF16 = jnp.bfloat16


def dot(left, right, contract=((1,), (0,))):
    return lax.dot_general(left, right, (contract, ((), ())), preferred_element_type=F32)


def dot_t(left, right):
    return dot(left, right, ((1,), (1,)))


def start_of(index, size):
    return pl.ds(pl.multiple_of(index * size, size), size)


def coordinates():
    row, core = lax.axis_index("rows"), lax.axis_index("tm")
    return row, core, lax.rem(row, 2), lax.rem(lax.div(row, 2), 2), lax.div(row, 4)


def peers_of(at):
    row, core, x, y, z = at
    found = {
        "x": (row + 1 - 2 * x, core),
        "y": (row + 2 - 4 * y, core),
        "s": (row, 1 - core),
    }
    for k in (1, 2, 3):
        found[k] = (lax.rem(z + k, 4) * 4 + lax.rem(row, 4), core)
    return found


def enter(peers):
    barrier = pltpu.get_barrier_semaphore()
    for peer in peers.values():
        pl.semaphore_signal(barrier, inc=1, device_id=peer, device_id_type=MESH_IDS)
    pl.semaphore_wait(barrier, len(peers))


class Links:
    def __init__(self, sems, peers):
        self.send, self.recv = sems
        self.peers = peers
        self.used = 0
        self.started = []

    def copy(self, src, dst, peer):
        slot = self.used
        self.used += 1
        made = pltpu.make_async_remote_copy(
            src_ref=src,
            dst_ref=dst,
            send_sem=self.send.at[slot],
            recv_sem=self.recv.at[slot],
            device_id=self.peers[peer],
            device_id_type=MESH_IDS,
        )
        self.started.append(made)
        return made

    def drain(self, skip=()):
        for made in self.started:
            if not any(made is s for s in skip):
                made.wait_send()


def gather_copies(full, links, at):
    row, core, x, y, z = at
    half = full.shape[4] // 2
    low, high = pl.ds(0, half), pl.ds(half, half)
    every = slice(None)
    table = [
        ("a1", (core, z, y, x), 1),
        ("a2", (core, z, y, x), 2),
        ("a3", (core, z, y, x), 3),
        ("b1", (core, every, y, x, low), "x"),
        ("b2", (core, every, y, x, high), "y"),
        ("c1", (core, every, y, every, low), "y"),
        ("c2", (core, every, every, x, high), "x"),
        ("da", (core, every, y, x), "s"),
        ("db1", (core, every, y, 1 - x, low), "s"),
        ("db2", (core, every, 1 - y, x, high), "s"),
        ("dc1", (core, every, 1 - y, every, low), "s"),
        ("dc2", (core, every, every, 1 - x, high), "s"),
    ]
    return {
        name: links.copy(full.at[where], full.at[where], peer) for name, where, peer in table
    }


GATHER_STEPS = (
    ((), ("a1", "a2", "a3")),
    (("a1", "a2", "a3"), ("b1", "b2", "da")),
    (("b1", "b2"), ("c1", "c2", "db1", "db2")),
    (("c1", "c2"), ("dc1", "dc2")),
    (("da", "db1", "db2", "dc1", "dc2"), ()),
)


def gather_step(copies, step):
    waits, starts = GATHER_STEPS[step]
    for name in waits:
        copies[name].wait_recv()
    for name in starts:
        copies[name].start()


def scatter_buffers(rows, columns):
    half = rows // 2
    return [
        ((4, 2, 2, rows, columns), BF16),
        ((4, 2, 2, rows, columns), BF16),
        ((2, 4, 2, half, columns), BF16),
        ((2, 4, half, columns), BF16),
        ((3, rows, columns), BF16),
    ]


class Scatter:
    def __init__(self, own, bufs, result, rows, links, at):
        self.own, self.result, self.rows, self.at = own, result, rows, at
        self.out, self.s_in, self.c_in, self.b_in, self.a_in = bufs
        row, core, x, y, z = at
        half = rows // 2
        self.half = half
        self.low, self.high = pl.ds(0, half), pl.ds(half, half)
        every = slice(None)
        low, high, out = self.low, self.high, self.out
        self.d = links.copy(out, self.s_in, "s")
        self.c1 = links.copy(out.at[every, 1 - y, every, low], self.c_in.at[0], "y")
        self.c2 = links.copy(out.at[every, every, 1 - x, high], self.c_in.at[1], "x")
        self.b1 = links.copy(out.at[every, y, 1 - x, low], self.b_in.at[0], "x")
        self.b2 = links.copy(out.at[every, 1 - y, x, high], self.b_in.at[1], "y")
        self.a = [
            links.copy(out.at[lax.rem(z + k, 4), y, x], self.a_in.at[k - 1], k) for k in (1, 2, 3)
        ]

    def mine(self, k, y, x, part):
        begin = ((k * 2 + y) * 2 + x) * self.rows + part * self.half
        return self.own[pl.ds(pl.multiple_of(begin, self.half), self.half), :] + self.s_in[
            k, y, x, pl.ds(part * self.half, self.half)
        ].astype(F32)

    def step(self, number):
        row, core, x, y, z = self.at
        low, high, out = self.low, self.high, self.out
        c_in, b_in = self.c_in, self.b_in
        if number == 0:
            self.d.start()
        if number == 1:
            self.d.wait()
            for k in range(4):
                for i in range(2):
                    out[k, 1 - y, i, low] = self.mine(k, 1 - y, i, 0).astype(BF16)
            self.c1.start()
            for k in range(4):
                for i in range(2):
                    out[k, i, 1 - x, high] = self.mine(k, i, 1 - x, 1).astype(BF16)
            self.c2.start()
        if number == 2:
            self.c1.wait_recv()
            for k in range(4):
                out[k, y, 1 - x, low] = (
                    self.mine(k, y, 1 - x, 0) + c_in[0, k, 1 - x].astype(F32)
                ).astype(BF16)
            self.b1.start()
            self.c2.wait_recv()
            for k in range(4):
                out[k, 1 - y, x, high] = (
                    self.mine(k, 1 - y, x, 1) + c_in[1, k, 1 - y].astype(F32)
                ).astype(BF16)
            self.b2.start()
        if number == 3:
            self.b1.wait_recv()
            self.b2.wait_recv()
            for k in (1, 2, 3):
                there = lax.rem(z + k, 4)
                out[there, y, x, low] = self.column(there, 0).astype(BF16)
                out[there, y, x, high] = self.column(there, 1).astype(BF16)
                self.a[k - 1].start()
            self.result[low, :] = self.column(z, 0)
            self.result[high, :] = self.column(z, 1)
        if number == 4:
            for k in range(3):
                self.a[k].wait_recv()
            self.result[...] = self.result[...] + (
                self.a_in[0].astype(F32) + self.a_in[1].astype(F32) + self.a_in[2].astype(F32)
            )

    def column(self, k, part):
        row, core, x, y, z = self.at
        place = x if part == 0 else y
        return (
            self.mine(k, y, x, part)
            + self.c_in[part, k, place].astype(F32)
            + self.b_in[part, k].astype(F32)
        )


def normal_tail(values):
    t = 1.0 / (1.0 + TAIL_P * jnp.abs(values))
    e = jnp.exp(-0.5 * (values * values))
    series = jnp.full_like(values, TAIL[-1])
    for term in TAIL[-2::-1]:
        series = series * t + term
    return series * t * e, e


TAIL_P = 0.4 / math.sqrt(2.0)
TAIL = (
    0.11283793097319604,
    0.11283480301555754,
    0.10392122984713166,
    0.08427214046581868,
    0.0707105879765068,
    -0.002791732410193116,
    0.08452735931959071,
    -0.09144066126533841,
    0.025128404380787478,
)


def lane_pattern(shape, size):
    return lax.rem(lax.broadcasted_iota(jnp.int32, shape, len(shape) - 1), size)


def turned(values, cosine, sine):
    first = lane_pattern(values.shape, HD) < HD // 2
    swapped = jnp.where(first, pltpu.roll(values, 96, 1), pltpu.roll(values, 32, 1))
    return values * cosine + swapped * sine


TILE = 256
BLOCK = 128
SPAN = BLOCK + REACH
PAIRS = H // 2

NAMES = [
    "y", "ig", "gq", "go", "gu", "gd", "gv",
]


def scratch_list(frames, width, hidden):
    blocks = frames // BLOCK
    ext = REACH + frames
    items = [
        ("wq", (2, 4, 2, 2, width // 16, 3 * width // 2), BF16),
        ("wo", (2, 4, 2, 2, width // 16, width // 2), BF16),
        ("wu", (2, 4, 2, 2, width // 16, hidden // 2), BF16),
        ("wd", (2, 4, 2, 2, hidden // 16, width // 2), BF16),
        ("vecs", (2, 8, width // 2), F32),
        ("segs", (2, 8, frames), F32),
        ("n1t", (width, frames), BF16),
        ("cos", (frames, 128), F32),
        ("sin", (frames, 128), F32),
        ("bias", (blocks, SPAN, BLOCK), BF16),
        ("qm", (PAIRS, 2 * frames, 128), BF16),
        ("kx", (PAIRS, ext, 128), BF16),
        ("vx", (PAIRS, ext, 128), BF16),
        ("kt", (PAIRS, 128, ext), BF16),
        ("vt", (PAIRS, 128, ext), BF16),
        ("probs", (PAIRS, blocks, SPAN, 2 * BLOCK), BF16),
        ("ot", (width, frames), BF16),
        ("n2t", (width, frames), BF16),
        ("act", (frames, hidden), BF16),
        ("du", (2, frames, hidden // 2), BF16),
        ("own_u", (width, hidden // 2), F32),
        ("own_d", (hidden * 2, 128), F32),
        ("own_o", (width, width // 2), F32),
        ("own_q", (width, 3 * width // 2), F32),
        ("dbmt", (width, frames), BF16),
        ("dba", (2, frames, width // 2), BF16),
        ("dom", (PAIRS, 2 * frames, 128), BF16),
        ("dx1", (frames, width), F32),
        ("dkx", (ext, 128), F32),
        ("dvx", (ext, 128), F32),
        ("h_out", (PAIRS, 2, REACH, 128), BF16),
        ("h_in", (PAIRS, 2, REACH, 128), BF16),
        ("acc", (8, width), F32),
        ("v_out", (3, 8, width // 2), F32),
        ("v_in", (3, 8, width // 2), F32),
        ("v_z", (4, 8, width // 2), F32),
        ("down_t", (width // 2, hidden // 16), F32),
    ]
    for name, rows, columns in (
        ("q", width // 16, 3 * width // 2),
        ("o", width // 16, width // 2),
        ("u", width // 16, hidden // 2),
        ("d", width // 2, hidden // 16),
    ):
        for i, (shape, kind) in enumerate(scatter_buffers(rows, columns)):
            if i > 0 or name in "qd":
                items.append(("s_%s%d" % (name, i), shape, kind))
    return items


SLOTS = 120


def layer_kernel(names, *refs):
    x_ref, dy_ref, seg_ref = refs[:3]
    shards, vectors = refs[3:7], refs[7:13]
    y_ref, ig_ref, gq, go, gu, gd, gv = refs[13:20]
    m = dict(zip(names, refs[20:-2]))
    at = coordinates()
    row, core, x, y, z = at
    peers = peers_of(at)
    links = Links(refs[-2:], peers)
    frames, width = x_ref.shape[1:]
    hidden = m["act"].shape[1]
    blocks, tiles = frames // BLOCK, frames // TILE
    factor = 1.0 / math.sqrt(HD)
    wq, wo, wu, wd = m["wq"], m["wo"], m["wu"], m["wd"]
    other = 1 - core

    for shard, full in zip(shards, (wq, wo, wu, wd)):
        full[core, z, y, x] = shard[...].astype(BF16)
    m["vecs"][core] = jnp.concatenate(
        [v[...].astype(BF16).astype(F32) for v in vectors]
        + [jnp.zeros((2, width // 2), F32)],
        axis=0,
    )
    m["segs"][core] = jnp.broadcast_to(seg_ref[...].astype(F32), (8, frames))
    enter(peers)
    vec_copy = links.copy(m["vecs"].at[core], m["vecs"].at[core], "s")
    seg_copy = links.copy(m["segs"].at[core], m["segs"].at[core], "s")
    gathers = [gather_copies(full, links, at) for full in (wq, wo, wu, wd)]
    vec_copy.start()
    seg_copy.start()
    for each in gathers:
        gather_step(each, 0)

    def vector(i):
        return jnp.concatenate([m["vecs"][0, i : i + 1, :], m["vecs"][1, i : i + 1, :]], axis=1)

    def normalized(values):
        average = jnp.mean(values, axis=-1, keepdims=True)
        centred = values - average
        variance = jnp.mean(centred * centred, axis=-1, keepdims=True)
        scale = lax.rsqrt(variance + EPSILON)
        return centred * scale, scale

    vec_copy.wait_recv()
    n1 = y_ref
    gain_one, bias_one = vector(0), vector(1)

    def norm_one(t, _):
        rows = start_of(t, TILE)
        unit, _scale = normalized(x_ref[0, rows, :].astype(F32))
        low = (unit * gain_one + bias_one).astype(BF16)
        n1[0, rows, :] = low
        m["n1t"][:, rows] = low.T
        return 0

    lax.fori_loop(0, tiles, norm_one, 0)
    gather_step(gathers[0], 1)

    seg_copy.wait_recv()
    segs = m["segs"]
    segc = m["own_d"]

    def spread(which, begin):
        line = segs[which, 0:1, pl.ds(pl.multiple_of(begin, BLOCK), BLOCK)]
        return jnp.broadcast_to(line, (BLOCK, BLOCK)).T

    for e in range(REACH // BLOCK):
        halo = spread(other, frames - REACH + e * BLOCK)
        segc[e * BLOCK : (e + 1) * BLOCK, :] = jnp.where(core > 0, halo, -1.0)

    lanes = lane_pattern((1, 128), HD // 2).astype(F32)
    frequency = jnp.exp(lanes * (-2.0 * math.log(10000.0) / HD))
    first_half = lane_pattern((BLOCK, 128), HD) < HD // 2

    def tables(b, _):
        rows = start_of(b, BLOCK)
        here = spread(core, b * BLOCK)
        segc[pl.ds(pl.multiple_of(REACH + b * BLOCK, BLOCK), BLOCK), :] = here
        count = jnp.zeros((BLOCK, BLOCK), F32)
        for which in range(2):
            for k in range(blocks):
                line = segs[which, 0:1, k * BLOCK : (k + 1) * BLOCK]
                count = count + jnp.where(line < here, 1.0, 0.0)
        began = jnp.sum(count, axis=1, keepdims=True)
        frame = lax.broadcasted_iota(jnp.int32, (BLOCK, 1), 0) + (core * frames + b * BLOCK)
        angle = (frame.astype(F32) - began) * frequency
        m["cos"][rows, :] = jnp.cos(angle)
        sine = jnp.sin(angle)
        m["sin"][rows, :] = jnp.where(first_half, -sine, sine)
        return 0

    lax.fori_loop(0, blocks, tables, 0)
    gather_step(gathers[0], 2)

    distance = (
        lax.broadcasted_iota(jnp.int32, (SPAN, BLOCK), 1)
        - lax.broadcasted_iota(jnp.int32, (SPAN, BLOCK), 0)
        + REACH
    )
    near = (distance >= 0) & (distance < WINDOW)

    def masks(b, _):
        keys = segc[pl.ds(pl.multiple_of(b * BLOCK, BLOCK), SPAN), :]
        line = segs[core, 0:1, start_of(b, BLOCK)]
        m["bias"][b] = jnp.where(near & (keys == line), 0.0, NEGATIVE).astype(BF16)
        return 0

    lax.fori_loop(0, blocks, masks, 0)
    gather_step(gathers[0], 3)
    gather_step(gathers[0], 4)
    for each in gathers[1:]:
        gather_step(each, 1)

    low_lanes = lane_pattern((1, 128), 128) < HD

    def two_heads(ref, p, b, value):
        zero = jnp.zeros_like(value)
        ref[p, pl.ds(pl.multiple_of(b * 2 * BLOCK, BLOCK), BLOCK), :] = jnp.where(
            low_lanes, value, zero
        )
        ref[p, pl.ds(pl.multiple_of((b * 2 + 1) * BLOCK, BLOCK), BLOCK), :] = jnp.where(
            low_lanes, zero, value
        )

    def project(t, _):
        rows = start_of(t, TILE)
        placed = pl.ds(pl.multiple_of(REACH + t * TILE, TILE), TILE)
        left = n1[0, rows, :]
        cosine, sine = m["cos"][rows, :], m["sin"][rows, :]
        for half in range(2):
            wide = dot(left, wq[half].reshape(width, -1))
            for j in range(6):
                chunk = wide[:, j * 128 : (j + 1) * 128]
                kind, p = divmod(half * 6 + j, PAIRS)
                if kind == 0:
                    value = (turned(chunk, cosine, sine).astype(BF16) * factor).astype(BF16)
                    for i in range(TILE // BLOCK):
                        two_heads(
                            m["qm"], p, t * (TILE // BLOCK) + i, value[i * BLOCK : (i + 1) * BLOCK]
                        )
                elif kind == 1:
                    value = turned(chunk, cosine, sine).astype(BF16)
                    m["kx"][p, placed, :] = value
                    m["kt"][p, :, placed] = value.T
                else:
                    value = chunk.astype(BF16)
                    m["vx"][p, placed, :] = value
                    m["vt"][p, :, placed] = value.T
        return 0

    lax.fori_loop(0, tiles, project, 0)
    tail, head = pl.ds(frames, REACH), pl.ds(0, REACH)
    halo_copies = [
        links.copy(m[r].at[:, tail], m[r].at[:, head], "s") for r in ("kx", "vx")
    ]
    for each in halo_copies:
        each.start()
    for each in gathers[1:]:
        gather_step(each, 2)
    for each in halo_copies:
        each.wait_recv()
    for p in range(PAIRS):
        m["kt"][p, :, 0:REACH] = m["kx"][p, 0:REACH, :].T
        m["vt"][p, :, 0:REACH] = m["vx"][p, 0:REACH, :].T

    mixed = ig_ref

    def heads_joined(both):
        return jnp.concatenate([both[:HD, :BLOCK], both[HD:, BLOCK:]], axis=0)

    def attend(b, _):
        rows = start_of(b, BLOCK)
        window = pl.ds(pl.multiple_of(b * BLOCK, BLOCK), SPAN)
        mask = m["bias"][b].astype(F32)
        mask = jnp.concatenate([mask, mask], axis=1)
        for p in range(PAIRS):
            scores = dot_t(m["kx"][p, window, :], m["qm"][p, start_of(b, 2 * BLOCK), :]) + mask
            top = jnp.max(scores, axis=0, keepdims=True)
            weights = jnp.exp(scores - top)
            total = jnp.sum(weights, axis=0, keepdims=True)
            probs = (weights * (1.0 / total)).astype(BF16)
            m["probs"][p, b] = probs
            joined = heads_joined(dot(m["vt"][p, :, window], probs))
            m["ot"][p * 128 : (p + 1) * 128, rows] = joined.astype(BF16)
            mixed[0, rows, p * 128 : (p + 1) * 128] = joined.T.astype(BF16)
        return 0

    lax.fori_loop(0, blocks, attend, 0)
    for each in gathers[1:]:
        gather_step(each, 3)
    for each in gathers[1:]:
        gather_step(each, 4)

    m["acc"][...] = jnp.zeros_like(m["acc"])
    acc = m["acc"]

    def add_to(i, values):
        acc[i : i + 1, :] = acc[i : i + 1, :] + jnp.sum(values, axis=0, keepdims=True)

    scale_one, gain_two, bias_two, scale_two = vector(2), vector(3), vector(4), vector(5)
    slope = m["own_u"]
    part = hidden // 4

    def norm_back(unit, scale, gain, grad):
        inner = grad * gain
        return scale * (
            inner
            - jnp.mean(inner, axis=-1, keepdims=True)
            - unit * jnp.mean(inner * unit, axis=-1, keepdims=True)
        )

    def middle(t, _):
        rows = start_of(t, TILE)
        both = mixed[0, rows, :]
        branch = jnp.concatenate(
            [dot(both, wo[h].reshape(width, -1)) for h in range(2)], axis=1
        )
        after = x_ref[0, rows, :].astype(F32) + scale_one * branch
        unit, scale = normalized(after)
        n2 = (unit * gain_two + bias_two).astype(BF16)
        m["n2t"][:, rows] = n2.T
        for n in range(4):
            half, columns = n // 2, pl.ds((n % 2) * part, part)
            up = dot(n2, wu[half, :, :, :, :, columns].reshape(width, part))
            tail_value, bell = normal_tail(up)
            cdf = jnp.where(up >= 0.0, 1.0 - tail_value, tail_value)
            m["act"][rows, n * part : (n + 1) * part] = (up * cdf).astype(BF16)
            slope[half * TILE : (half + 1) * TILE, columns] = cdf + up * (
                bell * (1.0 / math.sqrt(2.0 * math.pi))
            )
        act = m["act"][rows, :]
        branch_two = jnp.concatenate(
            [dot(act, wd[h].reshape(hidden, -1)) for h in range(2)], axis=1
        )
        y_ref[0, rows, :] = (after + scale_two * branch_two).astype(BF16)
        upstream = dy_ref[0, rows, :].astype(F32)
        add_to(5, upstream * branch_two)
        dbm = (upstream * scale_two).astype(BF16)
        m["dbmt"][:, rows] = dbm.T
        grad = jnp.zeros((TILE, width), F32)
        for n in range(4):
            half, columns = n // 2, pl.ds((n % 2) * part, part)
            back = dot_t(dbm[:, : width // 2], wd[0, n].reshape(part, -1)) + dot_t(
                dbm[:, width // 2 :], wd[1, n].reshape(part, -1)
            )
            du = (back * slope[half * TILE : (half + 1) * TILE, columns]).astype(BF16)
            m["du"][half, rows, columns] = du
            grad = grad + dot_t(du, wu[half, :, :, :, :, columns].reshape(width, part))
        add_to(3, grad * unit)
        add_to(4, grad)
        dx1 = upstream + norm_back(unit, scale, gain_two, grad)
        m["dx1"][rows, :] = dx1
        add_to(2, dx1 * branch)
        dba = (dx1 * scale_one).astype(BF16)
        m["dba"][0, rows, :] = dba[:, : width // 2]
        m["dba"][1, rows, :] = dba[:, width // 2 :]
        dmixed = (
            dot_t(dba[:, : width // 2], wo[0].reshape(width, -1))
            + dot_t(dba[:, width // 2 :], wo[1].reshape(width, -1))
        ).astype(BF16)
        for p in range(PAIRS):
            for i in range(TILE // BLOCK):
                two_heads(
                    m["dom"],
                    p,
                    t * (TILE // BLOCK) + i,
                    dmixed[i * BLOCK : (i + 1) * BLOCK, p * 128 : (p + 1) * 128],
                )
        return 0

    lax.fori_loop(0, tiles, middle, 0)

    for each in gathers:
        for made in each.values():
            made.wait_send()
    m["s_u0"], m["s_o0"] = wu.at[0], wo.at[0]

    def scatter(name, own, result, rows):
        bufs = [m["s_%s%d" % (name, i)] for i in range(5)]
        return Scatter(own, bufs, result, rows, links, at)

    sum_u = scatter("u", m["own_u"], gu, width // 16)
    sum_d = scatter("d", m["own_d"], m["down_t"], width // 2)
    sum_o = scatter("o", m["own_o"], go, width // 16)
    sum_q = scatter("q", m["own_q"], gq, width // 16)

    def down_grads(k, _):
        right = m["act"][:, start_of(k, hidden // 4)]
        for which, side in ((0, core), (1, other)):
            made = dot(m["dbmt"][start_of(side, width // 2), :], right)
            for i in range(4):
                piece = made[:, i * 128 : (i + 1) * 128]
                if which == 0:
                    m["own_d"][start_of(k * 4 + i, width // 2), :] = piece
                else:
                    sum_d.out[k, i // 2, i % 2] = piece.astype(BF16)
        return 0

    lax.fori_loop(0, 4, down_grads, 0)
    sum_d.step(0)

    def columns_of(sum_x, left, right_ref, step):
        def one(n, _):
            columns = start_of(n, step)
            sum_x.own[:, columns] = dot(left[...], right_ref[core, :, columns])
            made = dot(left[...], right_ref[other, :, columns]).astype(BF16)
            sum_x.out[:, :, :, :, columns] = made.reshape(4, 2, 2, -1, step)
            return 0

        lax.fori_loop(0, sum_x.own.shape[1] // step, one, 0)
        sum_x.step(0)

    columns_of(sum_u, m["n2t"], m["du"], 256)
    columns_of(sum_o, m["ot"], m["dba"], 256)
    dp = m["du"]

    plan = [
        [(sum_d, 1), (sum_u, 1)],
        [(sum_o, 1), (sum_d, 2), (sum_u, 2)],
        [(sum_o, 2), (sum_d, 3), (sum_u, 3)],
        [(sum_o, 3), (sum_d, 4), (sum_u, 4)],
    ]
    for p in range(PAIRS):
        dkx, dvx = m["dkx"], m["dvx"]
        dkx[...] = jnp.zeros_like(dkx)
        dvx[...] = jnp.zeros_like(dvx)

        def attend_back(b, _, p=p):
            rows = start_of(b, BLOCK)
            window = pl.ds(pl.multiple_of(b * BLOCK, BLOCK), SPAN)
            queries = m["qm"][p, start_of(b, 2 * BLOCK), :]
            dmixed = m["dom"][p, start_of(b, 2 * BLOCK), :]
            low = m["probs"][p, b]
            probs = low.astype(F32)
            dprobs = dot_t(m["vx"][p, window, :], dmixed)
            balance = jnp.sum(dprobs * probs, axis=0, keepdims=True)
            dscores = (probs * (dprobs - balance)).astype(BF16)
            dvx[window, :] = dvx[window, :] + dot(low, dmixed)
            dkx[window, :] = dkx[window, :] + dot(dscores, queries)
            joined = heads_joined(dot(m["kt"][p, :, window], dscores)).T * factor
            m["du"][0, rows, p * 128 : (p + 1) * 128] = turned(
                joined, m["cos"][rows, :], -m["sin"][rows, :]
            ).astype(BF16)
            return 0

        lax.fori_loop(0, 2, attend_back, 0)
        h_out, h_in = m["h_out"], m["h_in"]
        h_out[p, 0] = dkx[0:REACH, :].astype(BF16)
        h_out[p, 1] = dvx[0:REACH, :].astype(BF16)
        halo_back = links.copy(h_out.at[p], h_in.at[p], "s")
        halo_back.start()
        for one, step in plan[p]:
            one.step(step)
        lax.fori_loop(2, blocks, attend_back, 0)
        halo_back.wait_recv()
        dkx[tail, :] = dkx[tail, :] + h_in[p, 0].astype(F32)
        dvx[tail, :] = dvx[tail, :] + h_in[p, 1].astype(F32)
        k_half, k_at = divmod(PAIRS + p, 6)
        v_half, v_at = divmod(2 * PAIRS + p, 6)

        def finish(t, _, k_half=k_half, k_at=k_at, v_half=v_half, v_at=v_at):
            rows = start_of(t, TILE)
            placed = pl.ds(pl.multiple_of(REACH + t * TILE, TILE), TILE)
            dp[k_half, rows, k_at * 128 : (k_at + 1) * 128] = turned(
                dkx[placed, :], m["cos"][rows, :], -m["sin"][rows, :]
            ).astype(BF16)
            dp[v_half, rows, v_at * 128 : (v_at + 1) * 128] = dvx[placed, :].astype(BF16)
            return 0

        lax.fori_loop(0, tiles, finish, 0)

    sum_o.step(4)
    columns_of(sum_q, m["n1t"], dp, 256)

    def first(t, _):
        rows = start_of(t, TILE)
        grad = dot_t(dp[0, rows, : 3 * width // 2], wq[0].reshape(width, -1)) + dot_t(
            dp[1, rows, : 3 * width // 2], wq[1].reshape(width, -1)
        )
        unit, scale = normalized(x_ref[0, rows, :].astype(F32))
        add_to(0, grad * unit)
        add_to(1, grad)
        ig_ref[0, rows, :] = (
            m["dx1"][rows, :] + norm_back(unit, scale, gain_one, grad)
        ).astype(BF16)
        return 0

    lax.fori_loop(0, tiles, first, 0)

    v_out, v_in, v_z = m["v_out"], m["v_in"], m["v_z"]
    here, there = start_of(core, width // 2), start_of(other, width // 2)
    v_out[0] = acc[:, there]
    hops = [links.copy(v_out.at[i], v_in.at[i], peer) for i, peer in enumerate(("s", "y", "x"))]
    hops[0].start()
    sum_q.step(1)
    hops[0].wait_recv()
    v_out[1] = acc[:, here] + v_in[0]
    hops[1].start()
    sum_q.step(2)
    hops[1].wait_recv()
    v_out[2] = v_out[1] + v_in[1]
    hops[2].start()
    sum_q.step(3)
    hops[2].wait_recv()
    v_z[z] = v_out[2] + v_in[2]
    spreads = [links.copy(v_z.at[z], v_z.at[z], k) for k in (1, 2, 3)]
    for each in spreads:
        each.start()
    sum_q.step(4)
    gd[...] = m["down_t"][...].T
    for each in spreads:
        each.wait_recv()
    gv[...] = (v_z[0] + v_z[1]) + (v_z[2] + v_z[3])
    gathered = [made for each in gathers for made in each.values()]
    links.drain(skip=gathered + [one.d for one in (sum_u, sum_d, sum_o, sum_q)])


def local_staged(
    inputs,
    cotangent,
    segment_ids,
    qkv_weight,
    out_weight,
    up_weight,
    down_weight,
    *vectors,
):
    frames, width = inputs.shape[1:]
    hidden = up_weight.shape[1] * 2
    items = scratch_list(frames, width, hidden)
    whole = pl.BlockSpec(memory_space=pltpu.VMEM)
    outs = [
        jax.ShapeDtypeStruct(inputs.shape, BF16),
        jax.ShapeDtypeStruct(inputs.shape, BF16),
        *[
            jax.ShapeDtypeStruct(w.shape, F32)
            for w in (qkv_weight, out_weight, up_weight, down_weight)
        ],
        jax.ShapeDtypeStruct((8, width // 2), F32),
    ]
    results = pl.pallas_call(
        functools.partial(layer_kernel, [name for name, _, _ in items]),
        out_shape=outs,
        in_specs=[whole] * 13,
        out_specs=[whole] * 7,
        scratch_shapes=[pltpu.VMEM(shape, kind) for _, shape, kind in items]
        + [pltpu.SemaphoreType.DMA((SLOTS,)), pltpu.SemaphoreType.DMA((SLOTS,))],
        compiler_params=pltpu.CompilerParams(
            collective_id=0, has_side_effects=True, vmem_limit_bytes=VMEM_LIMIT
        ),
    )(
        inputs,
        cotangent,
        segment_ids,
        qkv_weight,
        out_weight,
        up_weight,
        down_weight,
        *[v.reshape(1, -1) for v in vectors],
    )
    sums = results[6]
    return (*results[:6], *[sums[i] for i in range(6)])


VMEM_LIMIT = 64 * 2**20


def solution(mesh):
    placed = (
        P("rows", "tm", None),
        P("rows", "tm", None),
        P("rows", "tm"),
        P("rows", "tm"),
        P("rows", "tm"),
        P("rows", "tm"),
        P("rows", "tm"),
        P("tm"),
        P("tm"),
        P("tm"),
        P("tm"),
        P("tm"),
        P("tm"),
    )
    staged = mesh.shape["rows"] == 16 and mesh.shape["tm"] == 2
    return jax.shard_map(
        local_staged if staged else local,
        mesh=mesh,
        in_specs=placed,
        out_specs=(
            P("rows", "tm", None),
            P("rows", "tm", None),
            P("rows", "tm"),
            P("rows", "tm"),
            P("rows", "tm"),
            P("rows", "tm"),
            P("tm"),
            P("tm"),
            P("tm"),
            P("tm"),
            P("tm"),
            P("tm"),
        ),
        check_vma=False,
    )
```

```python
import functools
import math

import jax
import jax.numpy as jnp
from jax import lax
from jax.experimental import pallas as pl
from jax.experimental.pallas import tpu as pltpu
from jax.sharding import PartitionSpec as P

H = 8
HD = 64
WINDOW = 250
REACH = 256
QBLOCK = 512


EPSILON = 1e-05
NEGATIVE = -1e30


def prefix(part, axis, combine, identity):
    place = lax.axis_index(axis)
    gathered = jax.tree.map(lambda a: lax.all_gather(a, axis), part)
    state = jax.tree.map(lambda a, e: jnp.zeros_like(a) + jnp.asarray(e, a.dtype), part, identity)

    def one(turn, state):
        return combine(
            state, jax.tree.map(lambda a: lax.dynamic_index_in_dim(a, turn, 0, False), gathered)
        )

    return lax.fori_loop(0, place, one, state)


def shifted(block, axis, distance):
    devices = range(lax.axis_size(axis))
    route = [(i - distance, i) for i in devices if i - distance in devices]
    return lax.ppermute(block, axis, route)


def layer_norm(values, gain_vec, bias_vec):
    average = jnp.mean(values, axis=-1, keepdims=True)
    centred = values - average
    variance = jnp.mean(centred * centred, axis=-1, keepdims=True)
    return centred * lax.rsqrt(variance + EPSILON) * gain_vec + bias_vec


def gelu_exact(values):
    return jax.nn.gelu(values, approximate=False)


def rotation_tables(positions):
    half_size = HD // 2
    ladder = jnp.arange(half_size, dtype=jnp.float32)
    frequency = jnp.exp(ladder * (-2.0 * math.log(10000.0) / HD))
    angles = positions.astype(jnp.float32)[:, None] * frequency[None, :]
    return (jnp.cos(angles)[:, None, :], jnp.sin(angles)[:, None, :])


def rotate(field, cosine, sine):
    half_size = field.shape[-1] // 2
    former = field[..., :half_size]
    latter = field[..., half_size:]
    return jnp.concatenate(
        [former * cosine - latter * sine, latter * cosine + former * sine], axis=-1
    )


def outer_sum(left, right):
    return lax.dot_general(
        left, right, (((0,), (0,)), ((), ())), preferred_element_type=jnp.float32
    )


def block_allowed(begin, segment, extended_segments, valid_keys):
    offsets = (
        jnp.arange(QBLOCK, dtype=jnp.int32)[:, None]
        - jnp.arange(QBLOCK + REACH, dtype=jnp.int32)[None, :]
        + REACH
    )
    near = (offsets >= 0) & (offsets < WINDOW)
    query_segments = segment[begin : begin + QBLOCK]
    key_segments = extended_segments[begin : begin + QBLOCK + REACH]
    key_valid = valid_keys[begin : begin + QBLOCK + REACH]
    return near & (query_segments[:, None] == key_segments[None, :]) & key_valid[None, :]


def block_scores(query_block, key_window, allowed):
    raw = jnp.einsum(
        "qhd,khd->hqk", query_block, key_window, preferred_element_type=jnp.float32
    ) * (1.0 / math.sqrt(HD))
    return jnp.where(allowed[None], raw, NEGATIVE)


def local(
    inputs,
    cotangent,
    segment_ids,
    qkv_weight,
    out_weight,
    up_weight,
    down_weight,
    norm_gain_one,
    norm_bias_one,
    attn_scale,
    norm_gain_two,
    norm_bias_two,
    mlp_scale,
):
    frames = inputs.shape[1]
    width = inputs.shape[2]
    low_type = jnp.bfloat16
    gathered = (
        lax.all_gather(qkv_weight.astype(low_type), "tm", axis=1, tiled=True),
        lax.all_gather(out_weight.astype(low_type), "tm", axis=1, tiled=True),
        lax.all_gather(up_weight.astype(low_type), "tm", axis=1, tiled=True),
        lax.all_gather(down_weight.astype(low_type), "tm", axis=1, tiled=True),
        lax.all_gather(norm_gain_one.astype(low_type), "tm", axis=0, tiled=True),
        lax.all_gather(norm_bias_one.astype(low_type), "tm", axis=0, tiled=True),
        lax.all_gather(attn_scale.astype(low_type), "tm", axis=0, tiled=True),
        lax.all_gather(norm_gain_two.astype(low_type), "tm", axis=0, tiled=True),
        lax.all_gather(norm_bias_two.astype(low_type), "tm", axis=0, tiled=True),
        lax.all_gather(mlp_scale.astype(low_type), "tm", axis=0, tiled=True),
    )
    w_qkv, w_out, w_up, w_down = (
        lax.all_gather(gathered[0], "rows", axis=0, tiled=True),
        lax.all_gather(gathered[1], "rows", axis=0, tiled=True),
        lax.all_gather(gathered[2], "rows", axis=0, tiled=True),
        lax.all_gather(gathered[3], "rows", axis=0, tiled=True),
    )
    gain_one, bias_one, scale_one, gain_two, bias_two, scale_two = [
        piece.astype(jnp.float32) for piece in gathered[4:]
    ]
    segment = segment_ids[0]
    index = jnp.arange(frames, dtype=jnp.int32)
    last_run = jnp.sum((segment == segment[frames - 1]).astype(jnp.int32), keepdims=True)

    def join_runs(earlier, later):
        extends = (later[1] == frames) & (later[0] == earlier[0])
        joined = jnp.where(extends, earlier[1] + later[1], later[1])
        vacant = later[0] < 0
        return (jnp.where(vacant, earlier[0], later[0]), jnp.where(vacant, earlier[1], joined))

    before_id, before_run = prefix(
        (segment[frames - 1 :], last_run),
        "tm",
        join_runs,
        (jnp.full((1,), -1, jnp.int32), jnp.zeros((1,), jnp.int32)),
    )
    change = jnp.concatenate([jnp.ones((1,), jnp.bool_), segment[1:] != segment[:-1]])
    starts = lax.cummax(jnp.where(change, index, jnp.zeros_like(index)), axis=0)
    positions = index - starts + jnp.where(segment == before_id[0], before_run[0], 0)
    cosine, sine = rotation_tables(positions)
    source = inputs[0].astype(jnp.float32)
    normed_one, norm_one_pull = jax.vjp(layer_norm, source, gain_one, bias_one)
    normed_one_low = normed_one.astype(low_type)
    projected = jnp.dot(normed_one_low, w_qkv, preferred_element_type=jnp.float32)
    queries = rotate(projected[:, :width].reshape(frames, H, HD), cosine, sine).astype(low_type)
    keys_flat = (
        rotate(projected[:, width : 2 * width].reshape(frames, H, HD), cosine, sine)
        .reshape(frames, width)
        .astype(low_type)
    )
    values_flat = projected[:, 2 * width :].astype(low_type)
    got_keys, got_values, got_segments = shifted((keys_flat, values_flat, segment), "tm", 1)
    got_keys = got_keys[frames - REACH :]
    got_values = got_values[frames - REACH :]
    got_segments = got_segments[frames - REACH :]
    extended_keys = jnp.concatenate([got_keys, keys_flat], axis=0).reshape(REACH + frames, H, HD)
    extended_values = jnp.concatenate([got_values, values_flat], axis=0).reshape(
        REACH + frames, H, HD
    )
    extended_segments = jnp.concatenate([got_segments, segment])
    valid_keys = (lax.axis_index("tm") > 0) | (jnp.arange(REACH + frames, dtype=jnp.int32) >= REACH)
    block_count = frames // QBLOCK
    mixed_parts = []
    log_sums = []
    for block in range(block_count):
        begin = block * QBLOCK
        allowed = block_allowed(begin, segment, extended_segments, valid_keys)
        scores = block_scores(
            queries[begin : begin + QBLOCK], extended_keys[begin : begin + QBLOCK + REACH], allowed
        )
        top = jnp.max(scores, axis=-1, keepdims=True)
        weights = jnp.exp(scores - top)
        total = jnp.sum(weights, axis=-1, keepdims=True)
        probs = (weights / total).astype(low_type)
        mixed_parts.append(
            jnp.einsum(
                "hqk,khd->qhd",
                probs,
                extended_values[begin : begin + QBLOCK + REACH],
                preferred_element_type=jnp.float32,
            )
        )
        log_sums.append(top + jnp.log(total))
    mixed_low = jnp.concatenate(mixed_parts, axis=0).reshape(frames, width).astype(low_type)
    branch = jnp.dot(mixed_low, w_out, preferred_element_type=jnp.float32)
    after = source + scale_one * branch
    normed_two, norm_two_pull = jax.vjp(layer_norm, after, gain_two, bias_two)
    normed_two_low = normed_two.astype(low_type)
    hidden = jnp.dot(normed_two_low, w_up, preferred_element_type=jnp.float32)
    active, gelu_pull = jax.vjp(gelu_exact, hidden)
    active_low = active.astype(low_type)
    branch_two = jnp.dot(active_low, w_down, preferred_element_type=jnp.float32)
    result = (after + scale_two * branch_two).astype(low_type)
    again = (
        lax.all_gather(qkv_weight.astype(low_type), "tm", axis=1, tiled=True),
        lax.all_gather(out_weight.astype(low_type), "tm", axis=1, tiled=True),
        lax.all_gather(up_weight.astype(low_type), "tm", axis=1, tiled=True),
        lax.all_gather(down_weight.astype(low_type), "tm", axis=1, tiled=True),
    )
    back_qkv, back_out, back_up, back_down = (
        lax.all_gather(again[0], "rows", axis=0, tiled=True),
        lax.all_gather(again[1], "rows", axis=0, tiled=True),
        lax.all_gather(again[2], "rows", axis=0, tiled=True),
        lax.all_gather(again[3], "rows", axis=0, tiled=True),
    )
    upstream = cotangent[0].astype(jnp.float32)
    grad_scale_two = jnp.sum(upstream * branch_two, axis=0)
    grad_branch_two = (upstream * scale_two).astype(low_type)
    grad_down = outer_sum(active_low, grad_branch_two)
    grad_active = lax.dot_general(
        grad_branch_two, back_down, (((1,), (1,)), ((), ())), preferred_element_type=jnp.float32
    )
    grad_hidden = gelu_pull(grad_active)[0].astype(low_type)
    grad_up = outer_sum(normed_two_low, grad_hidden)
    grad_normed_two = lax.dot_general(
        grad_hidden, back_up, (((1,), (1,)), ((), ())), preferred_element_type=jnp.float32
    )
    after_part, grad_gain_two, grad_bias_two = norm_two_pull(grad_normed_two)
    grad_after = upstream + after_part
    grad_scale_one = jnp.sum(grad_after * branch, axis=0)
    grad_branch = (grad_after * scale_one).astype(low_type)
    grad_out = outer_sum(mixed_low, grad_branch)
    grad_mixed = lax.dot_general(
        grad_branch, back_out, (((1,), (1,)), ((), ())), preferred_element_type=jnp.float32
    )
    grad_mixed = grad_mixed.astype(low_type).reshape(frames, H, HD)
    factor = 1.0 / math.sqrt(HD)
    grad_keys_ext = jnp.zeros((REACH + frames, H, HD), jnp.float32)
    grad_values_ext = jnp.zeros((REACH + frames, H, HD), jnp.float32)
    query_grads = []
    for block in range(block_count):
        begin = block * QBLOCK
        allowed = block_allowed(begin, segment, extended_segments, valid_keys)
        query_block = queries[begin : begin + QBLOCK]
        key_window = extended_keys[begin : begin + QBLOCK + REACH]
        value_window = extended_values[begin : begin + QBLOCK + REACH]
        scores = block_scores(query_block, key_window, allowed)
        probs_full = jnp.exp(scores - log_sums[block])
        probs_low = probs_full.astype(low_type)
        grad_out_block = grad_mixed[begin : begin + QBLOCK]
        grad_probs = jnp.einsum(
            "qhd,khd->hqk", grad_out_block, value_window, preferred_element_type=jnp.float32
        )
        grad_values_ext = grad_values_ext.at[begin : begin + QBLOCK + REACH].add(
            jnp.einsum(
                "hqk,qhd->khd", probs_low, grad_out_block, preferred_element_type=jnp.float32
            )
        )
        balance = jnp.sum(grad_probs * probs_full, axis=-1, keepdims=True)
        grad_scores = (probs_full * (grad_probs - balance)).astype(low_type)
        query_grads.append(
            jnp.einsum("hqk,khd->qhd", grad_scores, key_window, preferred_element_type=jnp.float32)
            * factor
        )
        grad_keys_ext = grad_keys_ext.at[begin : begin + QBLOCK + REACH].add(
            jnp.einsum("hqk,qhd->khd", grad_scores, query_block, preferred_element_type=jnp.float32)
            * factor
        )
    grad_keys_flat = grad_keys_ext.reshape(REACH + frames, width)
    grad_values_flat = grad_values_ext.reshape(REACH + frames, width)
    back_keys, back_values = (
        shifted(grad_keys_flat[:REACH].astype(jnp.bfloat16), "tm", -1).astype(jnp.float32),
        shifted(grad_values_flat[:REACH].astype(jnp.bfloat16), "tm", -1).astype(jnp.float32),
    )
    own_keys = grad_keys_flat[REACH:]
    own_values = grad_values_flat[REACH:]
    own_keys = jnp.concatenate(
        [own_keys[: frames - REACH], own_keys[frames - REACH :] + back_keys], axis=0
    )
    own_values = jnp.concatenate(
        [own_values[: frames - REACH], own_values[frames - REACH :] + back_values], axis=0
    )
    grad_queries = rotate(jnp.concatenate(query_grads, axis=0), cosine, -sine).reshape(
        frames, width
    )
    grad_keys = rotate(own_keys.reshape(frames, H, HD), cosine, -sine).reshape(frames, width)
    grad_projected = jnp.concatenate([grad_queries, grad_keys, own_values], axis=1).astype(low_type)
    grad_qkv = outer_sum(normed_one_low, grad_projected)
    grad_normed_one = lax.dot_general(
        grad_projected, back_qkv, (((1,), (1,)), ((), ())), preferred_element_type=jnp.float32
    )
    source_part, grad_gain_one, grad_bias_one = norm_one_pull(grad_normed_one)
    input_grad = (grad_after + source_part).astype(low_type)
    reduced = (
        lax.psum_scatter(grad_qkv, "tm", scatter_dimension=1, tiled=True),
        lax.psum_scatter(grad_out, "tm", scatter_dimension=1, tiled=True),
        lax.psum_scatter(grad_up, "tm", scatter_dimension=1, tiled=True),
        lax.psum_scatter(grad_down, "tm", scatter_dimension=1, tiled=True),
        lax.psum_scatter(grad_gain_one, "tm", scatter_dimension=0, tiled=True),
        lax.psum_scatter(grad_bias_one, "tm", scatter_dimension=0, tiled=True),
        lax.psum_scatter(grad_scale_one, "tm", scatter_dimension=0, tiled=True),
        lax.psum_scatter(grad_gain_two, "tm", scatter_dimension=0, tiled=True),
        lax.psum_scatter(grad_bias_two, "tm", scatter_dimension=0, tiled=True),
        lax.psum_scatter(grad_scale_two, "tm", scatter_dimension=0, tiled=True),
    )
    qkv_grad, out_grad, up_grad, down_grad = (
        lax.psum_scatter(reduced[0], "rows", scatter_dimension=0, tiled=True),
        lax.psum_scatter(reduced[1], "rows", scatter_dimension=0, tiled=True),
        lax.psum_scatter(reduced[2], "rows", scatter_dimension=0, tiled=True),
        lax.psum_scatter(reduced[3], "rows", scatter_dimension=0, tiled=True),
    )
    vector_sums = lax.psum(
        (reduced[4], reduced[5], reduced[6], reduced[7], reduced[8], reduced[9]), "rows"
    )
    return (
        result[None],
        input_grad[None],
        qkv_grad,
        out_grad,
        up_grad,
        down_grad,
        vector_sums[0],
        vector_sums[1],
        vector_sums[2],
        vector_sums[3],
        vector_sums[4],
        vector_sums[5],
    )


MESH_IDS = pl.DeviceIdType.MESH
F32 = jnp.float32
BF16 = jnp.bfloat16


def dot(left, right, contract=((1,), (0,))):
    return lax.dot_general(left, right, (contract, ((), ())), preferred_element_type=F32)


def dot_t(left, right):
    return dot(left, right, ((1,), (1,)))


def start_of(index, size):
    return pl.ds(pl.multiple_of(index * size, size), size)


def coordinates():
    row, core = lax.axis_index("rows"), lax.axis_index("tm")
    return row, core, lax.rem(row, 2), lax.rem(lax.div(row, 2), 2), lax.div(row, 4)


def peers_of(at):
    row, core, x, y, z = at
    found = {
        "x": (row + 1 - 2 * x, core),
        "y": (row + 2 - 4 * y, core),
        "s": (row, 1 - core),
    }
    for k in (1, 2, 3):
        found[k] = (lax.rem(z + k, 4) * 4 + lax.rem(row, 4), core)
    return found


def enter(peers):
    barrier = pltpu.get_barrier_semaphore()
    for peer in peers.values():
        pl.semaphore_signal(barrier, inc=1, device_id=peer, device_id_type=MESH_IDS)
    pl.semaphore_wait(barrier, len(peers))


class Links:
    def __init__(self, sems, peers):
        self.sems, self.peers, self.used = sems, peers, 0

    def slot(self):
        self.used += 1
        return self.sems.at[self.used - 1]

    def copy(self, src, dst, peer, send, recv):
        return pltpu.make_async_remote_copy(
            src_ref=src,
            dst_ref=dst,
            send_sem=send,
            recv_sem=recv,
            device_id=self.peers[peer],
            device_id_type=MESH_IDS,
        )

    def single(self, src, dst, peer):
        return self.copy(src, dst, peer, self.slot(), self.slot())


def await_bytes(like, sem):
    pltpu.make_async_copy(like, like, sem).wait()


class Gather:
    def __init__(self, units, i, links, at):
        full = units.at[i]
        row, core, x, y, z = at
        half = full.shape[4] // 2
        low, high = pl.ds(0, half), pl.ds(half, half)
        every = slice(None)
        near, far = links.slot(), links.slot()
        got = [links.slot() for _ in range(4)]

        def copy(where, peer, send, recv):
            return links.copy(full.at[where], full.at[where], peer, send, recv)

        self.starts = (
            [copy((core, z, y, x), k, near, got[0]) for k in (1, 2, 3)],
            [
                copy((core, every, y, x, low), "x", far, got[1]),
                copy((core, every, y, x, high), "y", far, got[1]),
                copy((core, every, y, x), "s", far, got[3]),
            ],
            [
                copy((core, every, y, every, low), "y", far, got[2]),
                copy((core, every, every, x, high), "x", far, got[2]),
                copy((core, every, y, 1 - x, low), "s", far, got[3]),
                copy((core, every, 1 - y, x, high), "s", far, got[3]),
            ],
            [
                copy((core, every, 1 - y, every, low), "s", far, got[3]),
                copy((core, every, every, 1 - x, high), "s", far, got[3]),
            ],
            [],
        )
        self.waits = (
            None,
            (full.at[core, 0:3, y, x], got[0]),
            (full.at[core, :, y, x], got[1]),
            (full.at[core, :, y], got[2]),
            (full.at[1 - core], got[3]),
        )
        self.sent = ((full.at[core, 0:3, y, x], near), (units.at[0:7, 0, 0], far))

    def step(self, number):
        if number > 0:
            await_bytes(*self.waits[number])
        for copy in self.starts[number]:
            copy.start()

    def drain(self):
        for like, sem in self.sent:
            await_bytes(like, sem)


class Scatter:
    def __init__(self, own, out, arrived, result, links, at, units):
        self.own, self.out, self.result, self.at = own, out, result, at
        self.s_in, self.c_in, self.b_in, self.a_in = arrived
        row, core, x, y, z = at
        self.rows = out.shape[3]
        half = self.half = self.rows // 2
        low, high = self.low, self.high = pl.ds(0, half), pl.ds(half, half)
        every = slice(None)
        self.d = links.single(out, self.s_in, "s")
        self.far = links.slot()
        self.got = [links.slot() for _ in range(3)]
        self.units = units

        def copy(src, dst, peer, which):
            return links.copy(src, dst, peer, self.far, self.got[which])

        self.c1 = copy(out.at[every, 1 - y, every, low], self.c_in.at[0], "y", 0)
        self.c2 = copy(out.at[every, every, 1 - x, high], self.c_in.at[1], "x", 0)
        self.b1 = copy(out.at[every, y, 1 - x, low], self.b_in.at[0], "x", 1)
        self.b2 = copy(out.at[every, 1 - y, x, high], self.b_in.at[1], "y", 1)
        self.a = [
            copy(out.at[lax.rem(z + k, 4), y, x], self.a_in.at[k - 1], k, 2) for k in (1, 2, 3)
        ]

    def mine(self, k, y, x, part):
        begin = ((k * 2 + y) * 2 + x) * self.rows + part * self.half
        return self.own[pl.ds(pl.multiple_of(begin, self.half), self.half), :] + self.s_in[
            k, y, x, pl.ds(part * self.half, self.half)
        ].astype(F32)

    def column(self, k, part):
        row, core, x, y, z = self.at
        place = x if part == 0 else y
        return (
            self.mine(k, y, x, part)
            + self.c_in[part, k, place].astype(F32)
            + self.b_in[part, k].astype(F32)
        )

    def step(self, number):
        row, core, x, y, z = self.at
        low, high, out = self.low, self.high, self.out
        c_in = self.c_in
        if number == 0:
            self.d.start()
        if number == 1:
            self.d.wait()
            for k in range(4):
                for i in range(2):
                    out[k, 1 - y, i, low] = self.mine(k, 1 - y, i, 0).astype(BF16)
            self.c1.start()
            for k in range(4):
                for i in range(2):
                    out[k, i, 1 - x, high] = self.mine(k, i, 1 - x, 1).astype(BF16)
            self.c2.start()
        if number == 2:
            await_bytes(c_in, self.got[0])
            for k in range(4):
                out[k, y, 1 - x, low] = (
                    self.mine(k, y, 1 - x, 0) + c_in[0, k, 1 - x].astype(F32)
                ).astype(BF16)
            self.b1.start()
            for k in range(4):
                out[k, 1 - y, x, high] = (
                    self.mine(k, 1 - y, x, 1) + c_in[1, k, 1 - y].astype(F32)
                ).astype(BF16)
            self.b2.start()
        if number == 3:
            await_bytes(self.b_in, self.got[1])
            for k in (1, 2, 3):
                there = lax.rem(z + k, 4)
                out[there, y, x, low] = self.column(there, 0).astype(BF16)
                out[there, y, x, high] = self.column(there, 1).astype(BF16)
                self.a[k - 1].start()
            self.own[low, :] = self.column(z, 0)
            self.own[high, :] = self.column(z, 1)
        if number == 4:
            await_bytes(self.a_in, self.got[2])
            self.result(
                self.own[: self.rows, :]
                + (self.a_in[0].astype(F32) + self.a_in[1].astype(F32) + self.a_in[2].astype(F32))
            )

    def drain(self):
        await_bytes(self.units.at[0:5, 0:3, 0, 0], self.far)


def gelu_and_slope(values):
    cdf = 0.5 + 0.5 * lax.erf(values * math.sqrt(0.5))
    bell = jnp.exp2((values * values) * (-0.5 * math.log2(math.e)))
    return values * cdf, cdf + (values * (1.0 / math.sqrt(2.0 * math.pi))) * bell


def lane_pattern(shape, size):
    return lax.rem(lax.broadcasted_iota(jnp.int32, shape, len(shape) - 1), size)


def turned(values, cosine, sine):
    first = lane_pattern(values.shape, HD) < HD // 2
    swapped = jnp.where(first, pltpu.roll(values, 96, 1), pltpu.roll(values, 32, 1))
    return values * cosine + swapped * sine


TILE = 256
BLOCK = 128
SPAN = BLOCK + REACH
PAIRS = H // 2
COLUMNS = 256
UNITS = 12
GROUP, OUT, DOWN, UP = 0, 3, (4, 6, 8, 10), (5, 7, 9, 11)
OFFSETS = (0, 2, 4, 6, 7)
CHUNKS = (
    (((0, 0), (1, 0)), ((2, 0), (2, 1))),
    (((0, 1), (1, 1)), ((2, 2), (1, 2))),
    (((0, 2), (0, 3)), ((2, 3), (1, 3))),
)


def place_of(kind, p):
    for g, cores in enumerate(CHUNKS):
        for c, pair in enumerate(cores):
            if (kind, p) in pair:
                return g, c, pair.index((kind, p))


def run(begin, end, body, events=None):
    def with_events(i, carried):
        for when, actions in sorted((events or {}).items()):

            @pl.when(i == when)
            def _(actions=actions):
                for action in actions:
                    action()

        body(i, carried)
        return 0

    lax.fori_loop(begin, end, with_events, 0)


def in_turn(count, stages, events):
    for i in range(count + len(stages) - 1):
        for action in events.get(i, []):
            action()
        for late, stage in enumerate(stages):
            if 0 <= i - late < count:
                stage(i - late)


def regroup(tiles, quarter, back=False):
    group = lax.broadcasted_iota(jnp.int32, (1, 128), 1) // 32
    out = jnp.zeros_like(tiles[0])
    for a in range(4):
        out = jnp.where(group == a, pltpu.roll(tiles[a], (a - quarter) * 32 % 128, 1), out)
    return out


def scratch_list(frames, width):
    blocks = frames // BLOCK
    ext = REACH + frames
    unit = (4, 2, 2, width // 16, COLUMNS)
    half = width // 32
    return [
        ("w", (UNITS, 2) + unit, BF16),
        ("vecs", (2, 8, width // 2), F32),
        ("segs", (2, 8, frames), F32),
        ("n1t", (width, frames), BF16),
        ("cos", (frames, 128), F32),
        ("sin", (frames, 128), F32),
        ("bias", (blocks, SPAN, BLOCK), BF16),
        ("qx", (PAIRS, frames, 128), BF16),
        ("kx", (PAIRS, ext, 128), BF16),
        ("vx", (PAIRS, ext, 128), BF16),
        ("kt", (PAIRS, 128, ext), BF16),
        ("vt", (PAIRS, 128, ext), BF16),
        ("probs", (PAIRS, blocks, SPAN, 2 * BLOCK), BF16),
        ("ot", (width, frames), BF16),
        ("n2t", (width, frames), BF16),
        ("actt", (2 * COLUMNS, frames), BF16),
        ("du", (2, frames, COLUMNS), BF16),
        ("after", (frames, width), F32),
        ("branch", (frames, width), BF16),
        ("branch_two", (frames, width), F32),
        ("dx1", (frames, width), F32),
        ("dba", (2, frames, width // 2), BF16),
        ("dox", (PAIRS, frames, 128), BF16),
        ("dp", (3, 2, frames, COLUMNS), BF16),
        ("dkx", (ext, 128), F32),
        ("dvx", (ext, 128), F32),
        ("h_out", (PAIRS, 2, REACH, 128), BF16),
        ("h_in", (PAIRS, 2, REACH, 128), BF16),
        ("acc", (8, width), F32),
        ("v_out", (3, 8, width // 2), F32),
        ("v_in", (3, 8, width // 2), F32),
        ("v_z", (4, 8, width // 2), F32),
        ("own", (UNITS - 3, width, COLUMNS), F32),
        ("up_sums", (4, width // 16, COLUMNS), F32),
        ("s_in", (UNITS,) + unit, BF16),
        ("c_in", (UNITS, 2, 4, 2, half, COLUMNS), BF16),
        ("b_in", (UNITS, 2, 4, half, COLUMNS), BF16),
        ("a_in", (UNITS, 3, width // 16, COLUMNS), BF16),
    ]


SLOTS = 12 * UNITS + 2 * (2 + 2 * PAIRS + PAIRS + 3) + 4


def layer_kernel(names, *refs):
    x_ref, dy_ref, seg_ref = refs[:3]
    wq_shard, wo_shard, wu_shard, wd_shard = refs[3:7]
    vectors = refs[7:13]
    y_ref, ig_ref, gq, go, gu, gd, gv = refs[13:20]
    m = dict(zip(names, refs[20:-1]))
    at = coordinates()
    row, core, x, y, z = at
    peers = peers_of(at)
    links = Links(refs[-1], peers)
    frames, width = x_ref.shape[1:]
    piece = width // 16
    blocks, tiles = frames // BLOCK, frames // TILE
    factor = 1.0 / math.sqrt(HD)
    w = m["w"]
    other = 1 - core

    def chunk_columns(g, j):
        offsets = []
        for c in range(2):
            kind, p = CHUNKS[g][c][j]
            offsets.append((kind * PAIRS + p - 6 * c) * 128)
        begin = offsets[0] + core * (offsets[1] - offsets[0])
        return pl.ds(pl.multiple_of(begin, 128), 128)

    for g in range(3):
        for j in range(2):
            w[g, core, z, y, x, :, j * 128 : (j + 1) * 128] = wq_shard[
                :, chunk_columns(g, j)
            ].astype(BF16)
    m["vecs"][core] = jnp.concatenate(
        [v[...].astype(BF16).astype(F32) for v in vectors]
        + [jnp.zeros((2, width // 2), F32)],
        axis=0,
    )
    m["segs"][core] = jnp.broadcast_to(seg_ref[...].astype(F32), (8, frames))
    enter(peers)
    vec_copy = links.single(m["vecs"].at[core], m["vecs"].at[core], "s")
    seg_copy = links.single(m["segs"].at[core], m["segs"].at[core], "s")
    gathers = [Gather(w, i, links, at) for i in range(UNITS)]

    def tick(k):
        for step in (4, 3, 2, 1, 0):
            if 0 <= k - OFFSETS[step] < UNITS:
                gathers[k - OFFSETS[step]].step(step)

    vec_copy.start()
    seg_copy.start()
    tick(0)
    w[OUT, core, z, y, x] = wo_shard[...].astype(BF16)
    for q in range(4):
        w[DOWN[q], core, z, y, x] = wd_shard[q * piece : (q + 1) * piece, :].astype(BF16)
    for q in range(4):
        for j in range(2):
            made = regroup(
                [wu_shard[:, (4 * j + a) * 128 : (4 * j + a + 1) * 128] for a in range(4)], q
            )
            w[UP[q], core, z, y, x, :, j * 128 : (j + 1) * 128] = made.astype(BF16)

    def vector(i):
        return jnp.concatenate([m["vecs"][0, i : i + 1, :], m["vecs"][1, i : i + 1, :]], axis=1)

    def normalized(values):
        average = jnp.mean(values, axis=-1, keepdims=True)
        centred = values - average
        variance = jnp.mean(centred * centred, axis=-1, keepdims=True)
        scale = lax.rsqrt(variance + EPSILON)
        return centred * scale, scale

    vec_copy.wait_recv()
    n1 = y_ref
    gain_one, bias_one = vector(0), vector(1)

    def norm_one(t, _):
        rows = start_of(t, TILE)
        unit, _scale = normalized(x_ref[0, rows, :].astype(F32))
        low = (unit * gain_one + bias_one).astype(BF16)
        n1[0, rows, :] = low
        m["n1t"][:, rows] = low.T

    tick(1)
    run(0, tiles, norm_one)
    tick(2)

    seg_copy.wait_recv()
    segs = m["segs"]

    def spread(which, begin):
        line = segs[which, 0:1, pl.ds(pl.multiple_of(begin, BLOCK), BLOCK)]
        return jnp.broadcast_to(line, (BLOCK, BLOCK)).T

    seg_blocks = m["own"]

    def seg_place(e):
        return (e // 8, pl.ds((e % 8) // 2 * BLOCK, BLOCK), pl.ds(e % 2 * BLOCK, BLOCK))

    for e in range(REACH // BLOCK):
        halo = spread(other, frames - REACH + e * BLOCK)
        seg_blocks[seg_place(e)] = jnp.where(core > 0, halo, -1.0)

    lanes = lane_pattern((1, 128), HD // 2).astype(F32)
    frequency = jnp.exp(lanes * (-2.0 * math.log(10000.0) / HD))
    first_half = lane_pattern((BLOCK, 128), HD) < HD // 2

    def tables(b, _):
        rows = start_of(b, BLOCK)
        here = spread(core, b * BLOCK)
        count = jnp.zeros((BLOCK, BLOCK), F32)
        for which in range(2):
            for k in range(blocks):
                line = segs[which, 0:1, k * BLOCK : (k + 1) * BLOCK]
                count = count + jnp.where(line < here, 1.0, 0.0)
        began = jnp.sum(count, axis=1, keepdims=True)
        frame = lax.broadcasted_iota(jnp.int32, (BLOCK, 1), 0) + (core * frames + b * BLOCK)
        angle = (frame.astype(F32) - began) * frequency
        m["cos"][rows, :] = jnp.cos(angle)
        sine = jnp.sin(angle)
        m["sin"][rows, :] = jnp.where(first_half, -sine, sine)

    run(0, blocks, tables, {blocks // 2: [lambda: tick(3)]})
    tick(4)

    for b in range(blocks):
        seg_blocks[seg_place(REACH // BLOCK + b)] = spread(core, b * BLOCK)
    distance = (
        lax.broadcasted_iota(jnp.int32, (SPAN, BLOCK), 1)
        - lax.broadcasted_iota(jnp.int32, (SPAN, BLOCK), 0)
        + REACH
    )
    near = (distance >= 0) & (distance < WINDOW)
    for b in range(blocks):
        keys = jnp.concatenate([seg_blocks[seg_place(b + i)] for i in range(SPAN // BLOCK)], axis=0)
        line = segs[core, 0:1, b * BLOCK : (b + 1) * BLOCK]
        m["bias"][b] = jnp.where(near & (keys == line), 0.0, NEGATIVE).astype(BF16)
    for k in (5, 6, 7):
        tick(k)

    low_lanes = lane_pattern((1, 128), 128) < HD

    def two_heads(value):
        zero = jnp.zeros_like(value)
        return jnp.concatenate(
            [jnp.where(low_lanes, value, zero), jnp.where(low_lanes, zero, value)], axis=0
        )

    def projection(g):
        def project(t, _):
            rows = start_of(t, TILE)
            placed = pl.ds(pl.multiple_of(REACH + t * TILE, TILE), TILE)
            left = n1[0, rows, :]
            cosine, sine = m["cos"][rows, :], m["sin"][rows, :]
            for c in range(2):
                wide = dot(left, w[g, c].reshape(width, COLUMNS))
                for j in range(2):
                    chunk = wide[:, j * 128 : (j + 1) * 128]
                    kind, p = CHUNKS[g][c][j]
                    if kind == 0:
                        turn = turned(chunk, cosine, sine).astype(BF16)
                        m["qx"][p, rows, :] = (turn * factor).astype(BF16)
                    elif kind == 1:
                        value = turned(chunk, cosine, sine).astype(BF16)
                        m["kx"][p, placed, :] = value
                        m["kt"][p, :, placed] = value.T
                    else:
                        value = chunk.astype(BF16)
                        m["vx"][p, placed, :] = value
                        m["vt"][p, :, placed] = value.T

        return project

    tail, head = pl.ds(frames, REACH), pl.ds(0, REACH)
    mixed = ig_ref

    def heads_joined(both):
        return jnp.concatenate([both[:HD, :BLOCK], both[HD:, BLOCK:]], axis=0)

    unit_rows = lax.broadcasted_iota(jnp.int32, (2 * BLOCK, BLOCK), 0)
    unit_lanes = lax.broadcasted_iota(jnp.int32, (2 * BLOCK, BLOCK), 1)
    picks = (lax.rem(unit_rows, BLOCK) == unit_lanes).astype(F32).astype(BF16)

    def block_rows(b):
        return pl.ds(b * BLOCK, BLOCK)

    def block_window(b):
        return pl.ds(b * BLOCK, SPAN)

    def spare(i):
        return m["after"].at[pl.ds(i // 2 * SPAN, SPAN), pl.ds(i % 2 * 2 * BLOCK, 2 * BLOCK)]

    def spare_low(i):
        return m["branch"].at[pl.ds(i // 2 * SPAN, SPAN), pl.ds(i % 2 * 2 * BLOCK, 2 * BLOCK)]

    def attend(p, events):
        def score(b):
            left = jnp.concatenate([m["kx"][p, block_window(b), :], m["bias"][b]], axis=1)
            right = jnp.concatenate([two_heads(m["qx"][p, block_rows(b), :]), picks], axis=1)
            spare(b % 4)[...] = dot_t(left, right)

        def soften(b):
            scores = spare(b % 4)[...]
            top = jnp.max(scores, axis=0, keepdims=True)
            weights = jnp.exp(scores - top)
            total = jnp.sum(weights, axis=0, keepdims=True)
            m["probs"][p, b] = (weights * (1.0 / total)).astype(BF16)

        def mix(b):
            joined = heads_joined(dot(m["vt"][p, :, block_window(b)], m["probs"][p, b]))
            m["ot"][p * 128 : (p + 1) * 128, block_rows(b)] = joined.astype(BF16)
            mixed[0, block_rows(b), p * 128 : (p + 1) * 128] = joined.T.astype(BF16)

        in_turn(blocks, (score, soften, mix), events)

    halos = {}

    def send_halo(kind, p):
        ref = m["kx"] if kind == 1 else m["vx"]
        halos[kind, p] = links.single(ref.at[p, tail], ref.at[p, head], "s")
        halos[kind, p].start()

    def take_halo(p):
        for kind, flat, turned_ref in ((1, m["kx"], m["kt"]), (2, m["vx"], m["vt"])):
            halos[kind, p].wait_recv()
            turned_ref[p, :, 0:REACH] = flat[p, 0:REACH, :].T

    for p in range(PAIRS):
        if p < 3:
            run(0, tiles, projection(p))
            for pair in CHUNKS[p]:
                for kind, q in pair:
                    if kind > 0:
                        send_halo(kind, q)
        take_halo(p)
        due = {
            2: [functools.partial(tick, 8 + 2 * p)],
            6: [functools.partial(tick, 9 + 2 * p)],
        }
        attend(p, due)

    m["acc"][...] = jnp.zeros_like(m["acc"])
    acc = m["acc"]

    def add_to(i, values):
        acc[i : i + 1, :] = acc[i : i + 1, :] + jnp.sum(values, axis=0, keepdims=True)

    scale_one, gain_two, bias_two, scale_two = vector(2), vector(3), vector(4), vector(5)
    n2 = y_ref
    dba = m["dba"]

    def norm_back(unit, scale, gain, grad):
        inner = grad * gain
        return scale * (
            inner
            - jnp.mean(inner, axis=-1, keepdims=True)
            - unit * jnp.mean(inner * unit, axis=-1, keepdims=True)
        )

    def norm_two(t, _):
        rows = start_of(t, TILE)
        both = mixed[0, rows, :]
        branch = jnp.concatenate(
            [dot(both, w[OUT, c].reshape(width, COLUMNS)) for c in range(2)], axis=1
        )
        m["branch"][rows, :] = branch.astype(BF16)
        after = x_ref[0, rows, :].astype(F32) + scale_one * branch
        m["after"][rows, :] = after
        unit, _scale = normalized(after)
        low = (unit * gain_two + bias_two).astype(BF16)
        n2[0, rows, :] = low
        m["n2t"][:, rows] = low.T
        dbm = (dy_ref[0, rows, :].astype(F32) * scale_two).astype(BF16)
        dba[0, rows, :] = dbm[:, : width // 2]
        dba[1, rows, :] = dbm[:, width // 2 :]

    run(0, tiles, norm_two)

    def result_of(i):
        def keep(value):
            if i < OUT:
                for j in range(2):
                    gq[:, chunk_columns(i, j)] = value[:, j * 128 : (j + 1) * 128]
            elif i == OUT:
                go[...] = value
            elif i in DOWN:
                q = DOWN.index(i)
                gd[q * piece : (q + 1) * piece, :] = value
            else:
                m["up_sums"][UP.index(i)] = value

        return keep

    sums = {}

    def unit_grads(i, left, right):
        gathers[i].drain()
        if i < OUT:
            sums[DOWN[i]].drain()
        place = DOWN[i] if i < OUT else i
        out, own = w.at[place, 0], m["own"].at[place - 3]
        arrived = [m[name].at[i] for name in ("s_in", "c_in", "b_in", "a_in")]
        sums[i] = Scatter(own, out, arrived, result_of(i), links, at, m["s_in"])
        own[...] = dot(left[...], right[core])
        out[...] = dot(left[...], right[other]).astype(BF16).reshape(4, 2, 2, piece, COLUMNS)
        sums[i].step(0)

    def step_of(i, number):
        return lambda: sums[i].step(number)

    def feed(q):
        def middle(t, _):
            rows = start_of(t, TILE)
            ups = [w[UP[q], h].reshape(width, COLUMNS) for h in range(2)]
            dbm = jnp.concatenate([dba[c, rows, :] for c in range(2)], axis=1)
            acts, dus = [], []
            for h in range(2):
                value, slope = gelu_and_slope(dot(n2[0, rows, :], ups[h]))
                act = value.astype(BF16)
                m["actt"][h * COLUMNS : (h + 1) * COLUMNS, rows] = act.T
                down = jnp.concatenate(
                    [w[DOWN[q], c, 2 * h : 2 * h + 2].reshape(COLUMNS, COLUMNS) for c in range(2)],
                    axis=1,
                )
                du = (dot_t(dbm, down) * slope).astype(BF16)
                m["du"][h, rows, :] = du
                acts.append(act)
                dus.append(du)
            act = jnp.concatenate(acts, axis=1)
            for c in range(2):
                columns = pl.ds(c * COLUMNS, COLUMNS)
                total = dot(act, w[DOWN[q], c].reshape(2 * COLUMNS, COLUMNS))
                if q > 0:
                    total = total + m["branch_two"][rows, columns]
                m["branch_two"][rows, columns] = total
            grad = dot_t(jnp.concatenate(dus, axis=1), jnp.concatenate(ups, axis=1))
            if q > 0:
                grad = grad + m["dx1"][rows, :]
            m["dx1"][rows, :] = grad

        return middle

    def steps_of(q, number):
        return [step_of(DOWN[q], number), step_of(UP[q], number)]

    def do(actions):
        for action in actions:
            action()

    for q in range(4):
        events = {i: [] for i in range(tiles)}
        if q == 0:
            events[1] += [functools.partial(tick, 16)]
            events[3] += [functools.partial(tick, 17)]
        if q == 1:
            events[2] += [functools.partial(tick, 18)]
        if q > 0:
            events[1] += steps_of(q - 1, 1)
        if q > 1:
            events[0] += steps_of(q - 2, 2)
        if q > 2:
            events[2] += steps_of(q - 3, 4)
        run(0, tiles, feed(q), events)
        if q > 1:
            do(steps_of(q - 2, 3))
        unit_grads(DOWN[q], m["actt"], dba)
        unit_grads(UP[q], m["n2t"], m["du"])

    def norm_two_back(t, _):
        rows = start_of(t, TILE)
        after, branch_two = m["after"][rows, :], m["branch_two"][rows, :]
        y_ref[0, rows, :] = (after + scale_two * branch_two).astype(BF16)
        upstream = dy_ref[0, rows, :].astype(F32)
        add_to(5, upstream * branch_two)
        unit, scale = normalized(after)
        grad = m["dx1"][rows, :]
        add_to(3, grad * unit)
        add_to(4, grad)
        dx1 = upstream + norm_back(unit, scale, gain_two, grad)
        m["dx1"][rows, :] = dx1
        add_to(2, dx1 * m["branch"][rows, :].astype(F32))
        low = (dx1 * scale_one).astype(BF16)
        sides = [low[:, : width // 2], low[:, width // 2 :]]
        for c in range(2):
            dba[c, rows, :] = sides[c]
        dmixed = (
            dot_t(sides[0], w[OUT, 0].reshape(width, COLUMNS))
            + dot_t(sides[1], w[OUT, 1].reshape(width, COLUMNS))
        ).astype(BF16)
        m["n2t"][:, rows] = dmixed.T
        for p in range(PAIRS):
            m["dox"][p, rows, :] = dmixed[:, p * 128 : (p + 1) * 128]

    run(
        0,
        tiles,
        norm_two_back,
        {0: steps_of(2, 2), 1: steps_of(3, 1)},
    )
    unit_grads(OUT, m["ot"], dba)

    dp = m["dp"]
    plan = [
        {2: steps_of(2, 3) + [step_of(OUT, 1)], 4: steps_of(3, 2) + steps_of(1, 4)},
        {2: [step_of(OUT, 2)], 4: steps_of(3, 3), 6: steps_of(2, 4), 7: [step_of(OUT, 3)]},
        {2: [step_of(GROUP, 1)], 4: steps_of(3, 4), 6: [step_of(OUT, 4)]},
        {0: [step_of(GROUP, 2)], 2: [step_of(GROUP + 1, 1)], 5: [step_of(GROUP, 3)]},
    ]

    def store_turned(kind, p, rows, value):
        g, c, j = place_of(kind, p)
        if kind < 2:
            value = turned(value, m["cos"][rows, :], -m["sin"][rows, :])
        dp[g, c, rows, j * 128 : (j + 1) * 128] = value.astype(BF16)

    backs = []
    for p in range(PAIRS):
        dkx, dvx = m["dkx"], m["dvx"]
        dkx[...] = jnp.zeros_like(dkx)
        dvx[...] = jnp.zeros_like(dvx)

        def probe(b, p=p):
            spare(b % 4)[...] = dot_t(
                m["vx"][p, block_window(b), :], two_heads(m["dox"][p, block_rows(b), :])
            )

        def weigh(b, p=p):
            probs = m["probs"][p, b].astype(F32)
            heads = (pl.ds(p * 128, 128), block_rows(b))
            shared = m["n2t"][heads].astype(F32) * m["ot"][heads].astype(F32)
            balance = jnp.concatenate(
                [
                    jnp.sum(shared[:HD], axis=0, keepdims=True),
                    jnp.sum(shared[HD:], axis=0, keepdims=True),
                ],
                axis=1,
            )
            spare_low(b % 4)[...] = (probs * (spare(b % 4)[...] - balance)).astype(BF16)

        def gather_back(b, p=p):
            window, rows = block_window(b), block_rows(b)
            dscores = spare_low(b % 4)[...]
            dvx[window, :] = dvx[window, :] + dot(
                m["probs"][p, b], two_heads(m["dox"][p, rows, :])
            )
            dkx[window, :] = dkx[window, :] + dot(dscores, two_heads(m["qx"][p, rows, :]))
            joined = heads_joined(dot(m["kt"][p, :, window], dscores)).T * factor
            store_turned(0, p, rows, joined)

        h_out, h_in = m["h_out"], m["h_in"]
        halo_back = links.single(h_out.at[p], h_in.at[p], "s")
        backs.append(halo_back)

        def send_back(p=p, halo_back=halo_back):
            h_out[p, 0] = dkx[0:REACH, :].astype(BF16)
            h_out[p, 1] = dvx[0:REACH, :].astype(BF16)
            halo_back.start()

        events = dict(plan[p])
        events[4] = [send_back] + events.get(4, [])
        in_turn(blocks, (probe, weigh, gather_back), events)
        halo_back.wait_recv()
        dkx[tail, :] = dkx[tail, :] + h_in[p, 0].astype(F32)
        dvx[tail, :] = dvx[tail, :] + h_in[p, 1].astype(F32)

        def finish(t, _, p=p):
            rows = start_of(t, TILE)
            placed = pl.ds(pl.multiple_of(REACH + t * TILE, TILE), TILE)
            store_turned(1, p, rows, dkx[placed, :])
            store_turned(2, p, rows, dvx[placed, :])

        run(0, tiles, finish)
        if p > 0:
            unit_grads(GROUP + p - 1, m["n1t"], dp.at[p - 1])

    sums[GROUP + 1].step(2)

    def first(t, _):
        rows = start_of(t, TILE)
        sides = [(g, c) for g in range(3) for c in range(2)]
        grad = dot_t(
            jnp.concatenate([dp[g, c, rows, :] for g, c in sides], axis=1),
            jnp.concatenate([w[g, c].reshape(width, COLUMNS) for g, c in sides], axis=1),
        )
        unit, scale = normalized(x_ref[0, rows, :].astype(F32))
        add_to(0, grad * unit)
        add_to(1, grad)
        ig_ref[0, rows, :] = (
            m["dx1"][rows, :] + norm_back(unit, scale, gain_one, grad)
        ).astype(BF16)

    run(
        0,
        tiles,
        first,
        {1: [step_of(GROUP + 2, 1)], 3: [step_of(GROUP, 4)]},
    )

    v_out, v_in, v_z = m["v_out"], m["v_in"], m["v_z"]
    here, there = start_of(core, width // 2), start_of(other, width // 2)
    v_out[0] = acc[:, there]
    hops = [links.single(v_out.at[i], v_in.at[i], peer) for i, peer in enumerate(("s", "y", "x"))]
    hops[0].start()
    hops[0].wait_recv()
    v_out[1] = acc[:, here] + v_in[0]
    hops[1].start()
    sums[GROUP + 2].step(2)
    sums[GROUP + 1].step(3)
    for j in range(2):
        for a in range(4):
            gu[:, (4 * j + a) * 128 : (4 * j + a + 1) * 128] = regroup(
                [m["up_sums"][q, :, j * 128 : (j + 1) * 128] for q in range(4)], a, True
            )
    hops[1].wait_recv()
    v_out[2] = v_out[1] + v_in[1]
    hops[2].start()
    sums[GROUP + 2].step(3)
    hops[2].wait_recv()
    v_z[z] = v_out[2] + v_in[2]
    spread_send, spread_recv = links.slot(), links.slot()
    spreads = [links.copy(v_z.at[z], v_z.at[z], k, spread_send, spread_recv) for k in (1, 2, 3)]
    for each in spreads:
        each.start()
    sums[GROUP + 1].step(4)
    sums[GROUP + 2].step(4)
    await_bytes(v_z.at[0:3], spread_recv)
    gv[...] = (v_z[0] + v_z[1]) + (v_z[2] + v_z[3])
    await_bytes(v_z.at[0:3], spread_send)
    for i, each in sums.items():
        if i not in DOWN[:3]:
            each.drain()
    for each in [vec_copy, seg_copy, *halos.values(), *backs, *hops]:
        each.wait_send()


def write_kernel(*refs):
    for source, target in zip(refs[:6], refs[7:13]):
        target[...] = source[...]
    for i, vector in enumerate(refs[13:]):
        vector[...] = refs[6][i : i + 1, :]


def local_staged(
    inputs,
    cotangent,
    segment_ids,
    qkv_weight,
    out_weight,
    up_weight,
    down_weight,
    *vectors,
):
    frames, width = inputs.shape[1:]
    items = scratch_list(frames, width)
    whole = pl.BlockSpec(memory_space=pltpu.VMEM)
    shapes = [
        jax.ShapeDtypeStruct(inputs.shape, BF16),
        jax.ShapeDtypeStruct(inputs.shape, BF16),
        *[
            jax.ShapeDtypeStruct(weight.shape, F32)
            for weight in (qkv_weight, out_weight, up_weight, down_weight)
        ],
    ]
    results = pl.pallas_call(
        functools.partial(layer_kernel, [name for name, _, _ in items]),
        out_shape=shapes + [jax.ShapeDtypeStruct((8, width // 2), F32)],
        in_specs=[whole] * 13,
        out_specs=[whole] * 7,
        scratch_shapes=[pltpu.VMEM(shape, kind) for _, shape, kind in items]
        + [pltpu.SemaphoreType.DMA((SLOTS,))],
        compiler_params=pltpu.CompilerParams(
            collective_id=0, has_side_effects=True, vmem_limit_bytes=VMEM_LIMIT
        ),
    )(
        inputs,
        cotangent,
        segment_ids,
        qkv_weight,
        out_weight,
        up_weight,
        down_weight,
        *[v.reshape(1, -1) for v in vectors],
    )
    written = pl.pallas_call(
        write_kernel,
        out_shape=shapes + [jax.ShapeDtypeStruct((1, width // 2), F32)] * 6,
        in_specs=[whole] * 7,
        out_specs=[whole] * 12,
    )(*results)
    return (*written[:6], *[v.reshape(-1) for v in written[6:]])


VMEM_LIMIT = 64 * 2**20


def solution(mesh):
    placed = (
        P("rows", "tm", None),
        P("rows", "tm", None),
        P("rows", "tm"),
        P("rows", "tm"),
        P("rows", "tm"),
        P("rows", "tm"),
        P("rows", "tm"),
        P("tm"),
        P("tm"),
        P("tm"),
        P("tm"),
        P("tm"),
        P("tm"),
    )
    staged = mesh.shape["rows"] == 16 and mesh.shape["tm"] == 2
    return jax.shard_map(
        local_staged if staged else local,
        mesh=mesh,
        in_specs=placed,
        out_specs=(
            P("rows", "tm", None),
            P("rows", "tm", None),
            P("rows", "tm"),
            P("rows", "tm"),
            P("rows", "tm"),
            P("rows", "tm"),
            P("tm"),
            P("tm"),
            P("tm"),
            P("tm"),
            P("tm"),
            P("tm"),
        ),
        check_vma=False,
    )
```

```python
import functools
import math

import jax
import jax.numpy as jnp
from jax import lax
from jax.experimental import pallas as pl
from jax.experimental.pallas import tpu as pltpu
from jax.sharding import PartitionSpec as P

H = 8
HD = 64
WINDOW = 250
REACH = 256
QBLOCK = 512


EPSILON = 1e-05
NEGATIVE = -1e30


def prefix(part, axis, combine, identity):
    place = lax.axis_index(axis)
    gathered = jax.tree.map(lambda a: lax.all_gather(a, axis), part)
    state = jax.tree.map(lambda a, e: jnp.zeros_like(a) + jnp.asarray(e, a.dtype), part, identity)

    def one(turn, state):
        return combine(
            state, jax.tree.map(lambda a: lax.dynamic_index_in_dim(a, turn, 0, False), gathered)
        )

    return lax.fori_loop(0, place, one, state)


def shifted(block, axis, distance):
    devices = range(lax.axis_size(axis))
    route = [(i - distance, i) for i in devices if i - distance in devices]
    return lax.ppermute(block, axis, route)


def layer_norm(values, gain_vec, bias_vec):
    average = jnp.mean(values, axis=-1, keepdims=True)
    centred = values - average
    variance = jnp.mean(centred * centred, axis=-1, keepdims=True)
    return centred * lax.rsqrt(variance + EPSILON) * gain_vec + bias_vec


def gelu_exact(values):
    return jax.nn.gelu(values, approximate=False)


def rotation_tables(positions):
    half_size = HD // 2
    ladder = jnp.arange(half_size, dtype=jnp.float32)
    frequency = jnp.exp(ladder * (-2.0 * math.log(10000.0) / HD))
    angles = positions.astype(jnp.float32)[:, None] * frequency[None, :]
    return (jnp.cos(angles)[:, None, :], jnp.sin(angles)[:, None, :])


def rotate(field, cosine, sine):
    half_size = field.shape[-1] // 2
    former = field[..., :half_size]
    latter = field[..., half_size:]
    return jnp.concatenate(
        [former * cosine - latter * sine, latter * cosine + former * sine], axis=-1
    )


def outer_sum(left, right):
    return lax.dot_general(
        left, right, (((0,), (0,)), ((), ())), preferred_element_type=jnp.float32
    )


def block_allowed(begin, segment, extended_segments, valid_keys):
    offsets = (
        jnp.arange(QBLOCK, dtype=jnp.int32)[:, None]
        - jnp.arange(QBLOCK + REACH, dtype=jnp.int32)[None, :]
        + REACH
    )
    near = (offsets >= 0) & (offsets < WINDOW)
    query_segments = segment[begin : begin + QBLOCK]
    key_segments = extended_segments[begin : begin + QBLOCK + REACH]
    key_valid = valid_keys[begin : begin + QBLOCK + REACH]
    return near & (query_segments[:, None] == key_segments[None, :]) & key_valid[None, :]


def block_scores(query_block, key_window, allowed):
    raw = jnp.einsum(
        "qhd,khd->hqk", query_block, key_window, preferred_element_type=jnp.float32
    ) * (1.0 / math.sqrt(HD))
    return jnp.where(allowed[None], raw, NEGATIVE)


def local(
    inputs,
    cotangent,
    segment_ids,
    qkv_weight,
    out_weight,
    up_weight,
    down_weight,
    norm_gain_one,
    norm_bias_one,
    attn_scale,
    norm_gain_two,
    norm_bias_two,
    mlp_scale,
):
    frames = inputs.shape[1]
    width = inputs.shape[2]
    low_type = jnp.bfloat16
    gathered = (
        lax.all_gather(qkv_weight.astype(low_type), "tm", axis=1, tiled=True),
        lax.all_gather(out_weight.astype(low_type), "tm", axis=1, tiled=True),
        lax.all_gather(up_weight.astype(low_type), "tm", axis=1, tiled=True),
        lax.all_gather(down_weight.astype(low_type), "tm", axis=1, tiled=True),
        lax.all_gather(norm_gain_one.astype(low_type), "tm", axis=0, tiled=True),
        lax.all_gather(norm_bias_one.astype(low_type), "tm", axis=0, tiled=True),
        lax.all_gather(attn_scale.astype(low_type), "tm", axis=0, tiled=True),
        lax.all_gather(norm_gain_two.astype(low_type), "tm", axis=0, tiled=True),
        lax.all_gather(norm_bias_two.astype(low_type), "tm", axis=0, tiled=True),
        lax.all_gather(mlp_scale.astype(low_type), "tm", axis=0, tiled=True),
    )
    w_qkv, w_out, w_up, w_down = (
        lax.all_gather(gathered[0], "rows", axis=0, tiled=True),
        lax.all_gather(gathered[1], "rows", axis=0, tiled=True),
        lax.all_gather(gathered[2], "rows", axis=0, tiled=True),
        lax.all_gather(gathered[3], "rows", axis=0, tiled=True),
    )
    gain_one, bias_one, scale_one, gain_two, bias_two, scale_two = [
        piece.astype(jnp.float32) for piece in gathered[4:]
    ]
    segment = segment_ids[0]
    index = jnp.arange(frames, dtype=jnp.int32)
    last_run = jnp.sum((segment == segment[frames - 1]).astype(jnp.int32), keepdims=True)

    def join_runs(earlier, later):
        extends = (later[1] == frames) & (later[0] == earlier[0])
        joined = jnp.where(extends, earlier[1] + later[1], later[1])
        vacant = later[0] < 0
        return (jnp.where(vacant, earlier[0], later[0]), jnp.where(vacant, earlier[1], joined))

    before_id, before_run = prefix(
        (segment[frames - 1 :], last_run),
        "tm",
        join_runs,
        (jnp.full((1,), -1, jnp.int32), jnp.zeros((1,), jnp.int32)),
    )
    change = jnp.concatenate([jnp.ones((1,), jnp.bool_), segment[1:] != segment[:-1]])
    starts = lax.cummax(jnp.where(change, index, jnp.zeros_like(index)), axis=0)
    positions = index - starts + jnp.where(segment == before_id[0], before_run[0], 0)
    cosine, sine = rotation_tables(positions)
    source = inputs[0].astype(jnp.float32)
    normed_one, norm_one_pull = jax.vjp(layer_norm, source, gain_one, bias_one)
    normed_one_low = normed_one.astype(low_type)
    projected = jnp.dot(normed_one_low, w_qkv, preferred_element_type=jnp.float32)
    queries = rotate(projected[:, :width].reshape(frames, H, HD), cosine, sine).astype(low_type)
    keys_flat = (
        rotate(projected[:, width : 2 * width].reshape(frames, H, HD), cosine, sine)
        .reshape(frames, width)
        .astype(low_type)
    )
    values_flat = projected[:, 2 * width :].astype(low_type)
    got_keys, got_values, got_segments = shifted((keys_flat, values_flat, segment), "tm", 1)
    got_keys = got_keys[frames - REACH :]
    got_values = got_values[frames - REACH :]
    got_segments = got_segments[frames - REACH :]
    extended_keys = jnp.concatenate([got_keys, keys_flat], axis=0).reshape(REACH + frames, H, HD)
    extended_values = jnp.concatenate([got_values, values_flat], axis=0).reshape(
        REACH + frames, H, HD
    )
    extended_segments = jnp.concatenate([got_segments, segment])
    valid_keys = (lax.axis_index("tm") > 0) | (jnp.arange(REACH + frames, dtype=jnp.int32) >= REACH)
    block_count = frames // QBLOCK
    mixed_parts = []
    log_sums = []
    for block in range(block_count):
        begin = block * QBLOCK
        allowed = block_allowed(begin, segment, extended_segments, valid_keys)
        scores = block_scores(
            queries[begin : begin + QBLOCK], extended_keys[begin : begin + QBLOCK + REACH], allowed
        )
        top = jnp.max(scores, axis=-1, keepdims=True)
        weights = jnp.exp(scores - top)
        total = jnp.sum(weights, axis=-1, keepdims=True)
        probs = (weights / total).astype(low_type)
        mixed_parts.append(
            jnp.einsum(
                "hqk,khd->qhd",
                probs,
                extended_values[begin : begin + QBLOCK + REACH],
                preferred_element_type=jnp.float32,
            )
        )
        log_sums.append(top + jnp.log(total))
    mixed_low = jnp.concatenate(mixed_parts, axis=0).reshape(frames, width).astype(low_type)
    branch = jnp.dot(mixed_low, w_out, preferred_element_type=jnp.float32)
    after = source + scale_one * branch
    normed_two, norm_two_pull = jax.vjp(layer_norm, after, gain_two, bias_two)
    normed_two_low = normed_two.astype(low_type)
    hidden = jnp.dot(normed_two_low, w_up, preferred_element_type=jnp.float32)
    active, gelu_pull = jax.vjp(gelu_exact, hidden)
    active_low = active.astype(low_type)
    branch_two = jnp.dot(active_low, w_down, preferred_element_type=jnp.float32)
    result = (after + scale_two * branch_two).astype(low_type)
    again = (
        lax.all_gather(qkv_weight.astype(low_type), "tm", axis=1, tiled=True),
        lax.all_gather(out_weight.astype(low_type), "tm", axis=1, tiled=True),
        lax.all_gather(up_weight.astype(low_type), "tm", axis=1, tiled=True),
        lax.all_gather(down_weight.astype(low_type), "tm", axis=1, tiled=True),
    )
    back_qkv, back_out, back_up, back_down = (
        lax.all_gather(again[0], "rows", axis=0, tiled=True),
        lax.all_gather(again[1], "rows", axis=0, tiled=True),
        lax.all_gather(again[2], "rows", axis=0, tiled=True),
        lax.all_gather(again[3], "rows", axis=0, tiled=True),
    )
    upstream = cotangent[0].astype(jnp.float32)
    grad_scale_two = jnp.sum(upstream * branch_two, axis=0)
    grad_branch_two = (upstream * scale_two).astype(low_type)
    grad_down = outer_sum(active_low, grad_branch_two)
    grad_active = lax.dot_general(
        grad_branch_two, back_down, (((1,), (1,)), ((), ())), preferred_element_type=jnp.float32
    )
    grad_hidden = gelu_pull(grad_active)[0].astype(low_type)
    grad_up = outer_sum(normed_two_low, grad_hidden)
    grad_normed_two = lax.dot_general(
        grad_hidden, back_up, (((1,), (1,)), ((), ())), preferred_element_type=jnp.float32
    )
    after_part, grad_gain_two, grad_bias_two = norm_two_pull(grad_normed_two)
    grad_after = upstream + after_part
    grad_scale_one = jnp.sum(grad_after * branch, axis=0)
    grad_branch = (grad_after * scale_one).astype(low_type)
    grad_out = outer_sum(mixed_low, grad_branch)
    grad_mixed = lax.dot_general(
        grad_branch, back_out, (((1,), (1,)), ((), ())), preferred_element_type=jnp.float32
    )
    grad_mixed = grad_mixed.astype(low_type).reshape(frames, H, HD)
    factor = 1.0 / math.sqrt(HD)
    grad_keys_ext = jnp.zeros((REACH + frames, H, HD), jnp.float32)
    grad_values_ext = jnp.zeros((REACH + frames, H, HD), jnp.float32)
    query_grads = []
    for block in range(block_count):
        begin = block * QBLOCK
        allowed = block_allowed(begin, segment, extended_segments, valid_keys)
        query_block = queries[begin : begin + QBLOCK]
        key_window = extended_keys[begin : begin + QBLOCK + REACH]
        value_window = extended_values[begin : begin + QBLOCK + REACH]
        scores = block_scores(query_block, key_window, allowed)
        probs_full = jnp.exp(scores - log_sums[block])
        probs_low = probs_full.astype(low_type)
        grad_out_block = grad_mixed[begin : begin + QBLOCK]
        grad_probs = jnp.einsum(
            "qhd,khd->hqk", grad_out_block, value_window, preferred_element_type=jnp.float32
        )
        grad_values_ext = grad_values_ext.at[begin : begin + QBLOCK + REACH].add(
            jnp.einsum(
                "hqk,qhd->khd", probs_low, grad_out_block, preferred_element_type=jnp.float32
            )
        )
        balance = jnp.sum(grad_probs * probs_full, axis=-1, keepdims=True)
        grad_scores = (probs_full * (grad_probs - balance)).astype(low_type)
        query_grads.append(
            jnp.einsum("hqk,khd->qhd", grad_scores, key_window, preferred_element_type=jnp.float32)
            * factor
        )
        grad_keys_ext = grad_keys_ext.at[begin : begin + QBLOCK + REACH].add(
            jnp.einsum("hqk,qhd->khd", grad_scores, query_block, preferred_element_type=jnp.float32)
            * factor
        )
    grad_keys_flat = grad_keys_ext.reshape(REACH + frames, width)
    grad_values_flat = grad_values_ext.reshape(REACH + frames, width)
    back_keys, back_values = (
        shifted(grad_keys_flat[:REACH].astype(jnp.bfloat16), "tm", -1).astype(jnp.float32),
        shifted(grad_values_flat[:REACH].astype(jnp.bfloat16), "tm", -1).astype(jnp.float32),
    )
    own_keys = grad_keys_flat[REACH:]
    own_values = grad_values_flat[REACH:]
    own_keys = jnp.concatenate(
        [own_keys[: frames - REACH], own_keys[frames - REACH :] + back_keys], axis=0
    )
    own_values = jnp.concatenate(
        [own_values[: frames - REACH], own_values[frames - REACH :] + back_values], axis=0
    )
    grad_queries = rotate(jnp.concatenate(query_grads, axis=0), cosine, -sine).reshape(
        frames, width
    )
    grad_keys = rotate(own_keys.reshape(frames, H, HD), cosine, -sine).reshape(frames, width)
    grad_projected = jnp.concatenate([grad_queries, grad_keys, own_values], axis=1).astype(low_type)
    grad_qkv = outer_sum(normed_one_low, grad_projected)
    grad_normed_one = lax.dot_general(
        grad_projected, back_qkv, (((1,), (1,)), ((), ())), preferred_element_type=jnp.float32
    )
    source_part, grad_gain_one, grad_bias_one = norm_one_pull(grad_normed_one)
    input_grad = (grad_after + source_part).astype(low_type)
    reduced = (
        lax.psum_scatter(grad_qkv, "tm", scatter_dimension=1, tiled=True),
        lax.psum_scatter(grad_out, "tm", scatter_dimension=1, tiled=True),
        lax.psum_scatter(grad_up, "tm", scatter_dimension=1, tiled=True),
        lax.psum_scatter(grad_down, "tm", scatter_dimension=1, tiled=True),
        lax.psum_scatter(grad_gain_one, "tm", scatter_dimension=0, tiled=True),
        lax.psum_scatter(grad_bias_one, "tm", scatter_dimension=0, tiled=True),
        lax.psum_scatter(grad_scale_one, "tm", scatter_dimension=0, tiled=True),
        lax.psum_scatter(grad_gain_two, "tm", scatter_dimension=0, tiled=True),
        lax.psum_scatter(grad_bias_two, "tm", scatter_dimension=0, tiled=True),
        lax.psum_scatter(grad_scale_two, "tm", scatter_dimension=0, tiled=True),
    )
    qkv_grad, out_grad, up_grad, down_grad = (
        lax.psum_scatter(reduced[0], "rows", scatter_dimension=0, tiled=True),
        lax.psum_scatter(reduced[1], "rows", scatter_dimension=0, tiled=True),
        lax.psum_scatter(reduced[2], "rows", scatter_dimension=0, tiled=True),
        lax.psum_scatter(reduced[3], "rows", scatter_dimension=0, tiled=True),
    )
    vector_sums = lax.psum(
        (reduced[4], reduced[5], reduced[6], reduced[7], reduced[8], reduced[9]), "rows"
    )
    return (
        result[None],
        input_grad[None],
        qkv_grad,
        out_grad,
        up_grad,
        down_grad,
        vector_sums[0],
        vector_sums[1],
        vector_sums[2],
        vector_sums[3],
        vector_sums[4],
        vector_sums[5],
    )


MESH_IDS = pl.DeviceIdType.MESH
F32 = jnp.float32
BF16 = jnp.bfloat16


def dot(left, right, contract=((1,), (0,))):
    return lax.dot_general(left, right, (contract, ((), ())), preferred_element_type=F32)


def dot_t(left, right):
    return dot(left, right, ((1,), (1,)))


def start_of(index, size):
    return pl.ds(pl.multiple_of(index * size, size), size)


def coordinates():
    row, core = lax.axis_index("rows"), lax.axis_index("tm")
    return row, core, lax.rem(row, 2), lax.rem(lax.div(row, 2), 2), lax.div(row, 4)


def peers_of(at):
    row, core, x, y, z = at
    found = {
        "x": (row + 1 - 2 * x, core),
        "y": (row + 2 - 4 * y, core),
        "s": (row, 1 - core),
    }
    for k in (1, 2, 3):
        found[k] = (lax.rem(z + k, 4) * 4 + lax.rem(row, 4), core)
    found["xy"] = (row + 3 - 2 * x - 4 * y, core)
    for k in range(1, 16):
        found["r", k] = (lax.rem(row + k, 16), core)
    return found


def greet(peers):
    for name in ["s"] + [("r", k) for k in range(1, 16)]:
        pl.semaphore_signal(
            pltpu.get_barrier_semaphore(), inc=1, device_id=peers[name], device_id_type=MESH_IDS
        )


def be_greeted():
    pl.semaphore_wait(pltpu.get_barrier_semaphore(), 16)


class Links:
    def __init__(self, sems, peers):
        self.sems, self.peers, self.used = sems, peers, 0

    def slot(self):
        self.used += 1
        return self.sems.at[self.used - 1]

    def copy(self, src, dst, peer, send, recv):
        return pltpu.make_async_remote_copy(
            src_ref=src,
            dst_ref=dst,
            send_sem=send,
            recv_sem=recv,
            device_id=self.peers[peer],
            device_id_type=MESH_IDS,
        )

    def single(self, src, dst, peer):
        return self.copy(src, dst, peer, self.slot(), self.slot())


def await_bytes(like, sem):
    pltpu.make_async_copy(like, like, sem).wait()


class Gather:
    def __init__(self, units, i, links, at):
        full = units.at[i]
        row, core, x, y, z = at
        half = full.shape[4] // 2
        low, high = pl.ds(0, half), pl.ds(half, half)
        every = slice(None)
        near, far = links.slot(), links.slot()
        got = [links.slot() for _ in range(4)]

        def copy(where, peer, send, recv):
            return links.copy(full.at[where], full.at[where], peer, send, recv)

        self.starts = (
            [copy((core, z, y, x), k, near, got[0]) for k in (1, 2, 3)],
            [
                copy((core, every, y, x, low), "x", far, got[1]),
                copy((core, every, y, x, high), "y", far, got[1]),
                copy((core, every, y, x), "s", far, got[3]),
            ],
            [
                copy((core, every, y, every, low), "y", far, got[2]),
                copy((core, every, every, x, high), "x", far, got[2]),
                copy((core, every, y, 1 - x, low), "s", far, got[3]),
                copy((core, every, 1 - y, x, high), "s", far, got[3]),
            ],
            [
                copy((core, every, 1 - y, every, low), "s", far, got[3]),
                copy((core, every, every, 1 - x, high), "s", far, got[3]),
            ],
            [],
        )
        self.waits = (
            None,
            (full.at[core, 0:3, y, x], got[0]),
            (full.at[core, :, y, x], got[1]),
            (full.at[core, :, y], got[2]),
            (full.at[1 - core], got[3]),
        )
        self.sent = ((full.at[core, 0:3, y, x], near), (units.at[0:7, 0, 0], far))

    def step(self, number):
        if number > 0:
            await_bytes(*self.waits[number])
        for copy in self.starts[number]:
            copy.start()

    def drain(self):
        for like, sem in self.sent:
            await_bytes(like, sem)


class GatherDirect:
    def __init__(self, units, i, links, at):
        full = units.at[i]
        row, core, x, y, z = at
        piece = full.at[core, z, y, x]
        self.sent, self.got, passed, self.whole = [links.slot() for _ in range(4)]
        self.starts = [
            links.copy(piece, piece, ("r", k), self.sent, self.got) for k in range(1, 16)
        ]
        self.over = links.copy(full.at[core], full.at[core], "s", passed, self.whole)
        self.fifteen = units.at[0:5, 0, 0:3, 0, 0]

    def step(self, number):
        if number == 0:
            for copy in self.starts:
                copy.start()
        if number == 1:
            await_bytes(self.fifteen, self.got)
            self.over.start()
        if number == 2:
            self.over.wait_recv()

    def drain(self):
        await_bytes(self.fifteen, self.sent)
        self.over.wait_send()


class GatherPlane:
    def __init__(self, units, i, links, at):
        full = units.at[i]
        row, core, x, y, z = at
        every = slice(None)
        near, far = links.slot(), links.slot()
        got = [links.slot() for _ in range(3)]

        def copy(where, peer, send, recv):
            return links.copy(full.at[where], full.at[where], peer, send, recv)

        column = (core, every, y, x)
        self.starts = (
            [copy((core, z, y, x), k, near, got[0]) for k in (1, 2, 3)],
            [copy(column, peer, far, got[1]) for peer in ("xy", "x", "y")]
            + [copy(column, "s", far, got[2])],
            [
                copy((core, every, y, 1 - x), "s", far, got[2]),
                copy((core, every, 1 - y), "s", far, got[2]),
            ],
            [],
        )
        self.waits = (
            None,
            (full.at[core, 0:3, y, x], got[0]),
            (units.at[0:3, 0, :, 0, 0], got[1]),
            (full.at[1 - core], got[2]),
        )
        self.sent = ((full.at[core, 0:3, y, x], near), (units.at[0:7, 0, 0], far))

    def step(self, number):
        if number > 0:
            await_bytes(*self.waits[number])
        for copy in self.starts[number]:
            copy.start()

    def drain(self):
        for like, sem in self.sent:
            await_bytes(like, sem)


class Scatter:
    def __init__(self, own, out, arrived, result, links, at, units):
        self.own, self.out, self.result, self.at = own, out, result, at
        self.s_in, self.c_in, self.b_in, self.a_in = arrived
        row, core, x, y, z = at
        self.rows = out.shape[3]
        half = self.half = self.rows // 2
        low, high = self.low, self.high = pl.ds(0, half), pl.ds(half, half)
        every = slice(None)
        self.d = links.single(out, self.s_in, "s")
        self.far = links.slot()
        self.got = [links.slot() for _ in range(3)]
        self.units = units

        def copy(src, dst, peer, which):
            return links.copy(src, dst, peer, self.far, self.got[which])

        self.c1 = copy(out.at[every, 1 - y, every, low], self.c_in.at[0], "y", 0)
        self.c2 = copy(out.at[every, every, 1 - x, high], self.c_in.at[1], "x", 0)
        self.b1 = copy(out.at[every, y, 1 - x, low], self.b_in.at[0], "x", 1)
        self.b2 = copy(out.at[every, 1 - y, x, high], self.b_in.at[1], "y", 1)
        self.a = [
            copy(out.at[lax.rem(z + k, 4), y, x], self.a_in.at[k - 1], k, 2) for k in (1, 2, 3)
        ]

    def mine(self, k, y, x, part):
        begin = ((k * 2 + y) * 2 + x) * self.rows + part * self.half
        return self.own[pl.ds(pl.multiple_of(begin, self.half), self.half), :] + self.s_in[
            k, y, x, pl.ds(part * self.half, self.half)
        ].astype(F32)

    def column(self, k, part):
        row, core, x, y, z = self.at
        place = x if part == 0 else y
        return (
            self.mine(k, y, x, part)
            + self.c_in[part, k, place].astype(F32)
            + self.b_in[part, k].astype(F32)
        )

    def step(self, number):
        row, core, x, y, z = self.at
        low, high, out = self.low, self.high, self.out
        c_in = self.c_in
        if number == 0:
            self.d.start()
        if number == 1:
            self.d.wait()
            for k in range(4):
                for i in range(2):
                    out[k, 1 - y, i, low] = self.mine(k, 1 - y, i, 0).astype(BF16)
            self.c1.start()
            for k in range(4):
                for i in range(2):
                    out[k, i, 1 - x, high] = self.mine(k, i, 1 - x, 1).astype(BF16)
            self.c2.start()
        if number == 2:
            await_bytes(c_in, self.got[0])
            for k in range(4):
                out[k, y, 1 - x, low] = (
                    self.mine(k, y, 1 - x, 0) + c_in[0, k, 1 - x].astype(F32)
                ).astype(BF16)
            self.b1.start()
            for k in range(4):
                out[k, 1 - y, x, high] = (
                    self.mine(k, 1 - y, x, 1) + c_in[1, k, 1 - y].astype(F32)
                ).astype(BF16)
            self.b2.start()
        if number == 3:
            await_bytes(self.b_in, self.got[1])
            for k in (1, 2, 3):
                there = lax.rem(z + k, 4)
                out[there, y, x, low] = self.column(there, 0).astype(BF16)
                out[there, y, x, high] = self.column(there, 1).astype(BF16)
                self.a[k - 1].start()
            self.own[low, :] = self.column(z, 0)
            self.own[high, :] = self.column(z, 1)
        if number == 4:
            await_bytes(self.a_in, self.got[2])
            self.result(
                self.own[: self.rows, :]
                + (self.a_in[0].astype(F32) + self.a_in[1].astype(F32) + self.a_in[2].astype(F32))
            )

    def drain(self):
        await_bytes(self.units.at[0:5, 0:3, 0, 0], self.far)


class ScatterDirect(Scatter):
    def __init__(self, own, out, arrived, result, links, at, units):
        self.own, self.out, self.result, self.at = own, out, result, at
        self.s_in, self.pieces = arrived
        row, core, x, y, z = at
        self.rows = out.shape[3]
        self.half = self.rows // 2
        self.units = units
        self.d = links.single(out, self.s_in, "s")
        self.far, self.got = links.slot(), links.slot()
        self.copies = []
        for k in range(1, 16):
            there = lax.rem(row + k, 16)
            where = (lax.div(there, 4), lax.rem(lax.div(there, 2), 2), lax.rem(there, 2))
            made = links.copy(out.at[where], self.pieces.at[k - 1], ("r", k), self.far, self.got)
            self.copies.append((where, made))

    def whole(self, z, y, x):
        return jnp.concatenate([self.mine(z, y, x, part) for part in range(2)], axis=0)

    def step(self, number):
        row, core, x, y, z = self.at
        if number == 0:
            self.d.start()
        if number == 1:
            self.d.wait()
            for where, copy in self.copies:
                self.out[where] = self.whole(*where).astype(BF16)
                copy.start()
            self.own[: self.rows, :] = self.whole(z, y, x)
        if number == 2:
            await_bytes(self.pieces, self.got)
            total = self.own[: self.rows, :]
            for k in range(15):
                total = total + self.pieces[k].astype(F32)
            self.result(total)


def gelu_and_slope(values):
    cdf = 0.5 + 0.5 * lax.erf(values * math.sqrt(0.5))
    bell = jnp.exp2((values * values) * (-0.5 * math.log2(math.e)))
    return values * cdf, cdf + (values * (1.0 / math.sqrt(2.0 * math.pi))) * bell


def lane_pattern(shape, size):
    return lax.rem(lax.broadcasted_iota(jnp.int32, shape, len(shape) - 1), size)


def turned(values, cosine, sine):
    return values * cosine + pltpu.roll(values, 64, 1) * sine


def swap_middle(values):
    group = lane_pattern((1, 128), 128) // 32
    return jnp.where(
        group == 1,
        pltpu.roll(values, 96, 1),
        jnp.where(group == 2, pltpu.roll(values, 32, 1), values),
    )


TILE = 256
BLOCK = 128
SPAN = BLOCK + REACH
PAIRS = H // 2
COLUMNS = 256
UNITS = 12
GROUP, OUT, DOWN, UP = 0, 3, (4, 6, 8, 10), (5, 7, 9, 11)
D0, U0, D1, U1, D2, U2, D3, U3 = range(4, 12)
DUE = {
    "tables": ((1, 1),),
    "masks": ((0, 1), (2, 1), (OUT, 0), (D0, 0), (0, 2)),
    ("before", 0): ((OUT, 1), (U0, 0)),
    ("during", 0): ((1, 2),),
    ("after", 0): ((1, 3), (D0, 1), (D1, 0)),
    ("before", 1): ((2, 2), (OUT, 2), (U0, 1), (U1, 0)),
    ("after", 1): ((2, 3), (D0, 2), (D1, 1), (D2, 0)),
    ("before", 2): ((OUT, 3), (U0, 2), (U1, 1), (U2, 0)),
    ("after", 2): ((OUT, 4), (D0, 3), (D1, 2), (D2, 1), (D3, 0)),
    ("after", 3): ((D0, 4), (U0, 3), (U1, 2), (U2, 1), (U3, 0)),
    ("norm", 2): ((D2, 2),),
    ("feed", 0, 0): ((U0, 4), (D1, 3), (D3, 1)),
    ("feed", 0, 1): ((D1, 4), (U1, 3), (U2, 2), (U3, 1)),
    ("feed", 0, 2): ((D2, 3), (D3, 2)),
    ("feed", 1, 0): ((U1, 4), (D2, 4)),
    ("feed", 1, 1): ((U2, 3), (U3, 2)),
    ("feed", 1, 2): ((D3, 3), (U2, 4)),
    ("feed", 2, 0): ((D3, 4),),
    ("feed", 2, 1): ((U3, 3),),
    ("feed", 2, 2): ((U3, 4),),
}
LAST = 2
CHUNKS = (
    (((0, 0), (1, 0)), ((2, 0), (2, 1))),
    (((0, 1), (1, 1)), ((2, 2), (1, 2))),
    (((0, 2), (0, 3)), ((2, 3), (1, 3))),
)


def place_of(kind, p):
    for g, cores in enumerate(CHUNKS):
        for c, pair in enumerate(cores):
            if (kind, p) in pair:
                return g, c, pair.index((kind, p))


def run(begin, end, body, events=None):
    def with_events(i, carried):
        for when, actions in sorted((events or {}).items()):

            @pl.when(i == when)
            def _(actions=actions):
                for action in actions:
                    action()

        body(i, carried)
        return 0

    lax.fori_loop(begin, end, with_events, 0)


def in_turn(count, stages, events):
    for i in range(count + len(stages) - 1):
        for action in events.get(i, []):
            action()
        for late, stage in enumerate(stages):
            if 0 <= i - late < count:
                stage(i - late)


def regroup(tiles, quarter, back=False):
    group = lax.broadcasted_iota(jnp.int32, (1, 128), 1) // 32
    out = jnp.zeros_like(tiles[0])
    for a in range(4):
        out = jnp.where(group == a, pltpu.roll(tiles[a], (a - quarter) * 32 % 128, 1), out)
    return out


def scratch_list(frames, width):
    blocks = frames // BLOCK
    ext = REACH + frames
    unit = (4, 2, 2, width // 16, COLUMNS)
    half = width // 32
    return [
        ("x", (frames, width), BF16),
        ("dy", (frames, width), BF16),
        ("y", (frames, width), BF16),
        ("mixed", (frames, width), BF16),
        ("wo", (width // 16, width // 2), F32),
        ("wu", (width // 16, 2 * width), F32),
        ("wd", (width // 4, width // 2), F32),
        ("w", (UNITS, 2) + unit, BF16),
        ("pos", (8, frames), F32),
        ("vecs", (2, 8, width // 2), F32),
        ("segs", (2, 8, frames), F32),
        ("n1t", (width, frames), BF16),
        ("cos", (frames, 128), F32),
        ("sin", (frames, 128), F32),
        ("bias", (blocks, SPAN, BLOCK), BF16),
        ("qx", (PAIRS, frames, 128), BF16),
        ("kx", (PAIRS, ext, 128), BF16),
        ("vx", (PAIRS, ext, 128), BF16),
        ("kt", (PAIRS, 128, ext), BF16),
        ("vt", (PAIRS, 128, ext), BF16),
        ("probs", (PAIRS, blocks, SPAN, 2 * BLOCK), BF16),
        ("ot", (width, frames), BF16),
        ("n2t", (width, frames), BF16),
        ("actt", (2 * COLUMNS, frames), BF16),
        ("du", (2, frames, COLUMNS), BF16),
        ("after", (frames, width), F32),
        ("branch", (frames, width), BF16),
        ("branch_two", (frames, width), F32),
        ("dx1", (frames, width), F32),
        ("dba", (2, frames, width // 2), BF16),
        ("dox", (PAIRS, frames, 128), BF16),
        ("dp", (3, 2, frames, COLUMNS), BF16),
        ("dkx", (ext, 128), F32),
        ("dvx", (ext, 128), F32),
        ("h_out", (PAIRS, 2, REACH, 128), BF16),
        ("h_in", (PAIRS, 2, REACH, 128), BF16),
        ("acc", (8, width), F32),
        ("v_out", (8, width // 2), F32),
        ("v_in", (8, width // 2), F32),
        ("v_all", (16, 8, width // 2), F32),
        ("pieces", (15, width // 16, COLUMNS), BF16),
        ("own", (UNITS - 3, width, COLUMNS), F32),
        ("up_sums", (4, width // 16, COLUMNS), F32),
        ("s_in", (UNITS,) + unit, BF16),
        ("c_in", (UNITS - 1, 2, 4, 2, half, COLUMNS), BF16),
        ("b_in", (UNITS - 1, 2, 4, half, COLUMNS), BF16),
        ("a_in", (UNITS - 1, 3, width // 16, COLUMNS), BF16),
    ]


SLOTS = 12 * UNITS + 2 * (2 + 2 * PAIRS + PAIRS) + 4


def layer_kernel(names, *refs):
    seg_ref, wq_shard = refs[2:4]
    vectors = refs[7:13]
    y_out, ig_out, gq, go, gu, gd, gv = refs[13:20]
    m = dict(zip(names, refs[20:-2]))
    x_ref, dy_ref, y_ref, mixed = m["x"], m["dy"], m["y"], m["mixed"]
    wo_shard, wu_shard, wd_shard = m["wo"], m["wu"], m["wd"]
    moves = refs[-2]
    loads = [
        pltpu.make_async_copy(source, target, moves.at[i])
        for i, (source, target) in enumerate(
            (
                (refs[0].at[0], x_ref),
                (refs[4], wo_shard),
                (refs[5], wu_shard),
                (refs[6], wd_shard),
                (refs[1].at[0], dy_ref),
            )
        )
    ]
    at = coordinates()
    row, core, x, y, z = at
    peers = peers_of(at)
    links = Links(refs[-1], peers)
    frames, width = x_ref.shape
    piece = width // 16
    blocks, tiles = frames // BLOCK, frames // TILE
    factor = 1.0 / math.sqrt(HD)
    w = m["w"]
    other = 1 - core

    def chunk_columns(g, j):
        offsets = []
        for c in range(2):
            kind, p = CHUNKS[g][c][j]
            offsets.append((kind * PAIRS + p - 6 * c) * 128)
        begin = offsets[0] + core * (offsets[1] - offsets[0])
        return pl.ds(pl.multiple_of(begin, 128), 128)

    def ordered(g, j, value):
        kinds = [CHUNKS[g][c][j][0] for c in range(2)]
        if kinds == [2, 2]:
            return value
        swapped = swap_middle(value)
        if 2 not in kinds:
            return swapped
        return jnp.where(core == kinds.index(2), value, swapped)

    greet(peers)
    for load in loads:
        load.start()
    for g in range(3):
        for j in range(2):
            w[g, core, z, y, x, :, j * 128 : (j + 1) * 128] = ordered(
                g, j, wq_shard[:, chunk_columns(g, j)]
            ).astype(BF16)
    m["vecs"][core] = jnp.concatenate(
        [v[...].astype(BF16).astype(F32) for v in vectors]
        + [jnp.zeros((2, width // 2), F32)],
        axis=0,
    )
    m["segs"][core] = jnp.broadcast_to(seg_ref[...].astype(F32), (8, frames))
    be_greeted()
    vec_copy = links.single(m["vecs"].at[core], m["vecs"].at[core], "s")
    seg_copy = links.single(m["segs"].at[core], m["segs"].at[core], "s")
    kinds = [GatherDirect, GatherPlane, GatherPlane] + [Gather] * (UNITS - 3)
    gathers = [kind(w, i, links, at) for i, kind in enumerate(kinds)]

    def due(*where):
        for i, step in DUE.get(where if len(where) > 1 else where[0], ()):
            gathers[i].step(step)

    vec_copy.start()
    seg_copy.start()
    for i in (1, 0, 2):
        gathers[i].step(0)
    for load in loads:
        load.wait()
    w[OUT, core, z, y, x] = wo_shard[...].astype(BF16)
    for q in range(4):
        w[DOWN[q], core, z, y, x] = wd_shard[q * piece : (q + 1) * piece, :].astype(BF16)
    for q in range(4):
        for j in range(2):
            made = regroup(
                [wu_shard[:, (4 * j + a) * 128 : (4 * j + a + 1) * 128] for a in range(4)], q
            )
            w[UP[q], core, z, y, x, :, j * 128 : (j + 1) * 128] = made.astype(BF16)

    def vector(i):
        return jnp.concatenate([m["vecs"][0, i : i + 1, :], m["vecs"][1, i : i + 1, :]], axis=1)

    def normalized(values):
        average = jnp.mean(values, axis=-1, keepdims=True)
        centred = values - average
        variance = jnp.mean(centred * centred, axis=-1, keepdims=True)
        scale = lax.rsqrt(variance + EPSILON)
        return centred * scale, scale

    vec_copy.wait_recv()
    n1 = y_ref
    gain_one, bias_one = vector(0), vector(1)

    def norm_one(t, _):
        rows = start_of(t, TILE)
        unit, _scale = normalized(x_ref[rows, :].astype(F32))
        low = (unit * gain_one + bias_one).astype(BF16)
        n1[rows, :] = low
        m["n1t"][:, rows] = low.T

    run(0, tiles, norm_one)

    seg_copy.wait_recv()
    segs = m["segs"]
    index = lax.broadcasted_iota(jnp.int32, (8, frames), 1)
    order = index.astype(F32)

    def starts_in(which):
        line = segs[which]
        change = (line != pltpu.roll(line, 1, 1)) | (index == 0)
        begun = jnp.where(change, order, 0.0)
        reach = 1
        while reach < frames:
            begun = jnp.maximum(begun, jnp.where(index >= reach, pltpu.roll(begun, reach, 1), 0.0))
            reach *= 2
        return begun

    running = (core > 0) & (segs[core] == segs[other][:, frames - 1 :])
    before = starts_in(other)[:, frames - 1 :]
    m["pos"][...] = order - jnp.where(
        running, before - (core * frames).astype(F32), starts_in(core)
    )
    seg_blocks = m["own"]

    def across(line):
        return jnp.broadcast_to(line, (BLOCK, BLOCK)).T

    def spread(which, begin):
        return across(segs[which, 0:1, begin : begin + BLOCK])

    def seg_place(e):
        return (e // 8, pl.ds((e % 8) // 2 * BLOCK, BLOCK), pl.ds(e % 2 * BLOCK, BLOCK))

    group = lane_pattern((1, 128), 128) // 32
    lanes = lane_pattern((1, 128), HD // 2).astype(F32)
    frequency = jnp.exp(lanes * (-2.0 * math.log(10000.0) / HD))
    near_half = lane_pattern((1, 128), 128) < HD
    quarter = frames // 4
    for i in range(quarter // BLOCK):
        position = across(m["pos"][0:1, i * BLOCK : (i + 1) * BLOCK])
        for a in range(1, 4):
            begin = a * quarter + i * BLOCK
            position = jnp.where(
                group == a, across(m["pos"][0:1, begin : begin + BLOCK]), position
            )
        angle = position * frequency
        for name, table in (("cos", jnp.cos(angle)), ("sin", jnp.sin(angle))):
            for a in range(4):
                begin = a * quarter + i * BLOCK
                wide = jnp.where(group == a, table, 0.0)
                wide = wide + pltpu.roll(wide, 32, 1)
                wide = wide + pltpu.roll(wide, 64, 1)
                if name == "sin":
                    wide = jnp.where(near_half, -wide, wide)
                m[name][begin : begin + BLOCK, :] = wide

    for e in range(REACH // BLOCK):
        halo = spread(other, frames - REACH + e * BLOCK)
        seg_blocks[seg_place(e)] = jnp.where(core > 0, halo, -1.0)
    for b in range(blocks):
        seg_blocks[seg_place(REACH // BLOCK + b)] = spread(core, b * BLOCK)
    due("tables")
    distance = (
        lax.broadcasted_iota(jnp.int32, (SPAN, BLOCK), 1)
        - lax.broadcasted_iota(jnp.int32, (SPAN, BLOCK), 0)
        + REACH
    )
    near = (distance >= 0) & (distance < WINDOW)
    for b in range(blocks):
        keys = jnp.concatenate([seg_blocks[seg_place(b + i)] for i in range(SPAN // BLOCK)], axis=0)
        line = segs[core, 0:1, b * BLOCK : (b + 1) * BLOCK]
        m["bias"][b] = jnp.where(near & (keys == line), 0.0, NEGATIVE).astype(BF16)
    due("masks")

    def two_heads(value, swapped=False):
        first = lax.rem(group, 2) == 0 if swapped else group < 2
        zero = jnp.zeros_like(value)
        return jnp.concatenate(
            [jnp.where(first, value, zero), jnp.where(first, zero, value)], axis=0
        )

    def projection(g):
        def project(t, _):
            rows = start_of(t, TILE)
            placed = pl.ds(pl.multiple_of(REACH + t * TILE, TILE), TILE)
            left = n1[rows, :]
            cosine, sine = m["cos"][rows, :], m["sin"][rows, :]
            for c in range(2):
                wide = dot(left, w[g, c].reshape(width, COLUMNS))
                for j in range(2):
                    chunk = wide[:, j * 128 : (j + 1) * 128]
                    kind, p = CHUNKS[g][c][j]
                    if kind == 0:
                        turn = turned(chunk, cosine, sine).astype(BF16)
                        m["qx"][p, rows, :] = (turn * factor).astype(BF16)
                    elif kind == 1:
                        value = turned(chunk, cosine, sine).astype(BF16)
                        m["kx"][p, placed, :] = value
                        m["kt"][p, :, placed] = value.T
                    else:
                        value = chunk.astype(BF16)
                        m["vx"][p, placed, :] = value
                        m["vt"][p, :, placed] = value.T

        return project

    tail, head = pl.ds(frames, REACH), pl.ds(0, REACH)

    def heads_joined(both, swapped=False):
        step = HD // 2 if swapped else HD
        return jnp.concatenate(
            [
                both[i : i + step, i // step % 2 * BLOCK : (i // step % 2 + 1) * BLOCK]
                for i in range(0, 2 * HD, step)
            ],
            axis=0,
        )

    unit_rows = lax.broadcasted_iota(jnp.int32, (2 * BLOCK, BLOCK), 0)
    unit_lanes = lax.broadcasted_iota(jnp.int32, (2 * BLOCK, BLOCK), 1)
    picks = (lax.rem(unit_rows, BLOCK) == unit_lanes).astype(F32).astype(BF16)

    def block_rows(b):
        return pl.ds(b * BLOCK, BLOCK)

    def block_window(b):
        return pl.ds(b * BLOCK, SPAN)

    def spare(i):
        return m["after"].at[pl.ds(i // 2 * SPAN, SPAN), pl.ds(i % 2 * 2 * BLOCK, 2 * BLOCK)]

    def spare_low(i):
        return m["branch"].at[pl.ds(i // 2 * SPAN, SPAN), pl.ds(i % 2 * 2 * BLOCK, 2 * BLOCK)]

    def attend(p, events):
        def score(b):
            left = jnp.concatenate([m["kx"][p, block_window(b), :], m["bias"][b]], axis=1)
            right = jnp.concatenate([two_heads(m["qx"][p, block_rows(b), :], True), picks], axis=1)
            spare(b % 4)[...] = dot_t(left, right)

        def soften(b):
            scores = spare(b % 4)[...]
            top = jnp.max(scores, axis=0, keepdims=True)
            weights = jnp.exp(scores - top)
            total = jnp.sum(weights, axis=0, keepdims=True)
            m["probs"][p, b] = (weights * (1.0 / total)).astype(BF16)

        def mix(b):
            joined = heads_joined(dot(m["vt"][p, :, block_window(b)], m["probs"][p, b]))
            m["ot"][p * 128 : (p + 1) * 128, block_rows(b)] = joined.astype(BF16)
            mixed[block_rows(b), p * 128 : (p + 1) * 128] = joined.T.astype(BF16)

        in_turn(blocks, (score, soften, mix), events)

    halos = {}

    def send_halo(kind, p):
        ref = m["kx"] if kind == 1 else m["vx"]
        halos[kind, p] = links.single(ref.at[p, tail], ref.at[p, head], "s")
        halos[kind, p].start()

    def take_halo(p):
        for kind, flat, turned_ref in ((1, m["kx"], m["kt"]), (2, m["vx"], m["vt"])):
            halos[kind, p].wait_recv()
            turned_ref[p, :, 0:REACH] = flat[p, 0:REACH, :].T

    for p in range(PAIRS):
        if p < 3:
            run(0, tiles, projection(p))
            for pair in CHUNKS[p]:
                for kind, q in pair:
                    if kind > 0:
                        send_halo(kind, q)
        take_halo(p)
        due("before", p)
        attend(p, {7: [functools.partial(due, "during", p)]} if p == 0 else {})
        due("after", p)

    m["acc"][...] = jnp.zeros_like(m["acc"])
    acc = m["acc"]

    def add_to(i, values):
        acc[i : i + 1, :] = acc[i : i + 1, :] + jnp.sum(values, axis=0, keepdims=True)

    scale_one, gain_two, bias_two, scale_two = vector(2), vector(3), vector(4), vector(5)
    n2 = y_ref
    dba = m["dba"]

    def norm_back(unit, scale, gain, grad):
        inner = grad * gain
        return scale * (
            inner
            - jnp.mean(inner, axis=-1, keepdims=True)
            - unit * jnp.mean(inner * unit, axis=-1, keepdims=True)
        )

    def norm_two(t, _):
        rows = start_of(t, TILE)
        both = mixed[rows, :]
        branch = jnp.concatenate(
            [dot(both, w[OUT, c].reshape(width, COLUMNS)) for c in range(2)], axis=1
        )
        m["branch"][rows, :] = branch.astype(BF16)
        after = x_ref[rows, :].astype(F32) + scale_one * branch
        m["after"][rows, :] = after
        unit, _scale = normalized(after)
        low = (unit * gain_two + bias_two).astype(BF16)
        n2[rows, :] = low
        m["n2t"][:, rows] = low.T
        dbm = (dy_ref[rows, :].astype(F32) * scale_two).astype(BF16)
        dba[0, rows, :] = dbm[:, : width // 2]
        dba[1, rows, :] = dbm[:, width // 2 :]

    run(0, tiles, norm_two, {2: [functools.partial(due, "norm", 2)]})

    def result_of(i):
        def keep(value):
            if i < OUT:
                for j in range(2):
                    gq[:, chunk_columns(i, j)] = ordered(
                        i, j, value[:, j * 128 : (j + 1) * 128]
                    )
            elif i == OUT:
                go[...] = value
            elif i in DOWN:
                q = DOWN.index(i)
                gd[q * piece : (q + 1) * piece, :] = value
            else:
                m["up_sums"][UP.index(i)] = value

        return keep

    sums = {}

    def unit_grads(i, left, right):
        gathers[i].drain()
        if i < OUT:
            sums[DOWN[i]].drain()
        place = DOWN[i] if i < OUT else i
        out, own = w.at[place, 0], m["own"].at[place - 3]
        if i == LAST:
            arrived, kind = [m["s_in"].at[i], m["pieces"]], ScatterDirect
        else:
            at_unit = i - (i > LAST)
            arrived = [m["s_in"].at[i]] + [m[n].at[at_unit] for n in ("c_in", "b_in", "a_in")]
            kind = Scatter
        sums[i] = kind(own, out, arrived, result_of(i), links, at, m["s_in"])
        own[...] = dot(left[...], right[core])
        out[...] = dot(left[...], right[other]).astype(BF16).reshape(4, 2, 2, piece, COLUMNS)
        sums[i].step(0)

    def step_of(i, number):
        return lambda: sums[i].step(number)

    def feed(q):
        def middle(pair, _):
            for t in range(2):
                one(2 * pair + t)

        def one(t):
            rows = start_of(t, TILE)
            ups = [w[UP[q], h].reshape(width, COLUMNS) for h in range(2)]
            dbm = jnp.concatenate([dba[c, rows, :] for c in range(2)], axis=1)
            acts, dus = [], []
            for h in range(2):
                value, slope = gelu_and_slope(dot(n2[rows, :], ups[h]))
                act = value.astype(BF16)
                m["actt"][h * COLUMNS : (h + 1) * COLUMNS, rows] = act.T
                down = jnp.concatenate(
                    [w[DOWN[q], c, 2 * h : 2 * h + 2].reshape(COLUMNS, COLUMNS) for c in range(2)],
                    axis=1,
                )
                du = (dot_t(dbm, down) * slope).astype(BF16)
                m["du"][h, rows, :] = du
                acts.append(act)
                dus.append(du)
            act = jnp.concatenate(acts, axis=1)
            for c in range(2):
                columns = pl.ds(c * COLUMNS, COLUMNS)
                total = dot(act, w[DOWN[q], c].reshape(2 * COLUMNS, COLUMNS))
                if q > 0:
                    total = total + m["branch_two"][rows, columns]
                m["branch_two"][rows, columns] = total
            grad = dot_t(jnp.concatenate(dus, axis=1), jnp.concatenate(ups, axis=1))
            if q > 0:
                grad = grad + m["dx1"][rows, :]
            m["dx1"][rows, :] = grad

        return middle

    def steps_of(q, number):
        return [step_of(DOWN[q], number), step_of(UP[q], number)]

    def do(actions):
        for action in actions:
            action()

    for q in range(4):
        due("feed", q, 0)
        events = {1: [functools.partial(due, "feed", q, 1)]}
        if q > 0:
            events[1] += steps_of(q - 1, 1)
        run(0, tiles // 2, feed(q), events)
        due("feed", q, 2)
        if q > 1:
            do(steps_of(q - 2, 2))
        unit_grads(DOWN[q], m["actt"], dba)
        unit_grads(UP[q], m["n2t"], m["du"])

    def norm_two_back(t, _):
        rows = start_of(t, TILE)
        after, branch_two = m["after"][rows, :], m["branch_two"][rows, :]
        y_ref[rows, :] = (after + scale_two * branch_two).astype(BF16)
        upstream = dy_ref[rows, :].astype(F32)
        add_to(5, upstream * branch_two)
        unit, scale = normalized(after)
        grad = m["dx1"][rows, :]
        add_to(3, grad * unit)
        add_to(4, grad)
        dx1 = upstream + norm_back(unit, scale, gain_two, grad)
        m["dx1"][rows, :] = dx1
        add_to(2, dx1 * m["branch"][rows, :].astype(F32))
        low = (dx1 * scale_one).astype(BF16)
        sides = [low[:, : width // 2], low[:, width // 2 :]]
        for c in range(2):
            dba[c, rows, :] = sides[c]
        dmixed = (
            dot_t(sides[0], w[OUT, 0].reshape(width, COLUMNS))
            + dot_t(sides[1], w[OUT, 1].reshape(width, COLUMNS))
        ).astype(BF16)
        m["n2t"][:, rows] = dmixed.T
        for p in range(PAIRS):
            m["dox"][p, rows, :] = dmixed[:, p * 128 : (p + 1) * 128]

    do(steps_of(0, 3))
    run(
        0,
        tiles,
        norm_two_back,
        {2: steps_of(3, 1)},
    )
    y_send = pltpu.make_async_copy(y_ref, y_out.at[0], moves.at[5])
    y_send.start()
    do(steps_of(2, 2))
    unit_grads(OUT, m["ot"], dba)
    do(steps_of(1, 3))

    dp = m["dp"]
    halfway = [
        [step_of(OUT, 1)],
        steps_of(2, 3) + steps_of(3, 2),
        [step_of(GROUP, 1)],
        [step_of(GROUP + 1, 1)],
    ]
    after_pair = [
        steps_of(0, 4),
        steps_of(1, 4) + [step_of(OUT, 2)],
        steps_of(2, 4) + steps_of(3, 3) + [step_of(OUT, 3)],
        [step_of(GROUP, 2)],
    ]

    def store_turned(kind, p, rows, value):
        g, c, j = place_of(kind, p)
        if kind < 2:
            value = turned(value, m["cos"][rows, :], -m["sin"][rows, :])
        dp[g, c, rows, j * 128 : (j + 1) * 128] = value.astype(BF16)

    backs = []
    for p in range(PAIRS):
        dkx, dvx = m["dkx"], m["dvx"]
        dkx[...] = jnp.zeros_like(dkx)
        dvx[...] = jnp.zeros_like(dvx)

        def probe(b, p=p):
            spare(b % 4)[...] = dot_t(
                m["vx"][p, block_window(b), :], two_heads(m["dox"][p, block_rows(b), :])
            )

        def weigh(b, p=p):
            probs = m["probs"][p, b].astype(F32)
            heads = (pl.ds(p * 128, 128), block_rows(b))
            shared = m["n2t"][heads].astype(F32) * m["ot"][heads].astype(F32)
            balance = jnp.concatenate(
                [
                    jnp.sum(shared[:HD], axis=0, keepdims=True),
                    jnp.sum(shared[HD:], axis=0, keepdims=True),
                ],
                axis=1,
            )
            spare_low(b % 4)[...] = (probs * (spare(b % 4)[...] - balance)).astype(BF16)

        def gather_back(b, p=p):
            window, rows = block_window(b), block_rows(b)
            dscores = spare_low(b % 4)[...]
            dvx[window, :] = dvx[window, :] + dot(
                m["probs"][p, b], two_heads(m["dox"][p, rows, :])
            )
            dkx[window, :] = dkx[window, :] + dot(dscores, two_heads(m["qx"][p, rows, :], True))
            joined = heads_joined(dot(m["kt"][p, :, window], dscores), True).T * factor
            store_turned(0, p, rows, joined)

        h_out, h_in = m["h_out"], m["h_in"]
        halo_back = links.single(h_out.at[p], h_in.at[p], "s")
        backs.append(halo_back)

        def send_back(p=p, halo_back=halo_back):
            h_out[p, 0] = dkx[0:REACH, :].astype(BF16)
            h_out[p, 1] = dvx[0:REACH, :].astype(BF16)
            halo_back.start()

        events = {4: [send_back] + halfway[p]}
        in_turn(blocks, (probe, weigh, gather_back), events)
        halo_back.wait_recv()
        dkx[tail, :] = dkx[tail, :] + h_in[p, 0].astype(F32)
        dvx[tail, :] = dvx[tail, :] + h_in[p, 1].astype(F32)

        def finish(t, _, p=p):
            rows = start_of(t, TILE)
            placed = pl.ds(pl.multiple_of(REACH + t * TILE, TILE), TILE)
            store_turned(1, p, rows, dkx[placed, :])
            store_turned(2, p, rows, dvx[placed, :])

        run(0, tiles, finish)
        do(after_pair[p])
        if p > 0:
            unit_grads(GROUP + p - 1, m["n1t"], dp.at[p - 1])


    def first(t, _):
        rows = start_of(t, TILE)
        sides = [(g, c) for g in range(3) for c in range(2)]
        grad = dot_t(
            jnp.concatenate([dp[g, c, rows, :] for g, c in sides], axis=1),
            jnp.concatenate([w[g, c].reshape(width, COLUMNS) for g, c in sides], axis=1),
        )
        unit, scale = normalized(x_ref[rows, :].astype(F32))
        add_to(0, grad * unit)
        add_to(1, grad)
        mixed[rows, :] = (
            m["dx1"][rows, :] + norm_back(unit, scale, gain_one, grad)
        ).astype(BF16)

    late = {1: [step_of(LAST, 1)], 3: [*steps_of(3, 4), step_of(OUT, 4), step_of(GROUP + 1, 2)]}
    run(0, tiles, first, late)
    sends = [pltpu.make_async_copy(mixed, ig_out.at[0], moves.at[6])]
    sends[0].start()

    v_out, v_in, v_all = m["v_out"], m["v_in"], m["v_all"]
    v_out[...] = acc[:, start_of(other, width // 2)]
    vector_hop = links.single(v_out, v_in, "s")
    vector_hop.start()
    sums[GROUP].step(3)
    vector_hop.wait_recv()
    v_all[row] = acc[:, start_of(core, width // 2)] + v_in[...]
    spread_send, spread_recv = links.slot(), links.slot()
    for k in range(1, 16):
        links.copy(v_all.at[row], v_all.at[row], ("r", k), spread_send, spread_recv).start()
    for j in range(2):
        for a in range(4):
            gu[:, (4 * j + a) * 128 : (4 * j + a + 1) * 128] = regroup(
                [m["up_sums"][q, :, j * 128 : (j + 1) * 128] for q in range(4)], a, True
            )
    sums[GROUP + 1].step(3)
    sums[GROUP].step(4)
    await_bytes(v_all.at[0:15], spread_recv)
    total = v_all[0]
    for r in range(1, 16):
        total = total + v_all[r]
    gv[...] = total
    sums[LAST].step(2)
    sums[GROUP + 1].step(4)
    await_bytes(v_all.at[0:15], spread_send)
    for i, each in sums.items():
        if i not in DOWN[:3]:
            each.drain()
    for each in [vec_copy, seg_copy, *halos.values(), *backs, vector_hop]:
        each.wait_send()
    y_send.wait()
    for each in sends:
        each.wait()


def write_kernel(*refs):
    for source, target in zip(refs[:6], refs[7:13]):
        target[...] = source[...]
    for i, vector in enumerate(refs[13:]):
        vector[...] = refs[6][i : i + 1, :]


def local_staged(
    inputs,
    cotangent,
    segment_ids,
    qkv_weight,
    out_weight,
    up_weight,
    down_weight,
    *vectors,
):
    frames, width = inputs.shape[1:]
    items = scratch_list(frames, width)
    whole = pl.BlockSpec(memory_space=pltpu.VMEM)
    anywhere = pl.BlockSpec(memory_space=pl.ANY)
    shapes = [
        jax.ShapeDtypeStruct(inputs.shape, BF16),
        jax.ShapeDtypeStruct(inputs.shape, BF16),
        *[
            jax.ShapeDtypeStruct(weight.shape, F32)
            for weight in (qkv_weight, out_weight, up_weight, down_weight)
        ],
    ]
    results = pl.pallas_call(
        functools.partial(layer_kernel, [name for name, _, _ in items]),
        out_shape=shapes + [jax.ShapeDtypeStruct((8, width // 2), F32)],
        in_specs=[anywhere] * 2 + [whole] * 2 + [anywhere] * 3 + [whole] * 6,
        out_specs=[anywhere] * 2 + [whole] * 5,
        scratch_shapes=[pltpu.VMEM(shape, kind) for _, shape, kind in items]
        + [pltpu.SemaphoreType.DMA((7,)), pltpu.SemaphoreType.DMA((SLOTS,))],
        compiler_params=pltpu.CompilerParams(
            collective_id=0, has_side_effects=True, vmem_limit_bytes=VMEM_LIMIT
        ),
    )(
        inputs,
        cotangent,
        segment_ids,
        qkv_weight,
        out_weight,
        up_weight,
        down_weight,
        *[v.reshape(1, -1) for v in vectors],
    )
    written = pl.pallas_call(
        write_kernel,
        out_shape=shapes + [jax.ShapeDtypeStruct((1, width // 2), F32)] * 6,
        in_specs=[whole] * 7,
        out_specs=[whole] * 12,
    )(*results)
    return (*written[:6], *[v.reshape(-1) for v in written[6:]])


VMEM_LIMIT = 64 * 2**20


def solution(mesh):
    placed = (
        P("rows", "tm", None),
        P("rows", "tm", None),
        P("rows", "tm"),
        P("rows", "tm"),
        P("rows", "tm"),
        P("rows", "tm"),
        P("rows", "tm"),
        P("tm"),
        P("tm"),
        P("tm"),
        P("tm"),
        P("tm"),
        P("tm"),
    )
    staged = mesh.shape["rows"] == 16 and mesh.shape["tm"] == 2
    return jax.shard_map(
        local_staged if staged else local,
        mesh=mesh,
        in_specs=placed,
        out_specs=(
            P("rows", "tm", None),
            P("rows", "tm", None),
            P("rows", "tm"),
            P("rows", "tm"),
            P("rows", "tm"),
            P("rows", "tm"),
            P("tm"),
            P("tm"),
            P("tm"),
            P("tm"),
            P("tm"),
            P("tm"),
        ),
        check_vma=False,
    )
```

```python
import functools
import math

import jax
import jax.numpy as jnp
from jax import lax
from jax.experimental import pallas as pl
from jax.experimental.pallas import tpu as pltpu
from jax.sharding import PartitionSpec as P

H = 8
HD = 64
WINDOW = 250
REACH = 256
QBLOCK = 512


EPSILON = 1e-05
NEGATIVE = -1e30


def prefix(part, axis, combine, identity):
    place = lax.axis_index(axis)
    gathered = jax.tree.map(lambda a: lax.all_gather(a, axis), part)
    state = jax.tree.map(lambda a, e: jnp.zeros_like(a) + jnp.asarray(e, a.dtype), part, identity)

    def one(turn, state):
        return combine(
            state, jax.tree.map(lambda a: lax.dynamic_index_in_dim(a, turn, 0, False), gathered)
        )

    return lax.fori_loop(0, place, one, state)


def shifted(block, axis, distance):
    devices = range(lax.axis_size(axis))
    route = [(i - distance, i) for i in devices if i - distance in devices]
    return lax.ppermute(block, axis, route)


def layer_norm(values, gain_vec, bias_vec):
    average = jnp.mean(values, axis=-1, keepdims=True)
    centred = values - average
    variance = jnp.mean(centred * centred, axis=-1, keepdims=True)
    return centred * lax.rsqrt(variance + EPSILON) * gain_vec + bias_vec


def gelu_exact(values):
    return jax.nn.gelu(values, approximate=False)


def rotation_tables(positions):
    half_size = HD // 2
    ladder = jnp.arange(half_size, dtype=jnp.float32)
    frequency = jnp.exp(ladder * (-2.0 * math.log(10000.0) / HD))
    angles = positions.astype(jnp.float32)[:, None] * frequency[None, :]
    return (jnp.cos(angles)[:, None, :], jnp.sin(angles)[:, None, :])


def rotate(field, cosine, sine):
    half_size = field.shape[-1] // 2
    former = field[..., :half_size]
    latter = field[..., half_size:]
    return jnp.concatenate(
        [former * cosine - latter * sine, latter * cosine + former * sine], axis=-1
    )


def outer_sum(left, right):
    return lax.dot_general(
        left, right, (((0,), (0,)), ((), ())), preferred_element_type=jnp.float32
    )


def block_allowed(begin, segment, extended_segments, valid_keys):
    offsets = (
        jnp.arange(QBLOCK, dtype=jnp.int32)[:, None]
        - jnp.arange(QBLOCK + REACH, dtype=jnp.int32)[None, :]
        + REACH
    )
    near = (offsets >= 0) & (offsets < WINDOW)
    query_segments = segment[begin : begin + QBLOCK]
    key_segments = extended_segments[begin : begin + QBLOCK + REACH]
    key_valid = valid_keys[begin : begin + QBLOCK + REACH]
    return near & (query_segments[:, None] == key_segments[None, :]) & key_valid[None, :]


def block_scores(query_block, key_window, allowed):
    raw = jnp.einsum(
        "qhd,khd->hqk", query_block, key_window, preferred_element_type=jnp.float32
    ) * (1.0 / math.sqrt(HD))
    return jnp.where(allowed[None], raw, NEGATIVE)


def local(
    inputs,
    cotangent,
    segment_ids,
    qkv_weight,
    out_weight,
    up_weight,
    down_weight,
    norm_gain_one,
    norm_bias_one,
    attn_scale,
    norm_gain_two,
    norm_bias_two,
    mlp_scale,
):
    frames = inputs.shape[1]
    width = inputs.shape[2]
    low_type = jnp.bfloat16
    gathered = (
        lax.all_gather(qkv_weight.astype(low_type), "tm", axis=1, tiled=True),
        lax.all_gather(out_weight.astype(low_type), "tm", axis=1, tiled=True),
        lax.all_gather(up_weight.astype(low_type), "tm", axis=1, tiled=True),
        lax.all_gather(down_weight.astype(low_type), "tm", axis=1, tiled=True),
        lax.all_gather(norm_gain_one.astype(low_type), "tm", axis=0, tiled=True),
        lax.all_gather(norm_bias_one.astype(low_type), "tm", axis=0, tiled=True),
        lax.all_gather(attn_scale.astype(low_type), "tm", axis=0, tiled=True),
        lax.all_gather(norm_gain_two.astype(low_type), "tm", axis=0, tiled=True),
        lax.all_gather(norm_bias_two.astype(low_type), "tm", axis=0, tiled=True),
        lax.all_gather(mlp_scale.astype(low_type), "tm", axis=0, tiled=True),
    )
    w_qkv, w_out, w_up, w_down = (
        lax.all_gather(gathered[0], "rows", axis=0, tiled=True),
        lax.all_gather(gathered[1], "rows", axis=0, tiled=True),
        lax.all_gather(gathered[2], "rows", axis=0, tiled=True),
        lax.all_gather(gathered[3], "rows", axis=0, tiled=True),
    )
    gain_one, bias_one, scale_one, gain_two, bias_two, scale_two = [
        piece.astype(jnp.float32) for piece in gathered[4:]
    ]
    segment = segment_ids[0]
    index = jnp.arange(frames, dtype=jnp.int32)
    last_run = jnp.sum((segment == segment[frames - 1]).astype(jnp.int32), keepdims=True)

    def join_runs(earlier, later):
        extends = (later[1] == frames) & (later[0] == earlier[0])
        joined = jnp.where(extends, earlier[1] + later[1], later[1])
        vacant = later[0] < 0
        return (jnp.where(vacant, earlier[0], later[0]), jnp.where(vacant, earlier[1], joined))

    before_id, before_run = prefix(
        (segment[frames - 1 :], last_run),
        "tm",
        join_runs,
        (jnp.full((1,), -1, jnp.int32), jnp.zeros((1,), jnp.int32)),
    )
    change = jnp.concatenate([jnp.ones((1,), jnp.bool_), segment[1:] != segment[:-1]])
    starts = lax.cummax(jnp.where(change, index, jnp.zeros_like(index)), axis=0)
    positions = index - starts + jnp.where(segment == before_id[0], before_run[0], 0)
    cosine, sine = rotation_tables(positions)
    source = inputs[0].astype(jnp.float32)
    normed_one, norm_one_pull = jax.vjp(layer_norm, source, gain_one, bias_one)
    normed_one_low = normed_one.astype(low_type)
    projected = jnp.dot(normed_one_low, w_qkv, preferred_element_type=jnp.float32)
    queries = rotate(projected[:, :width].reshape(frames, H, HD), cosine, sine).astype(low_type)
    keys_flat = (
        rotate(projected[:, width : 2 * width].reshape(frames, H, HD), cosine, sine)
        .reshape(frames, width)
        .astype(low_type)
    )
    values_flat = projected[:, 2 * width :].astype(low_type)
    got_keys, got_values, got_segments = shifted((keys_flat, values_flat, segment), "tm", 1)
    got_keys = got_keys[frames - REACH :]
    got_values = got_values[frames - REACH :]
    got_segments = got_segments[frames - REACH :]
    extended_keys = jnp.concatenate([got_keys, keys_flat], axis=0).reshape(REACH + frames, H, HD)
    extended_values = jnp.concatenate([got_values, values_flat], axis=0).reshape(
        REACH + frames, H, HD
    )
    extended_segments = jnp.concatenate([got_segments, segment])
    valid_keys = (lax.axis_index("tm") > 0) | (jnp.arange(REACH + frames, dtype=jnp.int32) >= REACH)
    block_count = frames // QBLOCK
    mixed_parts = []
    log_sums = []
    for block in range(block_count):
        begin = block * QBLOCK
        allowed = block_allowed(begin, segment, extended_segments, valid_keys)
        scores = block_scores(
            queries[begin : begin + QBLOCK], extended_keys[begin : begin + QBLOCK + REACH], allowed
        )
        top = jnp.max(scores, axis=-1, keepdims=True)
        weights = jnp.exp(scores - top)
        total = jnp.sum(weights, axis=-1, keepdims=True)
        probs = (weights / total).astype(low_type)
        mixed_parts.append(
            jnp.einsum(
                "hqk,khd->qhd",
                probs,
                extended_values[begin : begin + QBLOCK + REACH],
                preferred_element_type=jnp.float32,
            )
        )
        log_sums.append(top + jnp.log(total))
    mixed_low = jnp.concatenate(mixed_parts, axis=0).reshape(frames, width).astype(low_type)
    branch = jnp.dot(mixed_low, w_out, preferred_element_type=jnp.float32)
    after = source + scale_one * branch
    normed_two, norm_two_pull = jax.vjp(layer_norm, after, gain_two, bias_two)
    normed_two_low = normed_two.astype(low_type)
    hidden = jnp.dot(normed_two_low, w_up, preferred_element_type=jnp.float32)
    active, gelu_pull = jax.vjp(gelu_exact, hidden)
    active_low = active.astype(low_type)
    branch_two = jnp.dot(active_low, w_down, preferred_element_type=jnp.float32)
    result = (after + scale_two * branch_two).astype(low_type)
    again = (
        lax.all_gather(qkv_weight.astype(low_type), "tm", axis=1, tiled=True),
        lax.all_gather(out_weight.astype(low_type), "tm", axis=1, tiled=True),
        lax.all_gather(up_weight.astype(low_type), "tm", axis=1, tiled=True),
        lax.all_gather(down_weight.astype(low_type), "tm", axis=1, tiled=True),
    )
    back_qkv, back_out, back_up, back_down = (
        lax.all_gather(again[0], "rows", axis=0, tiled=True),
        lax.all_gather(again[1], "rows", axis=0, tiled=True),
        lax.all_gather(again[2], "rows", axis=0, tiled=True),
        lax.all_gather(again[3], "rows", axis=0, tiled=True),
    )
    upstream = cotangent[0].astype(jnp.float32)
    grad_scale_two = jnp.sum(upstream * branch_two, axis=0)
    grad_branch_two = (upstream * scale_two).astype(low_type)
    grad_down = outer_sum(active_low, grad_branch_two)
    grad_active = lax.dot_general(
        grad_branch_two, back_down, (((1,), (1,)), ((), ())), preferred_element_type=jnp.float32
    )
    grad_hidden = gelu_pull(grad_active)[0].astype(low_type)
    grad_up = outer_sum(normed_two_low, grad_hidden)
    grad_normed_two = lax.dot_general(
        grad_hidden, back_up, (((1,), (1,)), ((), ())), preferred_element_type=jnp.float32
    )
    after_part, grad_gain_two, grad_bias_two = norm_two_pull(grad_normed_two)
    grad_after = upstream + after_part
    grad_scale_one = jnp.sum(grad_after * branch, axis=0)
    grad_branch = (grad_after * scale_one).astype(low_type)
    grad_out = outer_sum(mixed_low, grad_branch)
    grad_mixed = lax.dot_general(
        grad_branch, back_out, (((1,), (1,)), ((), ())), preferred_element_type=jnp.float32
    )
    grad_mixed = grad_mixed.astype(low_type).reshape(frames, H, HD)
    factor = 1.0 / math.sqrt(HD)
    grad_keys_ext = jnp.zeros((REACH + frames, H, HD), jnp.float32)
    grad_values_ext = jnp.zeros((REACH + frames, H, HD), jnp.float32)
    query_grads = []
    for block in range(block_count):
        begin = block * QBLOCK
        allowed = block_allowed(begin, segment, extended_segments, valid_keys)
        query_block = queries[begin : begin + QBLOCK]
        key_window = extended_keys[begin : begin + QBLOCK + REACH]
        value_window = extended_values[begin : begin + QBLOCK + REACH]
        scores = block_scores(query_block, key_window, allowed)
        probs_full = jnp.exp(scores - log_sums[block])
        probs_low = probs_full.astype(low_type)
        grad_out_block = grad_mixed[begin : begin + QBLOCK]
        grad_probs = jnp.einsum(
            "qhd,khd->hqk", grad_out_block, value_window, preferred_element_type=jnp.float32
        )
        grad_values_ext = grad_values_ext.at[begin : begin + QBLOCK + REACH].add(
            jnp.einsum(
                "hqk,qhd->khd", probs_low, grad_out_block, preferred_element_type=jnp.float32
            )
        )
        balance = jnp.sum(grad_probs * probs_full, axis=-1, keepdims=True)
        grad_scores = (probs_full * (grad_probs - balance)).astype(low_type)
        query_grads.append(
            jnp.einsum("hqk,khd->qhd", grad_scores, key_window, preferred_element_type=jnp.float32)
            * factor
        )
        grad_keys_ext = grad_keys_ext.at[begin : begin + QBLOCK + REACH].add(
            jnp.einsum("hqk,qhd->khd", grad_scores, query_block, preferred_element_type=jnp.float32)
            * factor
        )
    grad_keys_flat = grad_keys_ext.reshape(REACH + frames, width)
    grad_values_flat = grad_values_ext.reshape(REACH + frames, width)
    back_keys, back_values = (
        shifted(grad_keys_flat[:REACH].astype(jnp.bfloat16), "tm", -1).astype(jnp.float32),
        shifted(grad_values_flat[:REACH].astype(jnp.bfloat16), "tm", -1).astype(jnp.float32),
    )
    own_keys = grad_keys_flat[REACH:]
    own_values = grad_values_flat[REACH:]
    own_keys = jnp.concatenate(
        [own_keys[: frames - REACH], own_keys[frames - REACH :] + back_keys], axis=0
    )
    own_values = jnp.concatenate(
        [own_values[: frames - REACH], own_values[frames - REACH :] + back_values], axis=0
    )
    grad_queries = rotate(jnp.concatenate(query_grads, axis=0), cosine, -sine).reshape(
        frames, width
    )
    grad_keys = rotate(own_keys.reshape(frames, H, HD), cosine, -sine).reshape(frames, width)
    grad_projected = jnp.concatenate([grad_queries, grad_keys, own_values], axis=1).astype(low_type)
    grad_qkv = outer_sum(normed_one_low, grad_projected)
    grad_normed_one = lax.dot_general(
        grad_projected, back_qkv, (((1,), (1,)), ((), ())), preferred_element_type=jnp.float32
    )
    source_part, grad_gain_one, grad_bias_one = norm_one_pull(grad_normed_one)
    input_grad = (grad_after + source_part).astype(low_type)
    reduced = (
        lax.psum_scatter(grad_qkv, "tm", scatter_dimension=1, tiled=True),
        lax.psum_scatter(grad_out, "tm", scatter_dimension=1, tiled=True),
        lax.psum_scatter(grad_up, "tm", scatter_dimension=1, tiled=True),
        lax.psum_scatter(grad_down, "tm", scatter_dimension=1, tiled=True),
        lax.psum_scatter(grad_gain_one, "tm", scatter_dimension=0, tiled=True),
        lax.psum_scatter(grad_bias_one, "tm", scatter_dimension=0, tiled=True),
        lax.psum_scatter(grad_scale_one, "tm", scatter_dimension=0, tiled=True),
        lax.psum_scatter(grad_gain_two, "tm", scatter_dimension=0, tiled=True),
        lax.psum_scatter(grad_bias_two, "tm", scatter_dimension=0, tiled=True),
        lax.psum_scatter(grad_scale_two, "tm", scatter_dimension=0, tiled=True),
    )
    qkv_grad, out_grad, up_grad, down_grad = (
        lax.psum_scatter(reduced[0], "rows", scatter_dimension=0, tiled=True),
        lax.psum_scatter(reduced[1], "rows", scatter_dimension=0, tiled=True),
        lax.psum_scatter(reduced[2], "rows", scatter_dimension=0, tiled=True),
        lax.psum_scatter(reduced[3], "rows", scatter_dimension=0, tiled=True),
    )
    vector_sums = lax.psum(
        (reduced[4], reduced[5], reduced[6], reduced[7], reduced[8], reduced[9]), "rows"
    )
    return (
        result[None],
        input_grad[None],
        qkv_grad,
        out_grad,
        up_grad,
        down_grad,
        vector_sums[0],
        vector_sums[1],
        vector_sums[2],
        vector_sums[3],
        vector_sums[4],
        vector_sums[5],
    )


MESH_IDS = pl.DeviceIdType.MESH
F32 = jnp.float32
BF16 = jnp.bfloat16


def dot(left, right, contract=((1,), (0,))):
    return lax.dot_general(left, right, (contract, ((), ())), preferred_element_type=F32)


def dot_t(left, right):
    return dot(left, right, ((1,), (1,)))


def start_of(index, size):
    return pl.ds(pl.multiple_of(index * size, size), size)


def coordinates():
    row, core = lax.axis_index("rows"), lax.axis_index("tm")
    return row, core, lax.rem(row, 2), lax.rem(lax.div(row, 2), 2), lax.div(row, 4)


def peers_of(at):
    row, core, x, y, z = at
    found = {
        "x": (row + 1 - 2 * x, core),
        "y": (row + 2 - 4 * y, core),
        "s": (row, 1 - core),
    }
    for k in (1, 2, 3):
        found[k] = (lax.rem(z + k, 4) * 4 + lax.rem(row, 4), core)
    found["xy"] = (row + 3 - 2 * x - 4 * y, core)
    for k in range(1, 16):
        found["r", k] = (lax.rem(row + k, 16), core)
    return found


def greet(peers):
    for name in ["s"] + [("r", k) for k in range(1, 16)]:
        pl.semaphore_signal(
            pltpu.get_barrier_semaphore(), inc=1, device_id=peers[name], device_id_type=MESH_IDS
        )


def be_greeted():
    pl.semaphore_wait(pltpu.get_barrier_semaphore(), 16)


class Links:
    def __init__(self, sems, peers):
        self.sems, self.peers, self.used = sems, peers, 0

    def slot(self):
        self.used += 1
        return self.sems.at[self.used - 1]

    def copy(self, src, dst, peer, send, recv):
        return pltpu.make_async_remote_copy(
            src_ref=src,
            dst_ref=dst,
            send_sem=send,
            recv_sem=recv,
            device_id=self.peers[peer],
            device_id_type=MESH_IDS,
        )

    def single(self, src, dst, peer):
        return self.copy(src, dst, peer, self.slot(), self.slot())


def await_bytes(like, sem):
    pltpu.make_async_copy(like, like, sem).wait()


class Gather:
    def __init__(self, units, i, links, at):
        full = units.at[i]
        row, core, x, y, z = at
        half = full.shape[4] // 2
        low, high = pl.ds(0, half), pl.ds(half, half)
        every = slice(None)
        near, far = links.slot(), links.slot()
        got = [links.slot() for _ in range(4)]

        def copy(where, peer, send, recv):
            return links.copy(full.at[where], full.at[where], peer, send, recv)

        self.starts = (
            [copy((core, z, y, x), k, near, got[0]) for k in (1, 2, 3)],
            [
                copy((core, every, y, x, low), "x", far, got[1]),
                copy((core, every, y, x, high), "y", far, got[1]),
                copy((core, every, y, x), "s", far, got[3]),
            ],
            [
                copy((core, every, y, every, low), "y", far, got[2]),
                copy((core, every, every, x, high), "x", far, got[2]),
                copy((core, every, y, 1 - x, low), "s", far, got[3]),
                copy((core, every, 1 - y, x, high), "s", far, got[3]),
            ],
            [
                copy((core, every, 1 - y, every, low), "s", far, got[3]),
                copy((core, every, every, 1 - x, high), "s", far, got[3]),
            ],
            [],
        )
        self.waits = (
            None,
            (full.at[core, 0:3, y, x], got[0]),
            (full.at[core, :, y, x], got[1]),
            (full.at[core, :, y], got[2]),
            (full.at[1 - core], got[3]),
        )
        self.sent = ((full.at[core, 0:3, y, x], near), (units.at[0:7, 0, 0], far))

    def step(self, number):
        if number > 0:
            await_bytes(*self.waits[number])
        for copy in self.starts[number]:
            copy.start()

    def drain(self):
        for like, sem in self.sent:
            await_bytes(like, sem)


class GatherDirect:
    def __init__(self, units, i, links, at):
        full = units.at[i]
        row, core, x, y, z = at
        piece = full.at[core, z, y, x]
        self.sent, self.got, passed, self.whole = [links.slot() for _ in range(4)]
        self.starts = [
            links.copy(piece, piece, ("r", k), self.sent, self.got) for k in range(1, 16)
        ]
        self.over = links.copy(full.at[core], full.at[core], "s", passed, self.whole)
        self.fifteen = units.at[0:5, 0, 0:3, 0, 0]

    def step(self, number):
        if number == 0:
            for copy in self.starts:
                copy.start()
        if number == 1:
            await_bytes(self.fifteen, self.got)
            self.over.start()
        if number == 2:
            self.over.wait_recv()

    def drain(self):
        await_bytes(self.fifteen, self.sent)
        self.over.wait_send()


class GatherPlane:
    def __init__(self, units, i, links, at):
        full = units.at[i]
        row, core, x, y, z = at
        every = slice(None)
        near, far = links.slot(), links.slot()
        got = [links.slot() for _ in range(3)]

        def copy(where, peer, send, recv):
            return links.copy(full.at[where], full.at[where], peer, send, recv)

        column = (core, every, y, x)
        self.starts = (
            [copy((core, z, y, x), k, near, got[0]) for k in (1, 2, 3)],
            [copy(column, peer, far, got[1]) for peer in ("xy", "x", "y")]
            + [copy(column, "s", far, got[2])],
            [
                copy((core, every, y, 1 - x), "s", far, got[2]),
                copy((core, every, 1 - y), "s", far, got[2]),
            ],
            [],
        )
        self.waits = (
            None,
            (full.at[core, 0:3, y, x], got[0]),
            (units.at[0:3, 0, :, 0, 0], got[1]),
            (full.at[1 - core], got[2]),
        )
        self.sent = ((full.at[core, 0:3, y, x], near), (units.at[0:7, 0, 0], far))

    def step(self, number):
        if number > 0:
            await_bytes(*self.waits[number])
        for copy in self.starts[number]:
            copy.start()

    def drain(self):
        for like, sem in self.sent:
            await_bytes(like, sem)


class Scatter:
    def __init__(self, own, out, arrived, result, links, at, units):
        self.own, self.out, self.result, self.at = own, out, result, at
        self.s_in, self.c_in, self.b_in, self.a_in = arrived
        row, core, x, y, z = at
        self.rows = out.shape[3]
        half = self.half = self.rows // 2
        low, high = self.low, self.high = pl.ds(0, half), pl.ds(half, half)
        every = slice(None)
        self.d = links.single(out, self.s_in, "s")
        self.far = links.slot()
        self.got = [links.slot() for _ in range(3)]
        self.units = units

        def copy(src, dst, peer, which):
            return links.copy(src, dst, peer, self.far, self.got[which])

        self.c1 = copy(out.at[every, 1 - y, every, low], self.c_in.at[0], "y", 0)
        self.c2 = copy(out.at[every, every, 1 - x, high], self.c_in.at[1], "x", 0)
        self.b1 = copy(out.at[every, y, 1 - x, low], self.b_in.at[0], "x", 1)
        self.b2 = copy(out.at[every, 1 - y, x, high], self.b_in.at[1], "y", 1)
        self.a = [
            copy(out.at[lax.rem(z + k, 4), y, x], self.a_in.at[k - 1], k, 2) for k in (1, 2, 3)
        ]

    def mine(self, k, y, x, part):
        begin = ((k * 2 + y) * 2 + x) * self.rows + part * self.half
        return self.own[pl.ds(pl.multiple_of(begin, self.half), self.half), :] + self.s_in[
            k, y, x, pl.ds(part * self.half, self.half)
        ].astype(F32)

    def column(self, k, part):
        row, core, x, y, z = self.at
        place = x if part == 0 else y
        return (
            self.mine(k, y, x, part)
            + self.c_in[part, k, place].astype(F32)
            + self.b_in[part, k].astype(F32)
        )

    def step(self, number):
        row, core, x, y, z = self.at
        low, high, out = self.low, self.high, self.out
        c_in = self.c_in
        if number == 0:
            self.d.start()
        if number == 1:
            self.d.wait()
            for k in range(4):
                for i in range(2):
                    out[k, 1 - y, i, low] = self.mine(k, 1 - y, i, 0).astype(BF16)
            self.c1.start()
            for k in range(4):
                for i in range(2):
                    out[k, i, 1 - x, high] = self.mine(k, i, 1 - x, 1).astype(BF16)
            self.c2.start()
        if number == 2:
            await_bytes(c_in, self.got[0])
            for k in range(4):
                out[k, y, 1 - x, low] = (
                    self.mine(k, y, 1 - x, 0) + c_in[0, k, 1 - x].astype(F32)
                ).astype(BF16)
            self.b1.start()
            for k in range(4):
                out[k, 1 - y, x, high] = (
                    self.mine(k, 1 - y, x, 1) + c_in[1, k, 1 - y].astype(F32)
                ).astype(BF16)
            self.b2.start()
        if number == 3:
            await_bytes(self.b_in, self.got[1])
            for k in (1, 2, 3):
                there = lax.rem(z + k, 4)
                out[there, y, x, low] = self.column(there, 0).astype(BF16)
                out[there, y, x, high] = self.column(there, 1).astype(BF16)
                self.a[k - 1].start()
            self.own[low, :] = self.column(z, 0)
            self.own[high, :] = self.column(z, 1)
        if number == 4:
            await_bytes(self.a_in, self.got[2])
            self.result(
                self.own[: self.rows, :]
                + (self.a_in[0].astype(F32) + self.a_in[1].astype(F32) + self.a_in[2].astype(F32))
            )

    def drain(self):
        await_bytes(self.units.at[0:5, 0:3, 0, 0], self.far)


class ScatterDirect(Scatter):
    def __init__(self, own, out, arrived, result, links, at, units):
        self.own, self.out, self.result, self.at = own, out, result, at
        self.s_in, self.pieces = arrived
        row, core, x, y, z = at
        self.rows = out.shape[3]
        self.half = self.rows // 2
        self.units = units
        self.d = links.single(out, self.s_in, "s")
        self.far, self.got = links.slot(), links.slot()
        self.copies = []
        for k in range(1, 16):
            there = lax.rem(row + k, 16)
            where = (lax.div(there, 4), lax.rem(lax.div(there, 2), 2), lax.rem(there, 2))
            made = links.copy(out.at[where], self.pieces.at[k - 1], ("r", k), self.far, self.got)
            self.copies.append((where, made))

    def whole(self, z, y, x):
        return jnp.concatenate([self.mine(z, y, x, part) for part in range(2)], axis=0)

    def step(self, number):
        row, core, x, y, z = self.at
        if number == 0:
            self.d.start()
        if number == 1:
            self.d.wait()
            for where, copy in self.copies:
                self.out[where] = self.whole(*where).astype(BF16)
                copy.start()
            self.own[: self.rows, :] = self.whole(z, y, x)
        if number == 2:
            await_bytes(self.pieces, self.got)
            total = self.own[: self.rows, :]
            for k in range(15):
                total = total + self.pieces[k].astype(F32)
            self.result(total)


def gelu_and_slope(values):
    cdf = 0.5 + 0.5 * lax.erf(values * math.sqrt(0.5))
    bell = jnp.exp2((values * values) * (-0.5 * math.log2(math.e)))
    return values * cdf, cdf + (values * (1.0 / math.sqrt(2.0 * math.pi))) * bell


def lane_pattern(shape, size):
    return lax.rem(lax.broadcasted_iota(jnp.int32, shape, len(shape) - 1), size)


def turned(values, cosine, sine):
    return values * cosine + pltpu.roll(values, 64, 1) * sine


def swap_middle(values):
    group = lane_pattern((1, 128), 128) // 32
    return jnp.where(
        group == 1,
        pltpu.roll(values, 96, 1),
        jnp.where(group == 2, pltpu.roll(values, 32, 1), values),
    )


TILE = 256
BLOCK = 128
SPAN = BLOCK + REACH
PAIRS = H // 2
COLUMNS = 256
UNITS = 12
GROUP, OUT, DOWN, UP = 0, 3, (4, 6, 8, 10), (5, 7, 9, 11)
D0, U0, D1, U1, D2, U2, D3, U3 = range(4, 12)
DUE = {
    "tables": ((1, 1),),
    "masks": ((0, 1), (2, 1), (OUT, 0), (D0, 0), (0, 2)),
    ("before", 0): ((OUT, 1), (U0, 0)),
    ("during", 0): ((1, 2),),
    ("after", 0): ((1, 3), (D0, 1), (D1, 0)),
    ("before", 1): ((2, 2), (OUT, 2), (U0, 1), (U1, 0)),
    ("after", 1): ((2, 3), (D0, 2), (D1, 1), (D2, 0)),
    ("before", 2): ((OUT, 3), (U0, 2), (U1, 1), (U2, 0)),
    ("after", 2): ((OUT, 4), (D0, 3), (D1, 2), (D2, 1), (D3, 0)),
    ("after", 3): ((D0, 4), (U0, 3), (U1, 2), (U2, 1), (U3, 0)),
    ("norm", 2): ((D2, 2),),
    ("feed", 0, 0): ((U0, 4), (D1, 3), (D3, 1)),
    ("feed", 0, 1): ((D1, 4), (U1, 3), (U2, 2), (U3, 1)),
    ("feed", 0, 2): ((D2, 3), (D3, 2)),
    ("feed", 1, 0): ((U1, 4), (D2, 4)),
    ("feed", 1, 1): ((U2, 3), (U3, 2)),
    ("feed", 1, 2): ((D3, 3), (U2, 4)),
    ("feed", 2, 0): ((D3, 4),),
    ("feed", 2, 1): ((U3, 3),),
    ("feed", 2, 2): ((U3, 4),),
}
LAST = 2
CHUNKS = (
    (((0, 0), (1, 0)), ((2, 0), (2, 1))),
    (((0, 1), (1, 1)), ((2, 2), (1, 2))),
    (((0, 2), (0, 3)), ((2, 3), (1, 3))),
)


def place_of(kind, p):
    for g, cores in enumerate(CHUNKS):
        for c, pair in enumerate(cores):
            if (kind, p) in pair:
                return g, c, pair.index((kind, p))


def run(begin, end, body, events=None):
    def with_events(i, carried):
        for when, actions in sorted((events or {}).items()):

            @pl.when(i == when)
            def _(actions=actions):
                for action in actions:
                    action()

        body(i, carried)
        return 0

    lax.fori_loop(begin, end, with_events, 0)


def in_turn(items, stages, events):
    for i in range(len(items) + len(stages) - 1):
        for action in events.get(i, []):
            action()
        for late, stage in enumerate(stages):
            if 0 <= i - late < len(items):
                stage(items[i - late])


def in_pairs(body):
    def both(i, carried):
        body(2 * i, carried)
        body(2 * i + 1, carried)

    return both


def regroup(tiles, quarter, back=False):
    group = lax.broadcasted_iota(jnp.int32, (1, 128), 1) // 32
    out = jnp.zeros_like(tiles[0])
    for a in range(4):
        out = jnp.where(group == a, pltpu.roll(tiles[a], (a - quarter) * 32 % 128, 1), out)
    return out


def scratch_list(frames, width):
    blocks = frames // BLOCK
    ext = REACH + frames
    unit = (4, 2, 2, width // 16, COLUMNS)
    half = width // 32
    return [
        ("x", (frames, width), BF16),
        ("dy", (frames, width), BF16),
        ("y", (frames, width), BF16),
        ("mixed", (frames, width), BF16),
        ("wo", (width // 16, width // 2), F32),
        ("wu", (width // 16, 2 * width), F32),
        ("wd", (width // 4, width // 2), F32),
        ("w", (UNITS, 2) + unit, BF16),
        ("pos", (8, frames), F32),
        ("vecs", (2, 8, width // 2), F32),
        ("segs", (2, 8, frames), F32),
        ("n1t", (width, frames), BF16),
        ("cos", (frames, 128), F32),
        ("sin", (frames, 128), F32),
        ("bias", (blocks, SPAN, BLOCK), BF16),
        ("qx", (PAIRS, frames, 128), BF16),
        ("kx", (PAIRS, ext, 128), BF16),
        ("vx", (PAIRS, ext, 128), BF16),
        ("kt", (PAIRS, 128, ext), BF16),
        ("vt", (PAIRS, 128, ext), BF16),
        ("probs", (PAIRS, blocks, SPAN, 2 * BLOCK), BF16),
        ("ot", (width, frames), BF16),
        ("n2t", (width, frames), BF16),
        ("actt", (2 * COLUMNS, frames), BF16),
        ("du", (2, frames, COLUMNS), BF16),
        ("after", (frames, width), F32),
        ("branch", (frames, width), BF16),
        ("branch_two", (frames, width), F32),
        ("dx1", (frames, width), F32),
        ("dba", (2, frames, width // 2), BF16),
        ("dox", (PAIRS, frames, 128), BF16),
        ("dp", (3, 2, frames, COLUMNS), BF16),
        ("dkx", (ext, 128), F32),
        ("dvx", (ext, 128), F32),
        ("h_out", (PAIRS, 2, REACH, 128), BF16),
        ("h_in", (PAIRS, 2, REACH, 128), BF16),
        ("acc", (8, width), F32),
        ("v_out", (8, width // 2), F32),
        ("v_in", (8, width // 2), F32),
        ("v_all", (16, 8, width // 2), F32),
        ("pieces", (15, width // 16, COLUMNS), BF16),
        ("own", (UNITS - 3, width, COLUMNS), F32),
        ("up_sums", (4, width // 16, COLUMNS), F32),
        ("s_in", (UNITS,) + unit, BF16),
        ("c_in", (UNITS - 1, 2, 4, 2, half, COLUMNS), BF16),
        ("b_in", (UNITS - 1, 2, 4, half, COLUMNS), BF16),
        ("a_in", (UNITS - 1, 3, width // 16, COLUMNS), BF16),
    ]


SLOTS = 12 * UNITS + 2 * (2 + 2 * PAIRS + PAIRS) + 4


def layer_kernel(names, *refs):
    seg_ref, wq_shard = refs[2:4]
    vectors = refs[7:13]
    y_out, ig_out, gq, go, gu, gd, gv = refs[13:20]
    m = dict(zip(names, refs[20:-2]))
    x_ref, dy_ref, y_ref, mixed = m["x"], m["dy"], m["y"], m["mixed"]
    wo_shard, wu_shard, wd_shard = m["wo"], m["wu"], m["wd"]
    moves = refs[-2]
    loads = [
        pltpu.make_async_copy(source, target, moves.at[i])
        for i, (source, target) in enumerate(
            (
                (refs[0].at[0], x_ref),
                (refs[4], wo_shard),
                (refs[5], wu_shard),
                (refs[6], wd_shard),
                (refs[1].at[0], dy_ref),
            )
        )
    ]
    at = coordinates()
    row, core, x, y, z = at
    peers = peers_of(at)
    links = Links(refs[-1], peers)
    frames, width = x_ref.shape
    piece = width // 16
    blocks, tiles = frames // BLOCK, frames // TILE
    factor = 1.0 / math.sqrt(HD)
    w = m["w"]
    other = 1 - core

    def chunk_columns(g, j):
        offsets = []
        for c in range(2):
            kind, p = CHUNKS[g][c][j]
            offsets.append((kind * PAIRS + p - 6 * c) * 128)
        begin = offsets[0] + core * (offsets[1] - offsets[0])
        return pl.ds(pl.multiple_of(begin, 128), 128)

    def ordered(g, j, value):
        kinds = [CHUNKS[g][c][j][0] for c in range(2)]
        if kinds == [2, 2]:
            return value
        swapped = swap_middle(value)
        if 2 not in kinds:
            return swapped
        return jnp.where(core == kinds.index(2), value, swapped)

    greet(peers)
    for load in loads:
        load.start()
    for g in range(3):
        for j in range(2):
            w[g, core, z, y, x, :, j * 128 : (j + 1) * 128] = ordered(
                g, j, wq_shard[:, chunk_columns(g, j)]
            ).astype(BF16)
    m["vecs"][core] = jnp.concatenate(
        [v[...].astype(BF16).astype(F32) for v in vectors]
        + [jnp.zeros((2, width // 2), F32)],
        axis=0,
    )
    m["segs"][core] = jnp.broadcast_to(seg_ref[...].astype(F32), (8, frames))
    be_greeted()
    vec_copy = links.single(m["vecs"].at[core], m["vecs"].at[core], "s")
    seg_copy = links.single(m["segs"].at[core], m["segs"].at[core], "s")
    kinds = [GatherDirect, GatherPlane, GatherPlane] + [Gather] * (UNITS - 3)
    gathers = [kind(w, i, links, at) for i, kind in enumerate(kinds)]

    def due(*where):
        for i, step in DUE.get(where if len(where) > 1 else where[0], ()):
            gathers[i].step(step)

    vec_copy.start()
    seg_copy.start()
    for i in (0, 1, 2):
        gathers[i].step(0)
    for load in loads:
        load.wait()
    w[OUT, core, z, y, x] = wo_shard[...].astype(BF16)
    for q in range(4):
        w[DOWN[q], core, z, y, x] = wd_shard[q * piece : (q + 1) * piece, :].astype(BF16)
    for q in range(4):
        for j in range(2):
            made = regroup(
                [wu_shard[:, (4 * j + a) * 128 : (4 * j + a + 1) * 128] for a in range(4)], q
            )
            w[UP[q], core, z, y, x, :, j * 128 : (j + 1) * 128] = made.astype(BF16)

    def vector(i):
        return jnp.concatenate([m["vecs"][0, i : i + 1, :], m["vecs"][1, i : i + 1, :]], axis=1)

    def normalized(values):
        average = jnp.mean(values, axis=-1, keepdims=True)
        centred = values - average
        variance = jnp.mean(centred * centred, axis=-1, keepdims=True)
        scale = lax.rsqrt(variance + EPSILON)
        return centred * scale, scale

    vec_copy.wait_recv()
    n1 = y_ref
    gain_one, bias_one = vector(0), vector(1)

    def norm_one(t, _):
        rows = start_of(t, TILE)
        unit, _scale = normalized(x_ref[rows, :].astype(F32))
        low = (unit * gain_one + bias_one).astype(BF16)
        n1[rows, :] = low
        m["n1t"][:, rows] = low.T

    run(0, tiles, norm_one)

    seg_copy.wait_recv()
    segs = m["segs"]
    index = lax.broadcasted_iota(jnp.int32, (8, frames), 1)
    order = index.astype(F32)

    def starts_in(which):
        line = segs[which]
        change = (line != pltpu.roll(line, 1, 1)) | (index == 0)
        begun = jnp.where(change, order, 0.0)
        reach = 1
        while reach < frames:
            begun = jnp.maximum(begun, jnp.where(index >= reach, pltpu.roll(begun, reach, 1), 0.0))
            reach *= 2
        return begun

    running = (core > 0) & (segs[core] == segs[other][:, frames - 1 :])
    before = starts_in(other)[:, frames - 1 :]
    m["pos"][...] = order - jnp.where(
        running, before - (core * frames).astype(F32), starts_in(core)
    )
    seg_blocks = m["own"]

    def across(line):
        return jnp.broadcast_to(line, (BLOCK, BLOCK)).T

    def spread(which, begin):
        return across(segs[which, 0:1, begin : begin + BLOCK])

    def seg_place(e):
        return (e // 8, pl.ds((e % 8) // 2 * BLOCK, BLOCK), pl.ds(e % 2 * BLOCK, BLOCK))

    group = lane_pattern((1, 128), 128) // 32
    lanes = lane_pattern((1, 128), HD // 2).astype(F32)
    frequency = jnp.exp(lanes * (-2.0 * math.log(10000.0) / HD))
    near_half = lane_pattern((1, 128), 128) < HD
    quarter = frames // 4
    for i in range(quarter // BLOCK):
        position = across(m["pos"][0:1, i * BLOCK : (i + 1) * BLOCK])
        for a in range(1, 4):
            begin = a * quarter + i * BLOCK
            position = jnp.where(
                group == a, across(m["pos"][0:1, begin : begin + BLOCK]), position
            )
        angle = position * frequency
        for name, table in (("cos", jnp.cos(angle)), ("sin", jnp.sin(angle))):
            for a in range(4):
                begin = a * quarter + i * BLOCK
                wide = jnp.where(group == a, table, 0.0)
                wide = wide + pltpu.roll(wide, 32, 1)
                wide = wide + pltpu.roll(wide, 64, 1)
                if name == "sin":
                    wide = jnp.where(near_half, -wide, wide)
                m[name][begin : begin + BLOCK, :] = wide

    for e in range(REACH // BLOCK):
        halo = spread(other, frames - REACH + e * BLOCK)
        seg_blocks[seg_place(e)] = jnp.where(core > 0, halo, -1.0)
    for b in range(blocks):
        seg_blocks[seg_place(REACH // BLOCK + b)] = spread(core, b * BLOCK)
    due("tables")
    distance = (
        lax.broadcasted_iota(jnp.int32, (SPAN, BLOCK), 1)
        - lax.broadcasted_iota(jnp.int32, (SPAN, BLOCK), 0)
        + REACH
    )
    near = (distance >= 0) & (distance < WINDOW)
    for b in range(blocks):
        keys = jnp.concatenate([seg_blocks[seg_place(b + i)] for i in range(SPAN // BLOCK)], axis=0)
        line = segs[core, 0:1, b * BLOCK : (b + 1) * BLOCK]
        m["bias"][b] = jnp.where(near & (keys == line), 0.0, NEGATIVE).astype(BF16)
    due("masks")

    def two_heads(value, swapped=False):
        first = lax.rem(group, 2) == 0 if swapped else group < 2
        zero = jnp.zeros_like(value)
        return jnp.concatenate(
            [jnp.where(first, value, zero), jnp.where(first, zero, value)], axis=0
        )

    def projection(g):
        def project(t, _):
            rows = start_of(t, TILE)
            placed = pl.ds(pl.multiple_of(REACH + t * TILE, TILE), TILE)
            left = n1[rows, :]
            cosine, sine = m["cos"][rows, :], m["sin"][rows, :]
            for c in range(2):
                wide = dot(left, w[g, c].reshape(width, COLUMNS))
                for j in range(2):
                    chunk = wide[:, j * 128 : (j + 1) * 128]
                    kind, p = CHUNKS[g][c][j]
                    if kind == 0:
                        turn = turned(chunk, cosine, sine).astype(BF16)
                        m["qx"][p, rows, :] = (turn * factor).astype(BF16)
                    elif kind == 1:
                        value = turned(chunk, cosine, sine).astype(BF16)
                        m["kx"][p, placed, :] = value
                        m["kt"][p, :, placed] = value.T
                    else:
                        value = chunk.astype(BF16)
                        m["vx"][p, placed, :] = value
                        m["vt"][p, :, placed] = value.T

        return project

    tail, head = pl.ds(frames, REACH), pl.ds(0, REACH)

    def heads_joined(both, swapped=False):
        step = HD // 2 if swapped else HD
        return jnp.concatenate(
            [
                both[i : i + step, i // step % 2 * BLOCK : (i // step % 2 + 1) * BLOCK]
                for i in range(0, 2 * HD, step)
            ],
            axis=0,
        )

    unit_rows = lax.broadcasted_iota(jnp.int32, (2 * BLOCK, BLOCK), 0)
    unit_lanes = lax.broadcasted_iota(jnp.int32, (2 * BLOCK, BLOCK), 1)
    picks = (lax.rem(unit_rows, BLOCK) == unit_lanes).astype(F32).astype(BF16)

    def block_rows(b):
        return pl.ds(b * BLOCK, BLOCK)

    def block_window(b):
        return pl.ds(b * BLOCK, SPAN)

    def spare(i):
        return m["after"].at[pl.ds(i // 2 * SPAN, SPAN), pl.ds(i % 2 * 2 * BLOCK, 2 * BLOCK)]

    def spare_low(i):
        return m["branch"].at[pl.ds(i // 2 * SPAN, SPAN), pl.ds(i % 2 * 2 * BLOCK, 2 * BLOCK)]

    def attend(p, events):
        def score(b):
            left = jnp.concatenate([m["kx"][p, block_window(b), :], m["bias"][b]], axis=1)
            right = jnp.concatenate([two_heads(m["qx"][p, block_rows(b), :], True), picks], axis=1)
            spare(b % 4)[...] = dot_t(left, right)

        def soften(b):
            scores = spare(b % 4)[...]
            top = jnp.max(scores, axis=0, keepdims=True)
            weights = jnp.exp(scores - top)
            total = jnp.sum(weights, axis=0, keepdims=True)
            m["probs"][p, b] = (weights * (1.0 / total)).astype(BF16)

        def mix(b):
            joined = heads_joined(dot(m["vt"][p, :, block_window(b)], m["probs"][p, b]))
            m["ot"][p * 128 : (p + 1) * 128, block_rows(b)] = joined.astype(BF16)
            mixed[block_rows(b), p * 128 : (p + 1) * 128] = joined.T.astype(BF16)

        in_turn([*range(2, blocks), 0, 1], (score, soften, mix), events)

    halos = {}

    def send_halo(kind, p):
        ref = m["kx"] if kind == 1 else m["vx"]
        halos[kind, p] = links.single(ref.at[p, tail], ref.at[p, head], "s")
        halos[kind, p].start()

    def take_halo(p):
        for kind, flat, turned_ref in ((1, m["kx"], m["kt"]), (2, m["vx"], m["vt"])):
            halos[kind, p].wait_recv()
            turned_ref[p, :, 0:REACH] = flat[p, 0:REACH, :].T

    for p in range(PAIRS):
        if p < 3:
            run(0, tiles // 2, in_pairs(projection(p)))
            for pair in CHUNKS[p]:
                for kind, q in pair:
                    if kind > 0:
                        send_halo(kind, q)
        due("before", p)
        take = functools.partial(take_halo, p)
        if p < 2:
            attend(p, {blocks - 2: [functools.partial(due, "during", p), take]})
        else:
            take()
            attend(p, {})
        due("after", p)

    m["acc"][...] = jnp.zeros_like(m["acc"])
    acc = m["acc"]

    def add_to(i, values):
        acc[i : i + 1, :] = acc[i : i + 1, :] + jnp.sum(values, axis=0, keepdims=True)

    scale_one, gain_two, bias_two, scale_two = vector(2), vector(3), vector(4), vector(5)
    n2 = y_ref
    dba = m["dba"]

    def norm_back(unit, scale, gain, grad):
        inner = grad * gain
        return scale * (
            inner
            - jnp.mean(inner, axis=-1, keepdims=True)
            - unit * jnp.mean(inner * unit, axis=-1, keepdims=True)
        )

    def norm_two(t, _):
        rows = start_of(t, TILE)
        both = mixed[rows, :]
        branch = jnp.concatenate(
            [dot(both, w[OUT, c].reshape(width, COLUMNS)) for c in range(2)], axis=1
        )
        m["branch"][rows, :] = branch.astype(BF16)
        after = x_ref[rows, :].astype(F32) + scale_one * branch
        m["after"][rows, :] = after
        unit, _scale = normalized(after)
        low = (unit * gain_two + bias_two).astype(BF16)
        n2[rows, :] = low
        m["n2t"][:, rows] = low.T
        dbm = (dy_ref[rows, :].astype(F32) * scale_two).astype(BF16)
        dba[0, rows, :] = dbm[:, : width // 2]
        dba[1, rows, :] = dbm[:, width // 2 :]

    run(0, tiles // 2, in_pairs(norm_two), {1: [functools.partial(due, "norm", 2)]})

    def result_of(i):
        def keep(value):
            if i < OUT:
                for j in range(2):
                    gq[:, chunk_columns(i, j)] = ordered(
                        i, j, value[:, j * 128 : (j + 1) * 128]
                    )
            elif i == OUT:
                go[...] = value
            elif i in DOWN:
                q = DOWN.index(i)
                gd[q * piece : (q + 1) * piece, :] = value
            else:
                m["up_sums"][UP.index(i)] = value

        return keep

    sums = {}

    def unit_grads(i, left, right):
        gathers[i].drain()
        if i < OUT:
            sums[DOWN[i]].drain()
        place = DOWN[i] if i < OUT else i
        out, own = w.at[place, 0], m["own"].at[place - 3]
        if i == LAST:
            arrived, kind = [m["s_in"].at[i], m["pieces"]], ScatterDirect
        else:
            at_unit = i - (i > LAST)
            arrived = [m["s_in"].at[i]] + [m[n].at[at_unit] for n in ("c_in", "b_in", "a_in")]
            kind = Scatter
        sums[i] = kind(own, out, arrived, result_of(i), links, at, m["s_in"])
        own[...] = dot(left[...], right[core])
        out[...] = dot(left[...], right[other]).astype(BF16).reshape(4, 2, 2, piece, COLUMNS)
        sums[i].step(0)

    def step_of(i, number):
        return lambda: sums[i].step(number)

    def feed(q):
        def middle(pair, _):
            for t in range(2):
                one(2 * pair + t)

        def one(t):
            rows = start_of(t, TILE)
            ups = [w[UP[q], h].reshape(width, COLUMNS) for h in range(2)]
            dbm = jnp.concatenate([dba[c, rows, :] for c in range(2)], axis=1)
            acts, dus = [], []
            for h in range(2):
                value, slope = gelu_and_slope(dot(n2[rows, :], ups[h]))
                act = value.astype(BF16)
                m["actt"][h * COLUMNS : (h + 1) * COLUMNS, rows] = act.T
                down = jnp.concatenate(
                    [w[DOWN[q], c, 2 * h : 2 * h + 2].reshape(COLUMNS, COLUMNS) for c in range(2)],
                    axis=1,
                )
                du = (dot_t(dbm, down) * slope).astype(BF16)
                m["du"][h, rows, :] = du
                acts.append(act)
                dus.append(du)
            act = jnp.concatenate(acts, axis=1)
            for c in range(2):
                columns = pl.ds(c * COLUMNS, COLUMNS)
                total = dot(act, w[DOWN[q], c].reshape(2 * COLUMNS, COLUMNS))
                if q > 0:
                    total = total + m["branch_two"][rows, columns]
                m["branch_two"][rows, columns] = total
            grad = dot_t(jnp.concatenate(dus, axis=1), jnp.concatenate(ups, axis=1))
            if q > 0:
                grad = grad + m["dx1"][rows, :]
            m["dx1"][rows, :] = grad

        return middle

    def steps_of(q, number):
        return [step_of(DOWN[q], number), step_of(UP[q], number)]

    def do(actions):
        for action in actions:
            action()

    for q in range(4):
        due("feed", q, 0)
        events = {1: [functools.partial(due, "feed", q, 1)]}
        if q > 0:
            events[1] += steps_of(q - 1, 1)
        run(0, tiles // 2, feed(q), events)
        due("feed", q, 2)
        if q > 1:
            do(steps_of(q - 2, 2))
        unit_grads(DOWN[q], m["actt"], dba)
        unit_grads(UP[q], m["n2t"], m["du"])

    def norm_two_back(t, _):
        rows = start_of(t, TILE)
        after, branch_two = m["after"][rows, :], m["branch_two"][rows, :]
        y_ref[rows, :] = (after + scale_two * branch_two).astype(BF16)
        upstream = dy_ref[rows, :].astype(F32)
        add_to(5, upstream * branch_two)
        unit, scale = normalized(after)
        grad = m["dx1"][rows, :]
        add_to(3, grad * unit)
        add_to(4, grad)
        dx1 = upstream + norm_back(unit, scale, gain_two, grad)
        m["dx1"][rows, :] = dx1
        add_to(2, dx1 * m["branch"][rows, :].astype(F32))
        low = (dx1 * scale_one).astype(BF16)
        sides = [low[:, : width // 2], low[:, width // 2 :]]
        for c in range(2):
            dba[c, rows, :] = sides[c]
        dmixed = (
            dot_t(sides[0], w[OUT, 0].reshape(width, COLUMNS))
            + dot_t(sides[1], w[OUT, 1].reshape(width, COLUMNS))
        ).astype(BF16)
        m["n2t"][:, rows] = dmixed.T
        for p in range(PAIRS):
            m["dox"][p, rows, :] = dmixed[:, p * 128 : (p + 1) * 128]

    do(steps_of(0, 3))
    run(
        0,
        tiles // 2,
        in_pairs(norm_two_back),
        {1: steps_of(3, 1)},
    )
    y_send = pltpu.make_async_copy(y_ref, y_out.at[0], moves.at[5])
    y_send.start()
    do(steps_of(2, 2))
    unit_grads(OUT, m["ot"], dba)
    do(steps_of(1, 3))

    dp = m["dp"]
    halfway = [
        [step_of(OUT, 1)],
        steps_of(2, 3) + steps_of(3, 2),
        [step_of(GROUP, 1)],
        [step_of(GROUP + 1, 1)],
    ]
    after_pair = [
        steps_of(0, 4),
        steps_of(1, 4) + [step_of(OUT, 2)],
        steps_of(2, 4) + steps_of(3, 3) + [step_of(OUT, 3)],
        [step_of(GROUP, 2)],
    ]

    def store_turned(kind, p, rows, value):
        g, c, j = place_of(kind, p)
        if kind < 2:
            value = turned(value, m["cos"][rows, :], -m["sin"][rows, :])
        dp[g, c, rows, j * 128 : (j + 1) * 128] = value.astype(BF16)

    backs = []
    for p in range(PAIRS):
        dkx, dvx = m["dkx"], m["dvx"]
        dkx[...] = jnp.zeros_like(dkx)
        dvx[...] = jnp.zeros_like(dvx)

        def probe(b, p=p):
            spare(b % 4)[...] = dot_t(
                m["vx"][p, block_window(b), :], two_heads(m["dox"][p, block_rows(b), :])
            )

        def weigh(b, p=p):
            probs = m["probs"][p, b].astype(F32)
            heads = (pl.ds(p * 128, 128), block_rows(b))
            shared = m["n2t"][heads].astype(F32) * m["ot"][heads].astype(F32)
            balance = jnp.concatenate(
                [
                    jnp.sum(shared[:HD], axis=0, keepdims=True),
                    jnp.sum(shared[HD:], axis=0, keepdims=True),
                ],
                axis=1,
            )
            spare_low(b % 4)[...] = (probs * (spare(b % 4)[...] - balance)).astype(BF16)

        def gather_back(b, p=p):
            window, rows = block_window(b), block_rows(b)
            dscores = spare_low(b % 4)[...]
            dvx[window, :] = dvx[window, :] + dot(
                m["probs"][p, b], two_heads(m["dox"][p, rows, :])
            )
            dkx[window, :] = dkx[window, :] + dot(dscores, two_heads(m["qx"][p, rows, :], True))
            joined = heads_joined(dot(m["kt"][p, :, window], dscores), True).T * factor
            store_turned(0, p, rows, joined)

        h_out, h_in = m["h_out"], m["h_in"]
        halo_back = links.single(h_out.at[p], h_in.at[p], "s")
        backs.append(halo_back)

        def send_back(p=p, halo_back=halo_back):
            h_out[p, 0] = dkx[0:REACH, :].astype(BF16)
            h_out[p, 1] = dvx[0:REACH, :].astype(BF16)
            halo_back.start()

        events = {4: [send_back] + halfway[p]}
        in_turn(range(blocks), (probe, weigh, gather_back), events)
        halo_back.wait_recv()
        dkx[tail, :] = dkx[tail, :] + h_in[p, 0].astype(F32)
        dvx[tail, :] = dvx[tail, :] + h_in[p, 1].astype(F32)

        def finish(t, _, p=p):
            rows = start_of(t, TILE)
            placed = pl.ds(pl.multiple_of(REACH + t * TILE, TILE), TILE)
            store_turned(1, p, rows, dkx[placed, :])
            store_turned(2, p, rows, dvx[placed, :])

        run(0, tiles, finish)
        do(after_pair[p])
        if p > 0:
            unit_grads(GROUP + p - 1, m["n1t"], dp.at[p - 1])


    def first(t, _):
        rows = start_of(t, TILE)
        sides = [(g, c) for g in range(3) for c in range(2)]
        grad = dot_t(
            jnp.concatenate([dp[g, c, rows, :] for g, c in sides], axis=1),
            jnp.concatenate([w[g, c].reshape(width, COLUMNS) for g, c in sides], axis=1),
        )
        unit, scale = normalized(x_ref[rows, :].astype(F32))
        add_to(0, grad * unit)
        add_to(1, grad)
        mixed[rows, :] = (
            m["dx1"][rows, :] + norm_back(unit, scale, gain_one, grad)
        ).astype(BF16)

    late = {1: [step_of(LAST, 1)], 3: [*steps_of(3, 4), step_of(OUT, 4), step_of(GROUP + 1, 2)]}
    run(0, tiles, first, late)
    sends = [pltpu.make_async_copy(mixed, ig_out.at[0], moves.at[6])]
    sends[0].start()

    v_out, v_in, v_all = m["v_out"], m["v_in"], m["v_all"]
    v_out[...] = acc[:, start_of(other, width // 2)]
    vector_hop = links.single(v_out, v_in, "s")
    vector_hop.start()
    sums[GROUP].step(3)
    vector_hop.wait_recv()
    v_all[row] = acc[:, start_of(core, width // 2)] + v_in[...]
    spread_send, spread_recv = links.slot(), links.slot()
    for k in range(1, 16):
        links.copy(v_all.at[row], v_all.at[row], ("r", k), spread_send, spread_recv).start()
    for j in range(2):
        for a in range(4):
            gu[:, (4 * j + a) * 128 : (4 * j + a + 1) * 128] = regroup(
                [m["up_sums"][q, :, j * 128 : (j + 1) * 128] for q in range(4)], a, True
            )
    sums[GROUP + 1].step(3)
    sums[GROUP].step(4)
    await_bytes(v_all.at[0:15], spread_recv)
    total = v_all[0]
    for r in range(1, 16):
        total = total + v_all[r]
    gv[...] = total
    sums[LAST].step(2)
    sums[GROUP + 1].step(4)
    await_bytes(v_all.at[0:15], spread_send)
    for i, each in sums.items():
        if i not in DOWN[:3]:
            each.drain()
    for each in [vec_copy, seg_copy, *halos.values(), *backs, vector_hop]:
        each.wait_send()
    y_send.wait()
    for each in sends:
        each.wait()


def write_kernel(*refs):
    for source, target in zip(refs[:6], refs[7:13]):
        target[...] = source[...]
    for i, vector in enumerate(refs[13:]):
        vector[...] = refs[6][i : i + 1, :]


def local_staged(
    inputs,
    cotangent,
    segment_ids,
    qkv_weight,
    out_weight,
    up_weight,
    down_weight,
    *vectors,
):
    frames, width = inputs.shape[1:]
    items = scratch_list(frames, width)
    whole = pl.BlockSpec(memory_space=pltpu.VMEM)
    anywhere = pl.BlockSpec(memory_space=pl.ANY)
    shapes = [
        jax.ShapeDtypeStruct(inputs.shape, BF16),
        jax.ShapeDtypeStruct(inputs.shape, BF16),
        *[
            jax.ShapeDtypeStruct(weight.shape, F32)
            for weight in (qkv_weight, out_weight, up_weight, down_weight)
        ],
    ]
    results = pl.pallas_call(
        functools.partial(layer_kernel, [name for name, _, _ in items]),
        out_shape=shapes + [jax.ShapeDtypeStruct((8, width // 2), F32)],
        in_specs=[anywhere] * 2 + [whole] * 2 + [anywhere] * 3 + [whole] * 6,
        out_specs=[anywhere] * 2 + [whole] * 5,
        scratch_shapes=[pltpu.VMEM(shape, kind) for _, shape, kind in items]
        + [pltpu.SemaphoreType.DMA((7,)), pltpu.SemaphoreType.DMA((SLOTS,))],
        compiler_params=pltpu.CompilerParams(
            collective_id=0, has_side_effects=True, vmem_limit_bytes=VMEM_LIMIT
        ),
    )(
        inputs,
        cotangent,
        segment_ids,
        qkv_weight,
        out_weight,
        up_weight,
        down_weight,
        *[v.reshape(1, -1) for v in vectors],
    )
    written = pl.pallas_call(
        write_kernel,
        out_shape=shapes + [jax.ShapeDtypeStruct((1, width // 2), F32)] * 6,
        in_specs=[whole] * 7,
        out_specs=[whole] * 12,
    )(*results)
    return (*written[:6], *[v.reshape(-1) for v in written[6:]])


VMEM_LIMIT = 64 * 2**20


def solution(mesh):
    placed = (
        P("rows", "tm", None),
        P("rows", "tm", None),
        P("rows", "tm"),
        P("rows", "tm"),
        P("rows", "tm"),
        P("rows", "tm"),
        P("rows", "tm"),
        P("tm"),
        P("tm"),
        P("tm"),
        P("tm"),
        P("tm"),
        P("tm"),
    )
    staged = mesh.shape["rows"] == 16 and mesh.shape["tm"] == 2
    return jax.shard_map(
        local_staged if staged else local,
        mesh=mesh,
        in_specs=placed,
        out_specs=(
            P("rows", "tm", None),
            P("rows", "tm", None),
            P("rows", "tm"),
            P("rows", "tm"),
            P("rows", "tm"),
            P("rows", "tm"),
            P("tm"),
            P("tm"),
            P("tm"),
            P("tm"),
            P("tm"),
            P("tm"),
        ),
        check_vma=False,
    )
```

```python
import functools
import math

import jax
import jax.numpy as jnp
from jax import lax
from jax.experimental import pallas as pl
from jax.experimental.pallas import tpu as pltpu
from jax.sharding import PartitionSpec as P

H = 8
HD = 64
WINDOW = 250
REACH = 256
QBLOCK = 512


EPSILON = 1e-05
NEGATIVE = -1e30


def prefix(part, axis, combine, identity):
    place = lax.axis_index(axis)
    gathered = jax.tree.map(lambda a: lax.all_gather(a, axis), part)
    state = jax.tree.map(lambda a, e: jnp.zeros_like(a) + jnp.asarray(e, a.dtype), part, identity)

    def one(turn, state):
        return combine(
            state, jax.tree.map(lambda a: lax.dynamic_index_in_dim(a, turn, 0, False), gathered)
        )

    return lax.fori_loop(0, place, one, state)


def shifted(block, axis, distance):
    devices = range(lax.axis_size(axis))
    route = [(i - distance, i) for i in devices if i - distance in devices]
    return lax.ppermute(block, axis, route)


def layer_norm(values, gain_vec, bias_vec):
    average = jnp.mean(values, axis=-1, keepdims=True)
    centred = values - average
    variance = jnp.mean(centred * centred, axis=-1, keepdims=True)
    return centred * lax.rsqrt(variance + EPSILON) * gain_vec + bias_vec


def gelu_exact(values):
    return jax.nn.gelu(values, approximate=False)


def rotation_tables(positions):
    half_size = HD // 2
    ladder = jnp.arange(half_size, dtype=jnp.float32)
    frequency = jnp.exp(ladder * (-2.0 * math.log(10000.0) / HD))
    angles = positions.astype(jnp.float32)[:, None] * frequency[None, :]
    return (jnp.cos(angles)[:, None, :], jnp.sin(angles)[:, None, :])


def rotate(field, cosine, sine):
    half_size = field.shape[-1] // 2
    former = field[..., :half_size]
    latter = field[..., half_size:]
    return jnp.concatenate(
        [former * cosine - latter * sine, latter * cosine + former * sine], axis=-1
    )


def outer_sum(left, right):
    return lax.dot_general(
        left, right, (((0,), (0,)), ((), ())), preferred_element_type=jnp.float32
    )


def block_allowed(begin, segment, extended_segments, valid_keys):
    offsets = (
        jnp.arange(QBLOCK, dtype=jnp.int32)[:, None]
        - jnp.arange(QBLOCK + REACH, dtype=jnp.int32)[None, :]
        + REACH
    )
    near = (offsets >= 0) & (offsets < WINDOW)
    query_segments = segment[begin : begin + QBLOCK]
    key_segments = extended_segments[begin : begin + QBLOCK + REACH]
    key_valid = valid_keys[begin : begin + QBLOCK + REACH]
    return near & (query_segments[:, None] == key_segments[None, :]) & key_valid[None, :]


def block_scores(query_block, key_window, allowed):
    raw = jnp.einsum(
        "qhd,khd->hqk", query_block, key_window, preferred_element_type=jnp.float32
    ) * (1.0 / math.sqrt(HD))
    return jnp.where(allowed[None], raw, NEGATIVE)


def local(
    inputs,
    cotangent,
    segment_ids,
    qkv_weight,
    out_weight,
    up_weight,
    down_weight,
    norm_gain_one,
    norm_bias_one,
    attn_scale,
    norm_gain_two,
    norm_bias_two,
    mlp_scale,
):
    frames = inputs.shape[1]
    width = inputs.shape[2]
    low_type = jnp.bfloat16
    gathered = (
        lax.all_gather(qkv_weight.astype(low_type), "tm", axis=1, tiled=True),
        lax.all_gather(out_weight.astype(low_type), "tm", axis=1, tiled=True),
        lax.all_gather(up_weight.astype(low_type), "tm", axis=1, tiled=True),
        lax.all_gather(down_weight.astype(low_type), "tm", axis=1, tiled=True),
        lax.all_gather(norm_gain_one.astype(low_type), "tm", axis=0, tiled=True),
        lax.all_gather(norm_bias_one.astype(low_type), "tm", axis=0, tiled=True),
        lax.all_gather(attn_scale.astype(low_type), "tm", axis=0, tiled=True),
        lax.all_gather(norm_gain_two.astype(low_type), "tm", axis=0, tiled=True),
        lax.all_gather(norm_bias_two.astype(low_type), "tm", axis=0, tiled=True),
        lax.all_gather(mlp_scale.astype(low_type), "tm", axis=0, tiled=True),
    )
    w_qkv, w_out, w_up, w_down = (
        lax.all_gather(gathered[0], "rows", axis=0, tiled=True),
        lax.all_gather(gathered[1], "rows", axis=0, tiled=True),
        lax.all_gather(gathered[2], "rows", axis=0, tiled=True),
        lax.all_gather(gathered[3], "rows", axis=0, tiled=True),
    )
    gain_one, bias_one, scale_one, gain_two, bias_two, scale_two = [
        piece.astype(jnp.float32) for piece in gathered[4:]
    ]
    segment = segment_ids[0]
    index = jnp.arange(frames, dtype=jnp.int32)
    last_run = jnp.sum((segment == segment[frames - 1]).astype(jnp.int32), keepdims=True)

    def join_runs(earlier, later):
        extends = (later[1] == frames) & (later[0] == earlier[0])
        joined = jnp.where(extends, earlier[1] + later[1], later[1])
        vacant = later[0] < 0
        return (jnp.where(vacant, earlier[0], later[0]), jnp.where(vacant, earlier[1], joined))

    before_id, before_run = prefix(
        (segment[frames - 1 :], last_run),
        "tm",
        join_runs,
        (jnp.full((1,), -1, jnp.int32), jnp.zeros((1,), jnp.int32)),
    )
    change = jnp.concatenate([jnp.ones((1,), jnp.bool_), segment[1:] != segment[:-1]])
    starts = lax.cummax(jnp.where(change, index, jnp.zeros_like(index)), axis=0)
    positions = index - starts + jnp.where(segment == before_id[0], before_run[0], 0)
    cosine, sine = rotation_tables(positions)
    source = inputs[0].astype(jnp.float32)
    normed_one, norm_one_pull = jax.vjp(layer_norm, source, gain_one, bias_one)
    normed_one_low = normed_one.astype(low_type)
    projected = jnp.dot(normed_one_low, w_qkv, preferred_element_type=jnp.float32)
    queries = rotate(projected[:, :width].reshape(frames, H, HD), cosine, sine).astype(low_type)
    keys_flat = (
        rotate(projected[:, width : 2 * width].reshape(frames, H, HD), cosine, sine)
        .reshape(frames, width)
        .astype(low_type)
    )
    values_flat = projected[:, 2 * width :].astype(low_type)
    got_keys, got_values, got_segments = shifted((keys_flat, values_flat, segment), "tm", 1)
    got_keys = got_keys[frames - REACH :]
    got_values = got_values[frames - REACH :]
    got_segments = got_segments[frames - REACH :]
    extended_keys = jnp.concatenate([got_keys, keys_flat], axis=0).reshape(REACH + frames, H, HD)
    extended_values = jnp.concatenate([got_values, values_flat], axis=0).reshape(
        REACH + frames, H, HD
    )
    extended_segments = jnp.concatenate([got_segments, segment])
    valid_keys = (lax.axis_index("tm") > 0) | (jnp.arange(REACH + frames, dtype=jnp.int32) >= REACH)
    block_count = frames // QBLOCK
    mixed_parts = []
    log_sums = []
    for block in range(block_count):
        begin = block * QBLOCK
        allowed = block_allowed(begin, segment, extended_segments, valid_keys)
        scores = block_scores(
            queries[begin : begin + QBLOCK], extended_keys[begin : begin + QBLOCK + REACH], allowed
        )
        top = jnp.max(scores, axis=-1, keepdims=True)
        weights = jnp.exp(scores - top)
        total = jnp.sum(weights, axis=-1, keepdims=True)
        probs = (weights / total).astype(low_type)
        mixed_parts.append(
            jnp.einsum(
                "hqk,khd->qhd",
                probs,
                extended_values[begin : begin + QBLOCK + REACH],
                preferred_element_type=jnp.float32,
            )
        )
        log_sums.append(top + jnp.log(total))
    mixed_low = jnp.concatenate(mixed_parts, axis=0).reshape(frames, width).astype(low_type)
    branch = jnp.dot(mixed_low, w_out, preferred_element_type=jnp.float32)
    after = source + scale_one * branch
    normed_two, norm_two_pull = jax.vjp(layer_norm, after, gain_two, bias_two)
    normed_two_low = normed_two.astype(low_type)
    hidden = jnp.dot(normed_two_low, w_up, preferred_element_type=jnp.float32)
    active, gelu_pull = jax.vjp(gelu_exact, hidden)
    active_low = active.astype(low_type)
    branch_two = jnp.dot(active_low, w_down, preferred_element_type=jnp.float32)
    result = (after + scale_two * branch_two).astype(low_type)
    again = (
        lax.all_gather(qkv_weight.astype(low_type), "tm", axis=1, tiled=True),
        lax.all_gather(out_weight.astype(low_type), "tm", axis=1, tiled=True),
        lax.all_gather(up_weight.astype(low_type), "tm", axis=1, tiled=True),
        lax.all_gather(down_weight.astype(low_type), "tm", axis=1, tiled=True),
    )
    back_qkv, back_out, back_up, back_down = (
        lax.all_gather(again[0], "rows", axis=0, tiled=True),
        lax.all_gather(again[1], "rows", axis=0, tiled=True),
        lax.all_gather(again[2], "rows", axis=0, tiled=True),
        lax.all_gather(again[3], "rows", axis=0, tiled=True),
    )
    upstream = cotangent[0].astype(jnp.float32)
    grad_scale_two = jnp.sum(upstream * branch_two, axis=0)
    grad_branch_two = (upstream * scale_two).astype(low_type)
    grad_down = outer_sum(active_low, grad_branch_two)
    grad_active = lax.dot_general(
        grad_branch_two, back_down, (((1,), (1,)), ((), ())), preferred_element_type=jnp.float32
    )
    grad_hidden = gelu_pull(grad_active)[0].astype(low_type)
    grad_up = outer_sum(normed_two_low, grad_hidden)
    grad_normed_two = lax.dot_general(
        grad_hidden, back_up, (((1,), (1,)), ((), ())), preferred_element_type=jnp.float32
    )
    after_part, grad_gain_two, grad_bias_two = norm_two_pull(grad_normed_two)
    grad_after = upstream + after_part
    grad_scale_one = jnp.sum(grad_after * branch, axis=0)
    grad_branch = (grad_after * scale_one).astype(low_type)
    grad_out = outer_sum(mixed_low, grad_branch)
    grad_mixed = lax.dot_general(
        grad_branch, back_out, (((1,), (1,)), ((), ())), preferred_element_type=jnp.float32
    )
    grad_mixed = grad_mixed.astype(low_type).reshape(frames, H, HD)
    factor = 1.0 / math.sqrt(HD)
    grad_keys_ext = jnp.zeros((REACH + frames, H, HD), jnp.float32)
    grad_values_ext = jnp.zeros((REACH + frames, H, HD), jnp.float32)
    query_grads = []
    for block in range(block_count):
        begin = block * QBLOCK
        allowed = block_allowed(begin, segment, extended_segments, valid_keys)
        query_block = queries[begin : begin + QBLOCK]
        key_window = extended_keys[begin : begin + QBLOCK + REACH]
        value_window = extended_values[begin : begin + QBLOCK + REACH]
        scores = block_scores(query_block, key_window, allowed)
        probs_full = jnp.exp(scores - log_sums[block])
        probs_low = probs_full.astype(low_type)
        grad_out_block = grad_mixed[begin : begin + QBLOCK]
        grad_probs = jnp.einsum(
            "qhd,khd->hqk", grad_out_block, value_window, preferred_element_type=jnp.float32
        )
        grad_values_ext = grad_values_ext.at[begin : begin + QBLOCK + REACH].add(
            jnp.einsum(
                "hqk,qhd->khd", probs_low, grad_out_block, preferred_element_type=jnp.float32
            )
        )
        balance = jnp.sum(grad_probs * probs_full, axis=-1, keepdims=True)
        grad_scores = (probs_full * (grad_probs - balance)).astype(low_type)
        query_grads.append(
            jnp.einsum("hqk,khd->qhd", grad_scores, key_window, preferred_element_type=jnp.float32)
            * factor
        )
        grad_keys_ext = grad_keys_ext.at[begin : begin + QBLOCK + REACH].add(
            jnp.einsum("hqk,qhd->khd", grad_scores, query_block, preferred_element_type=jnp.float32)
            * factor
        )
    grad_keys_flat = grad_keys_ext.reshape(REACH + frames, width)
    grad_values_flat = grad_values_ext.reshape(REACH + frames, width)
    back_keys, back_values = (
        shifted(grad_keys_flat[:REACH].astype(jnp.bfloat16), "tm", -1).astype(jnp.float32),
        shifted(grad_values_flat[:REACH].astype(jnp.bfloat16), "tm", -1).astype(jnp.float32),
    )
    own_keys = grad_keys_flat[REACH:]
    own_values = grad_values_flat[REACH:]
    own_keys = jnp.concatenate(
        [own_keys[: frames - REACH], own_keys[frames - REACH :] + back_keys], axis=0
    )
    own_values = jnp.concatenate(
        [own_values[: frames - REACH], own_values[frames - REACH :] + back_values], axis=0
    )
    grad_queries = rotate(jnp.concatenate(query_grads, axis=0), cosine, -sine).reshape(
        frames, width
    )
    grad_keys = rotate(own_keys.reshape(frames, H, HD), cosine, -sine).reshape(frames, width)
    grad_projected = jnp.concatenate([grad_queries, grad_keys, own_values], axis=1).astype(low_type)
    grad_qkv = outer_sum(normed_one_low, grad_projected)
    grad_normed_one = lax.dot_general(
        grad_projected, back_qkv, (((1,), (1,)), ((), ())), preferred_element_type=jnp.float32
    )
    source_part, grad_gain_one, grad_bias_one = norm_one_pull(grad_normed_one)
    input_grad = (grad_after + source_part).astype(low_type)
    reduced = (
        lax.psum_scatter(grad_qkv, "tm", scatter_dimension=1, tiled=True),
        lax.psum_scatter(grad_out, "tm", scatter_dimension=1, tiled=True),
        lax.psum_scatter(grad_up, "tm", scatter_dimension=1, tiled=True),
        lax.psum_scatter(grad_down, "tm", scatter_dimension=1, tiled=True),
        lax.psum_scatter(grad_gain_one, "tm", scatter_dimension=0, tiled=True),
        lax.psum_scatter(grad_bias_one, "tm", scatter_dimension=0, tiled=True),
        lax.psum_scatter(grad_scale_one, "tm", scatter_dimension=0, tiled=True),
        lax.psum_scatter(grad_gain_two, "tm", scatter_dimension=0, tiled=True),
        lax.psum_scatter(grad_bias_two, "tm", scatter_dimension=0, tiled=True),
        lax.psum_scatter(grad_scale_two, "tm", scatter_dimension=0, tiled=True),
    )
    qkv_grad, out_grad, up_grad, down_grad = (
        lax.psum_scatter(reduced[0], "rows", scatter_dimension=0, tiled=True),
        lax.psum_scatter(reduced[1], "rows", scatter_dimension=0, tiled=True),
        lax.psum_scatter(reduced[2], "rows", scatter_dimension=0, tiled=True),
        lax.psum_scatter(reduced[3], "rows", scatter_dimension=0, tiled=True),
    )
    vector_sums = lax.psum(
        (reduced[4], reduced[5], reduced[6], reduced[7], reduced[8], reduced[9]), "rows"
    )
    return (
        result[None],
        input_grad[None],
        qkv_grad,
        out_grad,
        up_grad,
        down_grad,
        vector_sums[0],
        vector_sums[1],
        vector_sums[2],
        vector_sums[3],
        vector_sums[4],
        vector_sums[5],
    )


MESH_IDS = pl.DeviceIdType.MESH
F32 = jnp.float32
BF16 = jnp.bfloat16


def dot(left, right, contract=((1,), (0,))):
    return lax.dot_general(left, right, (contract, ((), ())), preferred_element_type=F32)


def dot_t(left, right):
    return dot(left, right, ((1,), (1,)))


def start_of(index, size):
    return pl.ds(pl.multiple_of(index * size, size), size)


def coordinates():
    row, core = lax.axis_index("rows"), lax.axis_index("tm")
    return row, core, lax.rem(row, 2), lax.rem(lax.div(row, 2), 2), lax.div(row, 4)


def peers_of(at):
    row, core, x, y, z = at
    found = {
        "x": (row + 1 - 2 * x, core),
        "y": (row + 2 - 4 * y, core),
        "s": (row, 1 - core),
    }
    for k in (1, 2, 3):
        found[k] = (lax.rem(z + k, 4) * 4 + lax.rem(row, 4), core)
    found["xy"] = (row + 3 - 2 * x - 4 * y, core)
    for k in range(1, 16):
        found["r", k] = (lax.rem(row + k, 16), core)
    return found


def greet(peers):
    for name in ["s"] + [("r", k) for k in range(1, 16)]:
        pl.semaphore_signal(
            pltpu.get_barrier_semaphore(), inc=1, device_id=peers[name], device_id_type=MESH_IDS
        )


def be_greeted():
    pl.semaphore_wait(pltpu.get_barrier_semaphore(), 16)


class Links:
    def __init__(self, sems, peers):
        self.sems, self.peers, self.used = sems, peers, 0

    def slot(self):
        self.used += 1
        return self.sems.at[self.used - 1]

    def copy(self, src, dst, peer, send, recv):
        return pltpu.make_async_remote_copy(
            src_ref=src,
            dst_ref=dst,
            send_sem=send,
            recv_sem=recv,
            device_id=self.peers[peer],
            device_id_type=MESH_IDS,
        )

    def single(self, src, dst, peer):
        return self.copy(src, dst, peer, self.slot(), self.slot())


def await_bytes(like, sem):
    pltpu.make_async_copy(like, like, sem).wait()


class Gather:
    def __init__(self, units, i, links, at):
        full = units.at[i]
        row, core, x, y, z = at
        half = full.shape[4] // 2
        low, high = pl.ds(0, half), pl.ds(half, half)
        every = slice(None)
        near, far = links.slot(), links.slot()
        got = [links.slot() for _ in range(4)]

        def copy(where, peer, send, recv):
            return links.copy(full.at[where], full.at[where], peer, send, recv)

        self.starts = (
            [copy((core, z, y, x), k, near, got[0]) for k in (1, 2, 3)],
            [
                copy((core, every, y, x, low), "x", far, got[1]),
                copy((core, every, y, x, high), "y", far, got[1]),
                copy((core, every, y, x), "s", far, got[3]),
            ],
            [
                copy((core, every, y, every, low), "y", far, got[2]),
                copy((core, every, every, x, high), "x", far, got[2]),
                copy((core, every, y, 1 - x, low), "s", far, got[3]),
                copy((core, every, 1 - y, x, high), "s", far, got[3]),
            ],
            [
                copy((core, every, 1 - y, every, low), "s", far, got[3]),
                copy((core, every, every, 1 - x, high), "s", far, got[3]),
            ],
            [],
        )
        self.waits = (
            None,
            (full.at[core, 0:3, y, x], got[0]),
            (full.at[core, :, y, x], got[1]),
            (full.at[core, :, y], got[2]),
            (full.at[1 - core], got[3]),
        )
        self.sent = ((full.at[core, 0:3, y, x], near), (units.at[0:7, 0, 0], far))

    def step(self, number):
        if number > 0:
            await_bytes(*self.waits[number])
        for copy in self.starts[number]:
            copy.start()

    def drain(self):
        for like, sem in self.sent:
            await_bytes(like, sem)


class GatherDirect:
    def __init__(self, units, i, links, at):
        full = units.at[i]
        row, core, x, y, z = at
        piece = full.at[core, z, y, x]
        self.sent, self.got, passed, self.whole = [links.slot() for _ in range(4)]
        self.starts = [
            links.copy(piece, piece, ("r", k), self.sent, self.got) for k in range(1, 16)
        ]
        self.over = links.copy(full.at[core], full.at[core], "s", passed, self.whole)
        self.fifteen = units.at[0:5, 0, 0:3, 0, 0]

    def step(self, number):
        if number == 0:
            for copy in self.starts:
                copy.start()
        if number == 1:
            await_bytes(self.fifteen, self.got)
            self.over.start()
        if number == 2:
            self.over.wait_recv()

    def drain(self):
        await_bytes(self.fifteen, self.sent)
        self.over.wait_send()


class GatherPlane:
    def __init__(self, units, i, links, at):
        full = units.at[i]
        row, core, x, y, z = at
        every = slice(None)
        near, far = links.slot(), links.slot()
        got = [links.slot() for _ in range(3)]

        def copy(where, peer, send, recv):
            return links.copy(full.at[where], full.at[where], peer, send, recv)

        column = (core, every, y, x)
        self.starts = (
            [copy((core, z, y, x), k, near, got[0]) for k in (1, 2, 3)],
            [copy(column, peer, far, got[1]) for peer in ("xy", "x", "y")]
            + [copy(column, "s", far, got[2])],
            [
                copy((core, every, y, 1 - x), "s", far, got[2]),
                copy((core, every, 1 - y), "s", far, got[2]),
            ],
            [],
        )
        self.waits = (
            None,
            (full.at[core, 0:3, y, x], got[0]),
            (units.at[0:3, 0, :, 0, 0], got[1]),
            (full.at[1 - core], got[2]),
        )
        self.sent = ((full.at[core, 0:3, y, x], near), (units.at[0:7, 0, 0], far))

    def step(self, number):
        if number > 0:
            await_bytes(*self.waits[number])
        for copy in self.starts[number]:
            copy.start()

    def drain(self):
        for like, sem in self.sent:
            await_bytes(like, sem)


class Scatter:
    def __init__(self, own, out, arrived, result, links, at, units):
        self.own, self.out, self.result, self.at = own, out, result, at
        self.s_in, self.c_in, self.b_in, self.a_in = arrived
        row, core, x, y, z = at
        self.rows = out.shape[3]
        half = self.half = self.rows // 2
        low, high = self.low, self.high = pl.ds(0, half), pl.ds(half, half)
        every = slice(None)
        self.d = links.single(out, self.s_in, "s")
        self.far = links.slot()
        self.got = [links.slot() for _ in range(3)]
        self.units = units

        def copy(src, dst, peer, which):
            return links.copy(src, dst, peer, self.far, self.got[which])

        self.c1 = copy(out.at[every, 1 - y, every, low], self.c_in.at[0], "y", 0)
        self.c2 = copy(out.at[every, every, 1 - x, high], self.c_in.at[1], "x", 0)
        self.b1 = copy(out.at[every, y, 1 - x, low], self.b_in.at[0], "x", 1)
        self.b2 = copy(out.at[every, 1 - y, x, high], self.b_in.at[1], "y", 1)
        self.a = [
            copy(out.at[lax.rem(z + k, 4), y, x], self.a_in.at[k - 1], k, 2) for k in (1, 2, 3)
        ]

    def mine(self, k, y, x, part):
        begin = ((k * 2 + y) * 2 + x) * self.rows + part * self.half
        return self.own[pl.ds(pl.multiple_of(begin, self.half), self.half), :] + self.s_in[
            k, y, x, pl.ds(part * self.half, self.half)
        ].astype(F32)

    def column(self, k, part):
        row, core, x, y, z = self.at
        place = x if part == 0 else y
        return (
            self.mine(k, y, x, part)
            + self.c_in[part, k, place].astype(F32)
            + self.b_in[part, k].astype(F32)
        )

    def step(self, number):
        row, core, x, y, z = self.at
        low, high, out = self.low, self.high, self.out
        c_in = self.c_in
        if number == 0:
            self.d.start()
        if number == 1:
            self.d.wait()
            for k in range(4):
                for i in range(2):
                    out[k, 1 - y, i, low] = self.mine(k, 1 - y, i, 0).astype(BF16)
            self.c1.start()
            for k in range(4):
                for i in range(2):
                    out[k, i, 1 - x, high] = self.mine(k, i, 1 - x, 1).astype(BF16)
            self.c2.start()
        if number == 2:
            await_bytes(c_in, self.got[0])
            for k in range(4):
                out[k, y, 1 - x, low] = (
                    self.mine(k, y, 1 - x, 0) + c_in[0, k, 1 - x].astype(F32)
                ).astype(BF16)
            self.b1.start()
            for k in range(4):
                out[k, 1 - y, x, high] = (
                    self.mine(k, 1 - y, x, 1) + c_in[1, k, 1 - y].astype(F32)
                ).astype(BF16)
            self.b2.start()
        if number == 3:
            await_bytes(self.b_in, self.got[1])
            for k in (1, 2, 3):
                there = lax.rem(z + k, 4)
                out[there, y, x, low] = self.column(there, 0).astype(BF16)
                out[there, y, x, high] = self.column(there, 1).astype(BF16)
                self.a[k - 1].start()
            self.own[low, :] = self.column(z, 0)
            self.own[high, :] = self.column(z, 1)
        if number == 4:
            await_bytes(self.a_in, self.got[2])
            self.result(
                self.own[: self.rows, :]
                + (self.a_in[0].astype(F32) + self.a_in[1].astype(F32) + self.a_in[2].astype(F32))
            )

    def drain(self):
        await_bytes(self.units.at[0:5, 0:3, 0, 0], self.far)


class ScatterDirect(Scatter):
    def __init__(self, own, out, arrived, result, links, at, units):
        self.own, self.out, self.result, self.at = own, out, result, at
        self.s_in, self.pieces = arrived
        row, core, x, y, z = at
        self.rows = out.shape[3]
        self.half = self.rows // 2
        self.units = units
        self.d = links.single(out, self.s_in, "s")
        self.far, self.got = links.slot(), links.slot()
        self.copies = []
        for k in range(1, 16):
            there = lax.rem(row + k, 16)
            where = (lax.div(there, 4), lax.rem(lax.div(there, 2), 2), lax.rem(there, 2))
            made = links.copy(out.at[where], self.pieces.at[k - 1], ("r", k), self.far, self.got)
            self.copies.append((where, made))

    def whole(self, z, y, x):
        return jnp.concatenate([self.mine(z, y, x, part) for part in range(2)], axis=0)

    def step(self, number):
        row, core, x, y, z = self.at
        if number == 0:
            self.d.start()
        if number == 1:
            self.d.wait()
            for where, copy in self.copies:
                self.out[where] = self.whole(*where).astype(BF16)
                copy.start()
            self.own[: self.rows, :] = self.whole(z, y, x)
        if number == 2:
            await_bytes(self.pieces, self.got)
            total = self.own[: self.rows, :]
            for k in range(15):
                total = total + self.pieces[k].astype(F32)
            self.result(total)


def gelu_and_slope(values):
    cdf = 0.5 + 0.5 * lax.erf(values * math.sqrt(0.5))
    bell = jnp.exp2((values * values) * (-0.5 * math.log2(math.e)))
    return values * cdf, cdf + (values * (1.0 / math.sqrt(2.0 * math.pi))) * bell


def lane_pattern(shape, size):
    return lax.rem(lax.broadcasted_iota(jnp.int32, shape, len(shape) - 1), size)


def turned(values, cosine, sine):
    return values * cosine + pltpu.roll(values, 64, 1) * sine


def swap_middle(values):
    group = lane_pattern((1, 128), 128) // 32
    return jnp.where(
        group == 1,
        pltpu.roll(values, 96, 1),
        jnp.where(group == 2, pltpu.roll(values, 32, 1), values),
    )


TILE = 256
BLOCK = 128
SPAN = BLOCK + REACH
PAIRS = H // 2
COLUMNS = 256
UNITS = 12
GROUP, OUT, DOWN, UP = 0, 3, (4, 6, 8, 10), (5, 7, 9, 11)
D0, U0, D1, U1, D2, U2, D3, U3 = range(4, 12)
DUE = {
    "tables": ((1, 1),),
    "masks": ((0, 1), (2, 1), (OUT, 0), (D0, 0), (0, 2)),
    ("before", 0): ((OUT, 1), (U0, 0)),
    ("during", 0): ((1, 2),),
    ("after", 0): ((1, 3), (D0, 1), (D1, 0)),
    ("before", 1): ((2, 2), (OUT, 2), (U0, 1), (U1, 0)),
    ("after", 1): ((2, 3), (D0, 2), (D1, 1), (D2, 0)),
    ("before", 2): ((OUT, 3), (U0, 2), (U1, 1), (U2, 0)),
    ("after", 2): ((OUT, 4), (D0, 3), (D1, 2), (D2, 1), (D3, 0)),
    ("after", 3): ((D0, 4), (U0, 3), (U1, 2), (U2, 1), (U3, 0)),
    ("norm", 2): ((D2, 2),),
    ("feed", 0, 0): ((U0, 4), (D1, 3), (D3, 1)),
    ("feed", 0, 1): ((D1, 4), (U1, 3), (U2, 2), (U3, 1)),
    ("feed", 0, 2): ((D2, 3), (D3, 2)),
    ("feed", 1, 0): ((U1, 4), (D2, 4)),
    ("feed", 1, 1): ((U2, 3), (U3, 2)),
    ("feed", 1, 2): ((D3, 3), (U2, 4)),
    ("feed", 2, 0): ((D3, 4),),
    ("feed", 2, 1): ((U3, 3),),
    ("feed", 2, 2): ((U3, 4),),
}
LAST = 2
CHUNKS = (
    (((0, 0), (1, 0)), ((2, 0), (2, 1))),
    (((0, 1), (1, 1)), ((2, 2), (1, 2))),
    (((0, 2), (0, 3)), ((2, 3), (1, 3))),
)


def place_of(kind, p):
    for g, cores in enumerate(CHUNKS):
        for c, pair in enumerate(cores):
            if (kind, p) in pair:
                return g, c, pair.index((kind, p))


def run(begin, end, body, events=None):
    def with_events(i, carried):
        for when, actions in sorted((events or {}).items()):

            @pl.when(i == when)
            def _(actions=actions):
                for action in actions:
                    action()

        body(i, carried)
        return 0

    lax.fori_loop(begin, end, with_events, 0)


def in_turn(items, stages, events):
    for i in range(len(items) + len(stages) - 1):
        for action in events.get(i, []):
            action()
        for late, stage in enumerate(stages):
            if 0 <= i - late < len(items):
                stage(items[i - late])


def in_pairs(body):
    def both(i, carried):
        body(2 * i, carried)
        body(2 * i + 1, carried)

    return both


def regroup(tiles, quarter, back=False):
    group = lax.broadcasted_iota(jnp.int32, (1, 128), 1) // 32
    out = jnp.zeros_like(tiles[0])
    for a in range(4):
        out = jnp.where(group == a, pltpu.roll(tiles[a], (a - quarter) * 32 % 128, 1), out)
    return out


def scratch_list(frames, width):
    blocks = frames // BLOCK
    ext = REACH + frames
    unit = (4, 2, 2, width // 16, COLUMNS)
    half = width // 32
    return [
        ("x", (frames, width), BF16),
        ("dy", (frames, width), BF16),
        ("y", (frames, width), BF16),
        ("mixed", (frames, width), BF16),
        ("wo", (width // 16, width // 2), F32),
        ("wu", (width // 16, 2 * width), F32),
        ("wd", (width // 4, width // 2), F32),
        ("w", (UNITS, 2) + unit, BF16),
        ("pos", (8, frames), F32),
        ("vecs", (2, 8, width // 2), F32),
        ("segs", (2, 8, frames), F32),
        ("n1t", (width, frames), BF16),
        ("cos", (frames, 128), F32),
        ("sin", (frames, 128), F32),
        ("bias", (blocks, SPAN, BLOCK), BF16),
        ("qx", (PAIRS, frames, 128), BF16),
        ("kx", (PAIRS, ext, 128), BF16),
        ("vx", (PAIRS, ext, 128), BF16),
        ("kt", (PAIRS, 128, ext), BF16),
        ("vt", (PAIRS, 128, ext), BF16),
        ("probs", (PAIRS, blocks, SPAN, 2 * BLOCK), BF16),
        ("ot", (width, frames), BF16),
        ("n2t", (width, frames), BF16),
        ("actt", (2 * COLUMNS, frames), BF16),
        ("du", (2, frames, COLUMNS), BF16),
        ("after", (frames, width), F32),
        ("branch", (frames, width), BF16),
        ("branch_two", (frames, width), F32),
        ("dx1", (frames, width), F32),
        ("dba", (2, frames, width // 2), BF16),
        ("dox", (PAIRS, frames, 128), BF16),
        ("dp", (3, 2, frames, COLUMNS), BF16),
        ("dkx", (ext, 128), F32),
        ("dvx", (ext, 128), F32),
        ("h_out", (PAIRS, 2, REACH, 128), BF16),
        ("h_in", (PAIRS, 2, REACH, 128), BF16),
        ("acc", (8, width), F32),
        ("v_out", (8, width // 2), F32),
        ("v_in", (8, width // 2), F32),
        ("v_all", (16, 8, width // 2), F32),
        ("pieces", (15, width // 16, COLUMNS), BF16),
        ("own", (UNITS - 3, width, COLUMNS), F32),
        ("up_sums", (4, width // 16, COLUMNS), F32),
        ("s_in", (UNITS,) + unit, BF16),
        ("c_in", (UNITS - 1, 2, 4, 2, half, COLUMNS), BF16),
        ("b_in", (UNITS - 1, 2, 4, half, COLUMNS), BF16),
        ("a_in", (UNITS - 1, 3, width // 16, COLUMNS), BF16),
    ]


SLOTS = 12 * UNITS + 2 * (2 + 2 * PAIRS + PAIRS) + 4


def layer_kernel(names, *refs):
    seg_ref, wq_shard = refs[2:4]
    vectors = refs[7:13]
    y_out, ig_out, gq, go, gu, gd, gv = refs[13:20]
    m = dict(zip(names, refs[20:-2]))
    x_ref, dy_ref, y_ref, mixed = m["x"], m["dy"], m["y"], m["mixed"]
    wo_shard, wu_shard, wd_shard = m["wo"], m["wu"], m["wd"]
    moves = refs[-2]
    loads = [
        pltpu.make_async_copy(source, target, moves.at[i])
        for i, (source, target) in enumerate(
            (
                (refs[0].at[0], x_ref),
                (refs[4], wo_shard),
                (refs[5], wu_shard),
                (refs[6], wd_shard),
                (refs[1].at[0], dy_ref),
            )
        )
    ]
    at = coordinates()
    row, core, x, y, z = at
    peers = peers_of(at)
    links = Links(refs[-1], peers)
    frames, width = x_ref.shape
    piece = width // 16
    blocks, tiles = frames // BLOCK, frames // TILE
    factor = 1.0 / math.sqrt(HD)
    w = m["w"]
    other = 1 - core

    def chunk_columns(g, j):
        offsets = []
        for c in range(2):
            kind, p = CHUNKS[g][c][j]
            offsets.append((kind * PAIRS + p - 6 * c) * 128)
        begin = offsets[0] + core * (offsets[1] - offsets[0])
        return pl.ds(pl.multiple_of(begin, 128), 128)

    def ordered(g, j, value):
        kinds = [CHUNKS[g][c][j][0] for c in range(2)]
        if kinds == [2, 2]:
            return value
        swapped = swap_middle(value)
        if 2 not in kinds:
            return swapped
        return jnp.where(core == kinds.index(2), value, swapped)

    greet(peers)
    for load in loads:
        load.start()
    for g in range(3):
        for j in range(2):
            w[g, core, z, y, x, :, j * 128 : (j + 1) * 128] = ordered(
                g, j, wq_shard[:, chunk_columns(g, j)]
            ).astype(BF16)
    m["vecs"][core] = jnp.concatenate(
        [v[...].astype(BF16).astype(F32) for v in vectors]
        + [jnp.zeros((2, width // 2), F32)],
        axis=0,
    )
    m["segs"][core] = jnp.broadcast_to(seg_ref[...].astype(F32), (8, frames))
    be_greeted()
    vec_copy = links.single(m["vecs"].at[core], m["vecs"].at[core], "s")
    seg_copy = links.single(m["segs"].at[core], m["segs"].at[core], "s")
    kinds = [GatherDirect, GatherPlane, GatherPlane] + [Gather] * (UNITS - 3)
    gathers = [kind(w, i, links, at) for i, kind in enumerate(kinds)]

    def due(*where):
        for i, step in DUE.get(where if len(where) > 1 else where[0], ()):
            gathers[i].step(step)

    vec_copy.start()
    seg_copy.start()
    for i in (0, 1, 2):
        gathers[i].step(0)
    for load in loads:
        load.wait()
    w[OUT, core, z, y, x] = wo_shard[...].astype(BF16)
    for q in range(4):
        w[DOWN[q], core, z, y, x] = wd_shard[q * piece : (q + 1) * piece, :].astype(BF16)
    for q in range(4):
        for j in range(2):
            made = regroup(
                [wu_shard[:, (4 * j + a) * 128 : (4 * j + a + 1) * 128] for a in range(4)], q
            )
            w[UP[q], core, z, y, x, :, j * 128 : (j + 1) * 128] = made.astype(BF16)

    def vector(i):
        return jnp.concatenate([m["vecs"][0, i : i + 1, :], m["vecs"][1, i : i + 1, :]], axis=1)

    def normalized(values):
        average = jnp.mean(values, axis=-1, keepdims=True)
        centred = values - average
        variance = jnp.mean(centred * centred, axis=-1, keepdims=True)
        scale = lax.rsqrt(variance + EPSILON)
        return centred * scale, scale

    vec_copy.wait_recv()
    n1 = y_ref
    gain_one, bias_one = vector(0), vector(1)

    def norm_one(t, _):
        rows = start_of(t, TILE)
        unit, _scale = normalized(x_ref[rows, :].astype(F32))
        low = (unit * gain_one + bias_one).astype(BF16)
        n1[rows, :] = low
        m["n1t"][:, rows] = low.T

    run(0, tiles, norm_one)

    seg_copy.wait_recv()
    segs = m["segs"]
    index = lax.broadcasted_iota(jnp.int32, (8, frames), 1)
    order = index.astype(F32)

    def starts_in(which):
        line = segs[which]
        change = (line != pltpu.roll(line, 1, 1)) | (index == 0)
        begun = jnp.where(change, order, 0.0)
        reach = 1
        while reach < frames:
            begun = jnp.maximum(begun, jnp.where(index >= reach, pltpu.roll(begun, reach, 1), 0.0))
            reach *= 2
        return begun

    running = (core > 0) & (segs[core] == segs[other][:, frames - 1 :])
    before = starts_in(other)[:, frames - 1 :]
    m["pos"][...] = order - jnp.where(
        running, before - (core * frames).astype(F32), starts_in(core)
    )
    seg_blocks = m["own"]

    def across(line):
        return jnp.broadcast_to(line, (BLOCK, BLOCK)).T

    def spread(which, begin):
        return across(segs[which, 0:1, begin : begin + BLOCK])

    def seg_place(e):
        return (e // 8, pl.ds((e % 8) // 2 * BLOCK, BLOCK), pl.ds(e % 2 * BLOCK, BLOCK))

    group = lane_pattern((1, 128), 128) // 32
    lanes = lane_pattern((1, 128), HD // 2).astype(F32)
    frequency = jnp.exp(lanes * (-2.0 * math.log(10000.0) / HD))
    near_half = lane_pattern((1, 128), 128) < HD
    quarter = frames // 4
    for i in range(quarter // BLOCK):
        position = across(m["pos"][0:1, i * BLOCK : (i + 1) * BLOCK])
        for a in range(1, 4):
            begin = a * quarter + i * BLOCK
            position = jnp.where(
                group == a, across(m["pos"][0:1, begin : begin + BLOCK]), position
            )
        angle = position * frequency
        for name, table in (("cos", jnp.cos(angle)), ("sin", jnp.sin(angle))):
            for a in range(4):
                begin = a * quarter + i * BLOCK
                wide = jnp.where(group == a, table, 0.0)
                wide = wide + pltpu.roll(wide, 32, 1)
                wide = wide + pltpu.roll(wide, 64, 1)
                if name == "sin":
                    wide = jnp.where(near_half, -wide, wide)
                m[name][begin : begin + BLOCK, :] = wide

    for e in range(REACH // BLOCK):
        halo = spread(other, frames - REACH + e * BLOCK)
        seg_blocks[seg_place(e)] = jnp.where(core > 0, halo, -1.0)
    for b in range(blocks):
        seg_blocks[seg_place(REACH // BLOCK + b)] = spread(core, b * BLOCK)
    due("tables")
    distance = (
        lax.broadcasted_iota(jnp.int32, (SPAN, BLOCK), 1)
        - lax.broadcasted_iota(jnp.int32, (SPAN, BLOCK), 0)
        + REACH
    )
    near = (distance >= 0) & (distance < WINDOW)
    for b in range(blocks):
        keys = jnp.concatenate([seg_blocks[seg_place(b + i)] for i in range(SPAN // BLOCK)], axis=0)
        line = segs[core, 0:1, b * BLOCK : (b + 1) * BLOCK]
        m["bias"][b] = jnp.where(near & (keys == line), 0.0, NEGATIVE).astype(BF16)
    due("masks")

    def two_heads(value, swapped=False):
        first = lax.rem(group, 2) == 0 if swapped else group < 2
        zero = jnp.zeros_like(value)
        return jnp.concatenate(
            [jnp.where(first, value, zero), jnp.where(first, zero, value)], axis=0
        )

    def projection(g):
        def project(t, _):
            rows = start_of(t, TILE)
            placed = pl.ds(pl.multiple_of(REACH + t * TILE, TILE), TILE)
            left = n1[rows, :]
            cosine, sine = m["cos"][rows, :], m["sin"][rows, :]
            for c in range(2):
                wide = dot(left, w[g, c].reshape(width, COLUMNS))
                for j in range(2):
                    chunk = wide[:, j * 128 : (j + 1) * 128]
                    kind, p = CHUNKS[g][c][j]
                    if kind == 0:
                        turn = turned(chunk, cosine, sine).astype(BF16)
                        m["qx"][p, rows, :] = (turn * factor).astype(BF16)
                    elif kind == 1:
                        value = turned(chunk, cosine, sine).astype(BF16)
                        m["kx"][p, placed, :] = value
                        m["kt"][p, :, placed] = value.T
                    else:
                        value = chunk.astype(BF16)
                        m["vx"][p, placed, :] = value
                        m["vt"][p, :, placed] = value.T

        return project

    tail, head = pl.ds(frames, REACH), pl.ds(0, REACH)

    def heads_joined(both, swapped=False):
        step = HD // 2 if swapped else HD
        return jnp.concatenate(
            [
                both[i : i + step, i // step % 2 * BLOCK : (i // step % 2 + 1) * BLOCK]
                for i in range(0, 2 * HD, step)
            ],
            axis=0,
        )

    unit_rows = lax.broadcasted_iota(jnp.int32, (2 * BLOCK, BLOCK), 0)
    unit_lanes = lax.broadcasted_iota(jnp.int32, (2 * BLOCK, BLOCK), 1)
    picks = (lax.rem(unit_rows, BLOCK) == unit_lanes).astype(F32).astype(BF16)

    def block_rows(b):
        return pl.ds(b * BLOCK, BLOCK)

    def block_window(b):
        return pl.ds(b * BLOCK, SPAN)

    def spare(i):
        return m["after"].at[pl.ds(i // 2 * SPAN, SPAN), pl.ds(i % 2 * 2 * BLOCK, 2 * BLOCK)]

    def spare_low(i):
        return m["branch"].at[pl.ds(i // 2 * SPAN, SPAN), pl.ds(i % 2 * 2 * BLOCK, 2 * BLOCK)]

    def attend(p, events):
        def score(b):
            left = jnp.concatenate([m["kx"][p, block_window(b), :], m["bias"][b]], axis=1)
            right = jnp.concatenate([two_heads(m["qx"][p, block_rows(b), :], True), picks], axis=1)
            spare(b % 4)[...] = dot_t(left, right)

        def soften(b):
            scores = spare(b % 4)[...]
            top = jnp.max(scores, axis=0, keepdims=True)
            weights = jnp.exp(scores - top)
            total = jnp.sum(weights, axis=0, keepdims=True)
            m["probs"][p, b] = (weights * (1.0 / total)).astype(BF16)

        def mix(b):
            joined = heads_joined(dot(m["vt"][p, :, block_window(b)], m["probs"][p, b]))
            m["ot"][p * 128 : (p + 1) * 128, block_rows(b)] = joined.astype(BF16)
            mixed[block_rows(b), p * 128 : (p + 1) * 128] = joined.T.astype(BF16)

        in_turn([*range(2, blocks), 0, 1], (score, soften, mix), events)

    halos = {}

    def send_halo(kind, p):
        ref = m["kx"] if kind == 1 else m["vx"]
        halos[kind, p] = links.single(ref.at[p, tail], ref.at[p, head], "s")
        halos[kind, p].start()

    def take_halo(p):
        for kind, flat, turned_ref in ((1, m["kx"], m["kt"]), (2, m["vx"], m["vt"])):
            halos[kind, p].wait_recv()
            turned_ref[p, :, 0:REACH] = flat[p, 0:REACH, :].T

    for p in range(PAIRS):
        if p < 3:
            run(0, tiles // 2, in_pairs(projection(p)))
            for pair in CHUNKS[p]:
                for kind, q in pair:
                    if kind > 0:
                        send_halo(kind, q)
        due("before", p)
        take = functools.partial(take_halo, p)
        if p < 2:
            attend(p, {blocks - 2: [functools.partial(due, "during", p), take]})
        else:
            take()
            attend(p, {})
        due("after", p)

    m["acc"][...] = jnp.zeros_like(m["acc"])
    acc = m["acc"]

    def add_to(i, values):
        acc[i : i + 1, :] = acc[i : i + 1, :] + jnp.sum(values, axis=0, keepdims=True)

    scale_one, gain_two, bias_two, scale_two = vector(2), vector(3), vector(4), vector(5)
    n2 = y_ref
    dba = m["dba"]

    def norm_back(unit, scale, gain, grad):
        inner = grad * gain
        return scale * (
            inner
            - jnp.mean(inner, axis=-1, keepdims=True)
            - unit * jnp.mean(inner * unit, axis=-1, keepdims=True)
        )

    def norm_two(t, _):
        rows = start_of(t, TILE)
        both = mixed[rows, :]
        branch = jnp.concatenate(
            [dot(both, w[OUT, c].reshape(width, COLUMNS)) for c in range(2)], axis=1
        )
        m["branch"][rows, :] = branch.astype(BF16)
        after = x_ref[rows, :].astype(F32) + scale_one * branch
        m["after"][rows, :] = after
        unit, _scale = normalized(after)
        low = (unit * gain_two + bias_two).astype(BF16)
        n2[rows, :] = low
        m["n2t"][:, rows] = low.T
        dbm = (dy_ref[rows, :].astype(F32) * scale_two).astype(BF16)
        dba[0, rows, :] = dbm[:, : width // 2]
        dba[1, rows, :] = dbm[:, width // 2 :]

    run(0, tiles // 2, in_pairs(norm_two), {1: [functools.partial(due, "norm", 2)]})

    def result_of(i):
        def keep(value):
            if i < OUT:
                for j in range(2):
                    gq[:, chunk_columns(i, j)] = ordered(
                        i, j, value[:, j * 128 : (j + 1) * 128]
                    )
            elif i == OUT:
                go[...] = value
            elif i in DOWN:
                q = DOWN.index(i)
                gd[q * piece : (q + 1) * piece, :] = value
            else:
                m["up_sums"][UP.index(i)] = value

        return keep

    sums = {}

    def unit_grads(i, left, right):
        gathers[i].drain()
        if i < OUT:
            sums[DOWN[i]].drain()
        place = DOWN[i] if i < OUT else i
        out, own = w.at[place, 0], m["own"].at[place - 3]
        if i == LAST:
            arrived, kind = [m["s_in"].at[i], m["pieces"]], ScatterDirect
        else:
            at_unit = i - (i > LAST)
            arrived = [m["s_in"].at[i]] + [m[n].at[at_unit] for n in ("c_in", "b_in", "a_in")]
            kind = Scatter
        sums[i] = kind(own, out, arrived, result_of(i), links, at, m["s_in"])
        own[...] = dot(left[...], right[core])
        out[...] = dot(left[...], right[other]).astype(BF16).reshape(4, 2, 2, piece, COLUMNS)
        sums[i].step(0)

    def step_of(i, number):
        return lambda: sums[i].step(number)

    def feed(q):
        def middle(pair, _):
            for t in range(2):
                one(2 * pair + t)

        def one(t):
            rows = start_of(t, TILE)
            ups = [w[UP[q], h].reshape(width, COLUMNS) for h in range(2)]
            dbm = jnp.concatenate([dba[c, rows, :] for c in range(2)], axis=1)
            acts, dus = [], []
            for h in range(2):
                value, slope = gelu_and_slope(dot(n2[rows, :], ups[h]))
                act = value.astype(BF16)
                m["actt"][h * COLUMNS : (h + 1) * COLUMNS, rows] = act.T
                down = jnp.concatenate(
                    [w[DOWN[q], c, 2 * h : 2 * h + 2].reshape(COLUMNS, COLUMNS) for c in range(2)],
                    axis=1,
                )
                du = (dot_t(dbm, down) * slope).astype(BF16)
                m["du"][h, rows, :] = du
                acts.append(act)
                dus.append(du)
            act = jnp.concatenate(acts, axis=1)
            for c in range(2):
                columns = pl.ds(c * COLUMNS, COLUMNS)
                total = dot(act, w[DOWN[q], c].reshape(2 * COLUMNS, COLUMNS))
                if q > 0:
                    total = total + m["branch_two"][rows, columns]
                m["branch_two"][rows, columns] = total
            grad = dot_t(jnp.concatenate(dus, axis=1), jnp.concatenate(ups, axis=1))
            if q > 0:
                grad = grad + m["dx1"][rows, :]
            m["dx1"][rows, :] = grad

        return middle

    def steps_of(q, number):
        return [step_of(DOWN[q], number), step_of(UP[q], number)]

    def do(actions):
        for action in actions:
            action()

    for q in range(4):
        due("feed", q, 0)
        events = {1: [functools.partial(due, "feed", q, 1)]}
        if q > 0:
            events[1] += steps_of(q - 1, 1)
        run(0, tiles // 2, feed(q), events)
        due("feed", q, 2)
        if q > 1:
            do(steps_of(q - 2, 2))
        unit_grads(DOWN[q], m["actt"], dba)
        unit_grads(UP[q], m["n2t"], m["du"])

    def norm_two_back(t, _):
        rows = start_of(t, TILE)
        after, branch_two = m["after"][rows, :], m["branch_two"][rows, :]
        y_ref[rows, :] = (after + scale_two * branch_two).astype(BF16)
        upstream = dy_ref[rows, :].astype(F32)
        add_to(5, upstream * branch_two)
        unit, scale = normalized(after)
        grad = m["dx1"][rows, :]
        add_to(3, grad * unit)
        add_to(4, grad)
        dx1 = upstream + norm_back(unit, scale, gain_two, grad)
        m["dx1"][rows, :] = dx1
        add_to(2, dx1 * m["branch"][rows, :].astype(F32))
        low = (dx1 * scale_one).astype(BF16)
        sides = [low[:, : width // 2], low[:, width // 2 :]]
        for c in range(2):
            dba[c, rows, :] = sides[c]
        dmixed = (
            dot_t(sides[0], w[OUT, 0].reshape(width, COLUMNS))
            + dot_t(sides[1], w[OUT, 1].reshape(width, COLUMNS))
        ).astype(BF16)
        m["n2t"][:, rows] = dmixed.T
        for p in range(PAIRS):
            m["dox"][p, rows, :] = dmixed[:, p * 128 : (p + 1) * 128]

    do(steps_of(0, 3))
    run(
        0,
        tiles // 2,
        in_pairs(norm_two_back),
        {1: steps_of(3, 1)},
    )
    y_send = pltpu.make_async_copy(y_ref, y_out.at[0], moves.at[5])
    y_send.start()
    do(steps_of(2, 2))
    unit_grads(OUT, m["ot"], dba)
    do(steps_of(1, 3))

    dp = m["dp"]
    halfway = [
        [step_of(OUT, 1)],
        steps_of(2, 3) + steps_of(3, 2),
        [step_of(GROUP, 1)],
        [step_of(GROUP + 1, 1)],
    ]
    after_pair = [
        steps_of(0, 4),
        steps_of(1, 4) + [step_of(OUT, 2)],
        steps_of(2, 4) + steps_of(3, 3) + [step_of(OUT, 3)],
        [],
    ]

    def store_turned(kind, p, rows, value):
        g, c, j = place_of(kind, p)
        if kind < 2:
            value = turned(value, m["cos"][rows, :], -m["sin"][rows, :])
        dp[g, c, rows, j * 128 : (j + 1) * 128] = value.astype(BF16)

    backs = []
    for p in range(PAIRS):
        dkx, dvx = m["dkx"], m["dvx"]
        dkx[...] = jnp.zeros_like(dkx)
        dvx[...] = jnp.zeros_like(dvx)

        def probe(b, p=p):
            spare(b % 4)[...] = dot_t(
                m["vx"][p, block_window(b), :], two_heads(m["dox"][p, block_rows(b), :])
            )

        def weigh(b, p=p):
            probs = m["probs"][p, b].astype(F32)
            heads = (pl.ds(p * 128, 128), block_rows(b))
            shared = m["n2t"][heads].astype(F32) * m["ot"][heads].astype(F32)
            balance = jnp.concatenate(
                [
                    jnp.sum(shared[:HD], axis=0, keepdims=True),
                    jnp.sum(shared[HD:], axis=0, keepdims=True),
                ],
                axis=1,
            )
            spare_low(b % 4)[...] = (probs * (spare(b % 4)[...] - balance)).astype(BF16)

        def gather_back(b, p=p):
            window, rows = block_window(b), block_rows(b)
            dscores = spare_low(b % 4)[...]
            dvx[window, :] = dvx[window, :] + dot(
                m["probs"][p, b], two_heads(m["dox"][p, rows, :])
            )
            dkx[window, :] = dkx[window, :] + dot(dscores, two_heads(m["qx"][p, rows, :], True))
            joined = heads_joined(dot(m["kt"][p, :, window], dscores), True).T * factor
            store_turned(0, p, rows, joined)

        h_out, h_in = m["h_out"], m["h_in"]
        halo_back = links.single(h_out.at[p], h_in.at[p], "s")
        backs.append(halo_back)

        def send_back(p=p, halo_back=halo_back):
            h_out[p, 0] = dkx[0:REACH, :].astype(BF16)
            h_out[p, 1] = dvx[0:REACH, :].astype(BF16)
            halo_back.start()

        events = {4: [send_back] + halfway[p]}
        in_turn(range(blocks), (probe, weigh, gather_back), events)
        halo_back.wait_recv()
        dkx[tail, :] = dkx[tail, :] + h_in[p, 0].astype(F32)
        dvx[tail, :] = dvx[tail, :] + h_in[p, 1].astype(F32)

        def finish(t, _, p=p):
            rows = start_of(t, TILE)
            placed = pl.ds(pl.multiple_of(REACH + t * TILE, TILE), TILE)
            store_turned(1, p, rows, dkx[placed, :])
            store_turned(2, p, rows, dvx[placed, :])

        run(0, tiles, finish)
        do(after_pair[p])
        if p > 0:
            unit_grads(GROUP + p - 1, m["n1t"], dp.at[p - 1])
    sums[GROUP].step(2)


    def first(t, _):
        rows = start_of(t, TILE)
        sides = [(g, c) for g in range(3) for c in range(2)]
        grad = dot_t(
            jnp.concatenate([dp[g, c, rows, :] for g, c in sides], axis=1),
            jnp.concatenate([w[g, c].reshape(width, COLUMNS) for g, c in sides], axis=1),
        )
        unit, scale = normalized(x_ref[rows, :].astype(F32))
        add_to(0, grad * unit)
        add_to(1, grad)
        mixed[rows, :] = (
            m["dx1"][rows, :] + norm_back(unit, scale, gain_one, grad)
        ).astype(BF16)

    late = {1: [step_of(LAST, 1)], 3: [*steps_of(3, 4), step_of(OUT, 4), step_of(GROUP + 1, 2)]}
    run(0, tiles, first, late)
    sends = [pltpu.make_async_copy(mixed, ig_out.at[0], moves.at[6])]
    sends[0].start()

    v_out, v_in, v_all = m["v_out"], m["v_in"], m["v_all"]
    v_out[...] = acc[:, start_of(other, width // 2)]
    vector_hop = links.single(v_out, v_in, "s")
    vector_hop.start()
    sums[GROUP].step(3)
    vector_hop.wait_recv()
    v_all[row] = acc[:, start_of(core, width // 2)] + v_in[...]
    spread_send, spread_recv = links.slot(), links.slot()
    for k in range(1, 16):
        links.copy(v_all.at[row], v_all.at[row], ("r", k), spread_send, spread_recv).start()
    for j in range(2):
        for a in range(4):
            gu[:, (4 * j + a) * 128 : (4 * j + a + 1) * 128] = regroup(
                [m["up_sums"][q, :, j * 128 : (j + 1) * 128] for q in range(4)], a, True
            )
    sums[GROUP + 1].step(3)
    sums[GROUP].step(4)
    await_bytes(v_all.at[0:15], spread_recv)
    total = v_all[0]
    for r in range(1, 16):
        total = total + v_all[r]
    gv[...] = total
    sums[LAST].step(2)
    sums[GROUP + 1].step(4)
    await_bytes(v_all.at[0:15], spread_send)
    for i, each in sums.items():
        if i not in DOWN[:3]:
            each.drain()
    for each in [vec_copy, seg_copy, *halos.values(), *backs, vector_hop]:
        each.wait_send()
    y_send.wait()
    for each in sends:
        each.wait()


def write_kernel(*refs):
    for source, target in zip(refs[:6], refs[7:13]):
        target[...] = source[...]
    for i, vector in enumerate(refs[13:]):
        vector[...] = refs[6][i : i + 1, :]


def local_staged(
    inputs,
    cotangent,
    segment_ids,
    qkv_weight,
    out_weight,
    up_weight,
    down_weight,
    *vectors,
):
    frames, width = inputs.shape[1:]
    items = scratch_list(frames, width)
    whole = pl.BlockSpec(memory_space=pltpu.VMEM)
    anywhere = pl.BlockSpec(memory_space=pl.ANY)
    shapes = [
        jax.ShapeDtypeStruct(inputs.shape, BF16),
        jax.ShapeDtypeStruct(inputs.shape, BF16),
        *[
            jax.ShapeDtypeStruct(weight.shape, F32)
            for weight in (qkv_weight, out_weight, up_weight, down_weight)
        ],
    ]
    results = pl.pallas_call(
        functools.partial(layer_kernel, [name for name, _, _ in items]),
        out_shape=shapes + [jax.ShapeDtypeStruct((8, width // 2), F32)],
        in_specs=[anywhere] * 2 + [whole] * 2 + [anywhere] * 3 + [whole] * 6,
        out_specs=[anywhere] * 2 + [whole] * 5,
        scratch_shapes=[pltpu.VMEM(shape, kind) for _, shape, kind in items]
        + [pltpu.SemaphoreType.DMA((7,)), pltpu.SemaphoreType.DMA((SLOTS,))],
        compiler_params=pltpu.CompilerParams(
            collective_id=0, has_side_effects=True, vmem_limit_bytes=VMEM_LIMIT
        ),
    )(
        inputs,
        cotangent,
        segment_ids,
        qkv_weight,
        out_weight,
        up_weight,
        down_weight,
        *[v.reshape(1, -1) for v in vectors],
    )
    written = pl.pallas_call(
        write_kernel,
        out_shape=shapes + [jax.ShapeDtypeStruct((1, width // 2), F32)] * 6,
        in_specs=[whole] * 7,
        out_specs=[whole] * 12,
    )(*results)
    return (*written[:6], *[v.reshape(-1) for v in written[6:]])


VMEM_LIMIT = 64 * 2**20


def solution(mesh):
    placed = (
        P("rows", "tm", None),
        P("rows", "tm", None),
        P("rows", "tm"),
        P("rows", "tm"),
        P("rows", "tm"),
        P("rows", "tm"),
        P("rows", "tm"),
        P("tm"),
        P("tm"),
        P("tm"),
        P("tm"),
        P("tm"),
        P("tm"),
    )
    staged = mesh.shape["rows"] == 16 and mesh.shape["tm"] == 2
    return jax.shard_map(
        local_staged if staged else local,
        mesh=mesh,
        in_specs=placed,
        out_specs=(
            P("rows", "tm", None),
            P("rows", "tm", None),
            P("rows", "tm"),
            P("rows", "tm"),
            P("rows", "tm"),
            P("rows", "tm"),
            P("tm"),
            P("tm"),
            P("tm"),
            P("tm"),
            P("tm"),
            P("tm"),
        ),
        check_vma=False,
    )
```
